32 devices in a mesh: seq: 8 (over z, y), mp: 4 (over x, core).
Axes of the slice: x: 2, y: 2, z: 4, core: 2. Of those that a mesh axis runs over, the one named last changes fastest.
Arguments:
- tokens: bfloat16 [9792, 2048], P(('seq', 'mp')), may hold values from -6 to 6
- cotangent: bfloat16 [9792, 2048], P(('seq', 'mp')), may hold values from -6 to 6
- present: int32 [8, 4], P('seq'), may hold values from 0 to 1, as said below
- summary_mask: int32 [8, 4, 50], P('seq'), may hold values 0 or 1
- attention_weight: float32 [4, 2048, 2048], P(None, 'seq', 'mp'), may hold values from -0.5466517 to 0.5466517
- attention_first: float32 [4, 2048, 2048], P(None, 'seq', 'mp'), may hold values from -9.1552734e-05 to 9.1552734e-05
- attention_second: float32 [4, 2048, 2048], P(None, 'seq', 'mp'), may hold values from 5.163215e-10 to 4.170289e-09
- attention_average: float32 [4, 2048, 2048], P(None, 'seq', 'mp'), may hold values from -0.125 to 0.125
- hidden_weight: float32 [2, 2048, 8192], P(None, 'seq', 'mp'), may hold values from -0.09375 to 0.09375
- hidden_first: float32 [2, 2048, 8192], P(None, 'seq', 'mp'), may hold values from -9.1552734e-05 to 9.1552734e-05
- hidden_second: float32 [2, 2048, 8192], P(None, 'seq', 'mp'), may hold values from 5.163215e-10 to 4.170289e-09
- hidden_average: float32 [2, 2048, 8192], P(None, 'seq', 'mp'), may hold values from -0.09375 to 0.09375
- norm_params: float32 [6, 2048], P(None, 'seq'), may hold values from -1.2 to 2.2
- norm_first: float32 [6, 2048], P(None, 'seq'), may hold values from -0.00024414062 to 0.00024414062
- norm_second: float32 [6, 2048], P(None, 'seq'), may hold values from 4.5674593e-09 to 3.7731184e-08
- norm_average: float32 [6, 2048], P(None, 'seq'), may hold values from -1.2 to 2.2
- head_bias: float32 [2, 2048], P(None, ('mp', 'seq')), may hold values from -1.75 to 1.75
- head_first: float32 [2, 2048], P(None, ('mp', 'seq')), may hold values from -0.00024414062 to 0.00024414062
- head_second: float32 [2, 2048], P(None, ('mp', 'seq')), may hold values from 4.5674593e-09 to 3.7731184e-08
- head_average: float32 [2, 2048], P(None, ('mp', 'seq')), may hold values from -1.75 to 1.75
- unit_bias: float32 [8192], P(('mp', 'seq')), may hold values from -1.75 to 1.75
- unit_first: float32 [8192], P(('mp', 'seq')), may hold values from -9.1552734e-05 to 9.1552734e-05
- unit_second: float32 [8192], P(('mp', 'seq')), may hold values from 5.163215e-10 to 4.170289e-09
- unit_average: float32 [8192], P(('mp', 'seq')), may hold values from -1.75 to 1.75
Outputs:
- block_output: bfloat16 [9792, 2048], P(('seq', 'mp'))
- input_grad: bfloat16 [9792, 2048], P(('seq', 'mp'))
- grad_norm: float32 [], replicated
- attention_updated: float32 [4, 2048, 2048], P(None, 'seq', 'mp')
- attention_momentum: float32 [4, 2048, 2048], P(None, 'seq', 'mp')
- attention_variance: float32 [4, 2048, 2048], P(None, 'seq', 'mp')
- attention_averaged: float32 [4, 2048, 2048], P(None, 'seq', 'mp')
- attention_copy: bfloat16 [4, 2048, 2048], P(None, 'seq', 'mp')
- hidden_updated: float32 [2, 2048, 8192], P(None, 'seq', 'mp')
- hidden_momentum: float32 [2, 2048, 8192], P(None, 'seq', 'mp')
- hidden_variance: float32 [2, 2048, 8192], P(None, 'seq', 'mp')
- hidden_averaged: float32 [2, 2048, 8192], P(None, 'seq', 'mp')
- hidden_copy: bfloat16 [2, 2048, 8192], P(None, 'seq', 'mp')
- norm_updated: float32 [6, 2048], P(None, 'seq')
- norm_momentum: float32 [6, 2048], P(None, 'seq')
- norm_variance: float32 [6, 2048], P(None, 'seq')
- norm_averaged: float32 [6, 2048], P(None, 'seq')
- norm_copy: bfloat16 [6, 2048], P(None, 'seq')
- head_updated: float32 [2, 2048], P(None, ('mp', 'seq'))
- head_momentum: float32 [2, 2048], P(None, ('mp', 'seq'))
- head_variance: float32 [2, 2048], P(None, ('mp', 'seq'))
- head_averaged: float32 [2, 2048], P(None, ('mp', 'seq'))
- head_copy: bfloat16 [2, 2048], P(None, ('mp', 'seq'))
- unit_updated: float32 [8192], P(('mp', 'seq'))
- unit_momentum: float32 [8192], P(('mp', 'seq'))
- unit_variance: float32 [8192], P(('mp', 'seq'))
- unit_averaged: float32 [8192], P(('mp', 'seq'))
- unit_copy: bfloat16 [8192], P(('mp', 'seq'))
The draws below stay inside these ranges and needn't reach their ends.
Inputs may be any that keep to these rules, and one draw needn't show every extreme that they name: In every item the first and the last of the 4 segments are present.
All inputs are finite; a program needn't handle non-finite values. No bound on the sum of `summary_mask` on one device may be relied on, other than what follows from the above.
Results may differ from the reference program's by a relative error of at most 0.02.
Values may be sent and summed in bfloat16 or wider, within the bound.
A program may use at most 320 MiB of HBM per device.

```python
import math
import jax
import jax.numpy as jnp
from jax import lax

D = 2048
HEADS = 32
HEAD_DIM = 64
FF = 8192
SUMM = 50
NSEG = 4
SEG = 256
STEP = 10
ITEM = 1224
ITEMS = 8
ROWS = 9792
NPARAMS = 50356224


def rising_scale(key, width):
    ramp_up = jnp.arange(width, dtype=jnp.float32) / max(width - 1, 1)
    roughness = jax.random.uniform(key, (width,), jnp.float32, 0.8, 1.25)
    return jnp.exp(math.log(3.0) * (ramp_up - 0.5)) * roughness


def attention_layout(key, unit_draw):
    column = rising_scale(key, D)
    flat_ones = jnp.ones((D,), jnp.float32)
    output_scale = math.sqrt((SEG + SUMM) / (8.0 * D))
    slab_scales = jnp.stack([flat_ones * D ** (-0.5), flat_ones * D ** (-0.5), column * D ** (-0.5), flat_ones * output_scale])
    return unit_draw * slab_scales[:, None, :]


def draw_attention_weight(key, part):
    key = jax.random.fold_in(key, 1)
    array_shape = (4, D, D)
    unit_draw = jnp.clip(jax.random.normal(key, array_shape, jnp.float32), -4.0, 4.0)
    return attention_layout(jax.random.fold_in(key, 7), unit_draw)


def norm_layout(key, unit_draw):
    gain_first = rising_scale(jax.random.fold_in(key, 1), D)
    gain_second = rising_scale(jax.random.fold_in(key, 2), D)
    shifts = 0.3 * unit_draw
    return jnp.stack([gain_first, shifts[0], gain_second, shifts[1], shifts[2], shifts[3]])


def draw_norm_params(key, part):
    key = jax.random.fold_in(key, 3)
    unit_draw = jnp.clip(jax.random.normal(key, (4, D), jnp.float32), -4.0, 4.0)
    return norm_layout(jax.random.fold_in(key, 9), unit_draw)


def draw_norm_average(key, part):
    key = jax.random.fold_in(key, 5)
    unit_draw = jnp.clip(jax.random.normal(key, (4, D), jnp.float32), -4.0, 4.0)
    return norm_layout(jax.random.fold_in(key, 9), unit_draw)


def draw_present(key, part):
    key = jax.random.fold_in(key, 11)
    drawn_values = jax.random.randint(key, (ITEMS, NSEG), 0, ITEMS)
    chosen = drawn_values <= jnp.arange(ITEMS, dtype=jnp.int32)[:, None]
    columns = jnp.arange(NSEG, dtype=jnp.int32)[None, :]
    edge_rows = (columns == 0) | (columns == NSEG - 1)
    return jnp.where(edge_rows | chosen, 1, 0).astype(jnp.int32)


def plant(values, own_key, least, top_value):
    shape = values.shape
    index_at = [jax.random.randint(jax.random.fold_in(own_key, axis), (), 0, shape[axis]) for axis in range(len(shape))]
    values = values.at[tuple(index_at)].set(least)
    longest = shape.index(max(shape))
    index_at[longest] = (index_at[longest] + 1) % shape[longest]
    return values.at[tuple(index_at)].set(top_value)


def block_scale(own_key, dims, split, least, top_value):
    factor_of = 1.0
    for dim, shards_of in split:
        draws = jax.random.uniform(jax.random.fold_in(jax.random.fold_in(own_key, 6), dim), (shards_of,), jnp.float32, least / len(split), top_value / len(split))
        factor_of = factor_of * jnp.repeat(jnp.exp(draws), dims[dim] // shards_of).reshape((-1,) + (1,) * (len(dims) - 1 - dim))
    return factor_of


def noise(rng, dims, scale, limit, shards=(), kind=jnp.bfloat16):
    entries = scale * jax.random.normal(rng, dims, jnp.float32)
    if shards:
        entries = entries * block_scale(rng, dims, shards, -0.22, 0.18)
    return jnp.clip(entries, -limit, limit).astype(kind)


def setup_inputs(seed: int = 0) -> dict:
    key_list = jax.random.split(jax.random.key(seed), 25)
    tokens = noise(key_list[0], (ROWS, D), 1.0, 6.0, ((0, 32),))
    cotangent = noise(key_list[1], (ROWS, D), 1.0, 6.0, ((0, 32),))
    present = draw_present(jax.random.fold_in(key_list[24], 71), 0)
    summary_mask = plant((jax.random.randint(key_list[3], (ITEMS, NSEG, SUMM), 0, 4) < 3).astype(jnp.int32), jax.random.fold_in(key_list[3], 1), 0, 1)
    attention_weight = draw_attention_weight(jax.random.fold_in(key_list[24], 71), 0)
    attention_first = noise(key_list[5], (4, D, D), (0.111 * NPARAMS ** -0.5), 9.1552734375e-05, ((1, 8), (2, 4)), jnp.float32)
    attention_second = jnp.clip(jnp.exp(math.log(4.17028900301375e-09) - 2.089011 * jax.random.uniform(key_list[6], (4, D, D), jnp.float32) ** block_scale(key_list[6], (4, D, D), ((1, 8), (2, 4)), -0.2, 0.2)), 5.163214855663512e-10, 4.17028900301375e-09)
    attention_average = noise(key_list[7], (4, D, D), D ** -0.5, 0.125, ((1, 8), (2, 4)), jnp.float32)
    hidden_weight = noise(key_list[8], (2, D, FF), (2 * D) ** -0.5, 0.09375, ((1, 8), (2, 4)), jnp.float32)
    hidden_first = noise(key_list[9], (2, D, FF), (0.111 * NPARAMS ** -0.5), 9.1552734375e-05, ((1, 8), (2, 4)), jnp.float32)
    hidden_second = jnp.clip(jnp.exp(math.log(4.17028900301375e-09) - 2.089011 * jax.random.uniform(key_list[10], (2, D, FF), jnp.float32) ** block_scale(key_list[10], (2, D, FF), ((1, 8), (2, 4)), -0.2, 0.2)), 5.163214855663512e-10, 4.17028900301375e-09)
    hidden_average = noise(key_list[11], (2, D, FF), (2 * D) ** -0.5, 0.09375, ((1, 8), (2, 4)), jnp.float32)
    norm_params = draw_norm_params(jax.random.fold_in(key_list[24], 71), 0)
    norm_first = noise(key_list[13], (6, D), (0.33 * NPARAMS ** -0.5), 0.00024414062, ((1, 8),), jnp.float32)
    norm_second = jnp.clip(jnp.exp(math.log(3.773118351091398e-08) - 2.1115298 * jax.random.uniform(key_list[14], (6, D), jnp.float32) ** block_scale(key_list[14], (6, D), ((1, 8),), -0.2, 0.2)), 4.567459299664733e-09, 3.773118351091398e-08)
    norm_average = draw_norm_average(jax.random.fold_in(key_list[24], 71), 0)
    head_bias = noise(key_list[16], (2, D), 0.3, 1.75, ((1, 32),), jnp.float32)
    head_first = noise(key_list[17], (2, D), (0.33 * NPARAMS ** -0.5), 0.00024414062, ((1, 32),), jnp.float32)
    head_second = jnp.clip(jnp.exp(math.log(3.773118351091398e-08) - 2.1115298 * jax.random.uniform(key_list[18], (2, D), jnp.float32) ** block_scale(key_list[18], (2, D), ((1, 32),), -0.2, 0.2)), 4.567459299664733e-09, 3.773118351091398e-08)
    head_average = noise(key_list[19], (2, D), 0.3, 1.75, ((1, 32),), jnp.float32)
    unit_bias = noise(key_list[20], (FF,), 0.3, 1.75, ((0, 32),), jnp.float32)
    unit_first = noise(key_list[21], (FF,), (0.111 * NPARAMS ** -0.5), 9.1552734375e-05, ((0, 32),), jnp.float32)
    unit_second = jnp.clip(jnp.exp(math.log(4.17028900301375e-09) - 2.089011 * jax.random.uniform(key_list[22], (FF,), jnp.float32) ** block_scale(key_list[22], (FF,), ((0, 32),), -0.2, 0.2)), 5.163214855663512e-10, 4.17028900301375e-09)
    unit_average = noise(key_list[23], (FF,), 0.3, 1.75, ((0, 32),), jnp.float32)
    return dict(tokens=tokens, cotangent=cotangent, present=present, summary_mask=summary_mask, attention_weight=attention_weight, attention_first=attention_first, attention_second=attention_second, attention_average=attention_average, hidden_weight=hidden_weight, hidden_first=hidden_first, hidden_second=hidden_second, hidden_average=hidden_average, norm_params=norm_params, norm_first=norm_first, norm_second=norm_second, norm_average=norm_average, head_bias=head_bias, head_first=head_first, head_second=head_second, head_average=head_average, unit_bias=unit_bias, unit_first=unit_first, unit_second=unit_second, unit_average=unit_average)


@jax.custom_vjp
def low(v):
    return lax.optimization_barrier(v.astype(jnp.bfloat16)).astype(jnp.float32)

@jax.custom_vjp
def low_back(v):
    return v

def low_keep(v):
    return (low(v), None)

def low_pass(kept, grad):
    return (grad,)

def back_keep(v):
    return (v, None)

def back_low(kept, grad):
    return (low(grad),)
low.defvjp(low_keep, low_pass)
low_back.defvjp(back_keep, back_low)
norm_eps = 1e-05
beta_first = 0.9
beta_second = 0.95
adam_eps = 1e-08
clip_limit = 1.0
weight_decay = 0.1
average_keep = 0.6
vector_rate = 0.4
highest = lax.Precision.HIGHEST

def matmul(left, right):
    return jnp.dot(left, right, precision=highest)

def layer_norm(value, gain, shift):
    center = value - lax.optimization_barrier(jnp.mean(value, axis=-1, keepdims=True))
    spread = lax.optimization_barrier(jnp.mean(center * center, axis=-1, keepdims=True))
    return center * lax.rsqrt(spread + norm_eps) * gain + shift

def item_layout(present, summary):
    period = SEG + SUMM
    places = jnp.arange(NSEG * period, dtype=jnp.int32)
    segment = places // period
    slot_place = places % period - SEG
    segment_hit = segment[:, None] == jnp.arange(NSEG, dtype=jnp.int32)[None, :]
    slot_hit = slot_place[:, None] == jnp.arange(SUMM, dtype=jnp.int32)[None, :]
    segment_on = lax.optimization_barrier(jnp.sum(jnp.where(segment_hit, present[None, :], 0), axis=1, dtype=jnp.int32))
    both_hit = segment_hit[:, :, None] & slot_hit[:, None, :]
    slot_on = lax.optimization_barrier(jnp.sum(jnp.where(both_hit, summary[None], 0), axis=(1, 2), dtype=jnp.int32))
    summary_row = slot_place >= 0
    row_kept = segment_on * jnp.where(summary_row, slot_on, 1)
    return (places, segment, summary_row, row_kept)

def visible(query_places, query_segment, places, segment, summary_row, row_kept):
    same_segment = (segment[None, :] == query_segment[:, None]) & (places[None, :] <= query_places[:, None])
    earlier_summary = summary_row[None, :] & (segment[None, :] < query_segment[:, None])
    itself = places[None, :] == query_places[:, None]
    return itself | (row_kept[None, :] == 1) & (same_segment | earlier_summary)

def item_forward(params, token_rows, present, summary):
    attention, hidden, norms, head_terms, unit_terms = params
    places, segment, summary_row, row_kept = item_layout(present, summary)
    allowed = visible(places, segment, places, segment, summary_row, row_kept)
    row_weight = row_kept.astype(jnp.float32)[:, None]
    normed = low(layer_norm(token_rows, norms[0], norms[1]))
    queries = low_back(low(matmul(normed, attention[0]) + head_terms[0]))
    key_rows = low_back(low(matmul(normed, attention[1])))
    values = low_back(low(matmul(normed, attention[2]) + head_terms[1]))
    score_scale = HEAD_DIM ** (-0.5)

    def by_head(matrix):
        return matrix.reshape(-1, HEADS, HEAD_DIM).transpose(1, 0, 2)

    def one_head(operands):
        query_head, key_head, value_head = operands
        scores = low_back(matmul(query_head, key_head.T) * score_scale)
        softmaxed = jax.nn.softmax(jnp.where(allowed, scores, -1e+30), axis=-1)
        return matmul(low(softmaxed), value_head)
    context = lax.map(jax.checkpoint(one_head), (by_head(queries), by_head(key_rows), by_head(values)))
    context = low_back(low(context.transpose(1, 0, 2).reshape(-1, D)))
    attended = low_back(matmul(context, attention[3].T)) + norms[4]
    middle = token_rows + row_weight * attended
    second = low(layer_norm(middle, norms[2], norms[3]))
    pre_act = low_back(matmul(second, hidden[0]) + unit_terms)
    activated = low(jax.nn.gelu(pre_act, approximate=True))
    feed_out = low_back(matmul(activated, hidden[1].T)) + norms[5]
    return middle + row_weight * feed_out

def adam_step(master, grad, first, second, average, factor, rate, decay):
    clipped = grad * factor
    first_new = beta_first * first + (1.0 - beta_first) * clipped
    second_new = beta_second * second + (1.0 - beta_second) * clipped * clipped
    first_hat = first_new / (1.0 - beta_first ** STEP)
    second_hat = second_new / (1.0 - beta_second ** STEP)
    master_new = master - rate * (first_hat / (jnp.sqrt(second_hat) + adam_eps) + decay * master)
    average_new = average_keep * average + (1.0 - average_keep) * master_new
    return (master_new, first_new, second_new, average_new, master_new.astype(jnp.bfloat16))

def reference(tokens, cotangent, present, summary_mask, attention_weight, attention_first, attention_second, attention_average, hidden_weight, hidden_first, hidden_second, hidden_average, norm_params, norm_first, norm_second, norm_average, head_bias, head_first, head_second, head_average, unit_bias, unit_first, unit_second, unit_average):
    masters = (attention_weight, hidden_weight, norm_params, head_bias, unit_bias)
    inputs = tokens.astype(jnp.float32).reshape(ITEMS, ITEM, D)

    def forward(params, token_rows):
        rounded = tuple((low(master) for master in params))

        def per_item(operands):
            item_rows, item_present, item_summary = operands
            return item_forward(rounded, item_rows, item_present, item_summary)
        return lax.map(jax.checkpoint(per_item), (token_rows, present, summary_mask))
    outputs, pull_back = jax.vjp(forward, masters, inputs)
    grads, input_grads = pull_back(cotangent.astype(jnp.float32).reshape(ITEMS, ITEM, D))
    squares = jnp.float32(0.0)
    for grad in grads:
        squares = squares + jnp.sum(grad * grad)
    grad_norm = jnp.sqrt(squares)
    factor = jnp.minimum(1.0, clip_limit / (grad_norm + 1e-06))
    hidden_rate = jnp.array([D ** (-0.5), FF ** (-0.5)], jnp.float32)[:, None, None]
    attention_out = adam_step(attention_weight, grads[0], attention_first, attention_second, attention_average, factor, D ** (-0.5), weight_decay)
    hidden_out = adam_step(hidden_weight, grads[1], hidden_first, hidden_second, hidden_average, factor, hidden_rate, weight_decay)
    norm_out = adam_step(norm_params, grads[2], norm_first, norm_second, norm_average, factor, vector_rate, 0.0)
    head_out = adam_step(head_bias, grads[3], head_first, head_second, head_average, factor, vector_rate, 0.0)
    unit_out = adam_step(unit_bias, grads[4], unit_first, unit_second, unit_average, factor, vector_rate, 0.0)
    block_output = outputs.reshape(ROWS, D).astype(jnp.bfloat16)
    input_grad = input_grads.reshape(ROWS, D).astype(jnp.bfloat16)
    return (block_output, input_grad, grad_norm, attention_out[0], attention_out[1], attention_out[2], attention_out[3], attention_out[4], hidden_out[0], hidden_out[1], hidden_out[2], hidden_out[3], hidden_out[4], norm_out[0], norm_out[1], norm_out[2], norm_out[3], norm_out[4], head_out[0], head_out[1], head_out[2], head_out[3], head_out[4], unit_out[0], unit_out[1], unit_out[2], unit_out[3], unit_out[4])
```

```python
import functools

import jax
import jax.numpy as jnp
import numpy as np
from jax import lax
from jax.experimental import pallas as pl
from jax.experimental.pallas import tpu as pltpu
from jax.sharding import PartitionSpec as P

D = 2048
HEAD_DIM = 64
FF = 8192
SUMM = 50
NSEG = 4
SEG = 256
STEP = 10
PERIOD = SEG + SUMM
SEG_PAD = 320
SLAB = 64
KEYS = SLAB * (NSEG - 1) + SEG_PAD

norm_eps = 1e-05
beta_first = 0.9
beta_second = 0.95
adam_eps = 1e-08
clip_limit = 1.0
weight_decay = 0.1
average_keep = 0.6
vector_rate = 0.4
score_scale = HEAD_DIM ** (-0.5)
query_blocks = ((0, 128), (128, 256), (256, SEG_PAD))

f32 = jnp.float32
bf16 = jnp.bfloat16


def seq_grid():
    count = lax.axis_size("seq")
    inner = count // 4
    return count // inner, inner


def shift_outer(value, step):
    outer, inner = seq_grid()
    pairs = [
        (a * inner + b, ((a + step) % outer) * inner + b) for a in range(outer) for b in range(inner)
    ]
    return lax.ppermute(value, "seq", pairs)


def shift_inner(value, step):
    outer, inner = seq_grid()
    pairs = [
        (a * inner + b, a * inner + (b + step) % inner) for a in range(outer) for b in range(inner)
    ]
    return lax.ppermute(value, "seq", pairs)


def swap(value, bits):
    return lax.ppermute(value, "mp", [(m, m ^ bits) for m in range(lax.axis_size("mp"))])


def feature_order():
    outer, inner = seq_grid()
    me = lax.axis_index("seq")
    mine_a, mine_b = me // inner, me % inner
    return jnp.stack(
        [
            ((mine_a - i + outer) % outer) * inner + (mine_b - j + inner) % inner
            for j in range(inner)
            for i in range(outer)
        ]
    ).astype(jnp.int32)


def row_codes():
    count = lax.axis_size("mp")
    return [high * 2 + low for low in range(2) for high in range(count // 2)]


def gather_weight(own):
    outer, inner = seq_grid()
    line = [own]
    for _ in range(outer - 1):
        line.append(shift_outer(line[-1], 1))
    blocks = list(line)
    for _ in range(inner - 1):
        line = [shift_inner(part, 1) for part in line]
        blocks += line
    return jnp.concatenate(blocks, axis=0)


def scatter_weight(block_grad):
    outer, inner = seq_grid()
    total = None
    for i in reversed(range(outer)):
        part = block_grad(inner - 1, i)
        for j in reversed(range(inner - 1)):
            part = block_grad(j, i) + shift_inner(part.astype(bf16), -1).astype(f32)
        if total is not None:
            part = part + shift_outer(total.astype(bf16), -1).astype(f32)
        total = part
    return total


def gather_rows(own):
    count = lax.axis_size("mp")
    high = [own]
    for bit in range(1, count.bit_length() - 1):
        high = high + [swap(part, 1 << bit) for part in high]
    low = [swap(part, 1) for part in high]
    return jnp.concatenate(high + low, axis=0)


def scatter_rows(part):
    count = lax.axis_size("mp")
    half = part.shape[0] // 2
    kept = part[:half].astype(f32) + swap(part[half:], 1).astype(f32)
    rows = half // (count // 2)
    total = kept[:rows]
    for high in range(1, count // 2):
        total = total + swap(kept[high * rows : (high + 1) * rows].astype(bf16), high * 2).astype(f32)
    return total


def to_blocks_kernel(order_ref, in_ref, out_ref):
    rows = in_ref.shape[0]
    out_ref[...] = jnp.zeros_like(out_ref)
    out_ref[:rows, :] = in_ref[...]


def to_blocks(value, order, rows_padded):
    rows, width = value.shape
    count = order.shape[0]
    wide = width // count
    return pl.pallas_call(
        to_blocks_kernel,
        out_shape=jax.ShapeDtypeStruct((rows_padded, width), value.dtype),
        grid_spec=pltpu.PrefetchScalarGridSpec(
            num_scalar_prefetch=1,
            grid=(count,),
            in_specs=[pl.BlockSpec((rows, wide), lambda n, order_ref: (0, order_ref[n]))],
            out_specs=pl.BlockSpec((rows_padded, wide), lambda n, order_ref: (0, n)),
        ),
        name="to_blocks",
    )(order, value)


def from_blocks_kernel(order_ref, in_ref, out_ref):
    rows = out_ref.shape[0]
    out_ref[...] = in_ref[:rows, :].astype(out_ref.dtype)


def from_blocks(value, order, rows):
    rows_padded, width = value.shape
    count = order.shape[0]
    wide = width // count
    return pl.pallas_call(
        from_blocks_kernel,
        out_shape=jax.ShapeDtypeStruct((rows, width), bf16),
        grid_spec=pltpu.PrefetchScalarGridSpec(
            num_scalar_prefetch=1,
            grid=(count,),
            in_specs=[pl.BlockSpec((rows_padded, wide), lambda n, order_ref: (0, n))],
            out_specs=pl.BlockSpec((rows, wide), lambda n, order_ref: (0, order_ref[n])),
        ),
        name="from_blocks",
    )(order, value)


def segment_starts(me, mp_count, rows_padded):
    group = mp_count // NSEG
    starts = []
    for s in range(NSEG):
        pieces = []
        for r in range(group):
            code = jnp.bitwise_xor(me, s * group + r)
            place = jnp.bitwise_and(code, 1) * (mp_count // 2) + lax.shift_right_logical(code, 1)
            pieces.append(pl.multiple_of(place * rows_padded, rows_padded))
        starts.append(pieces)
    return starts


def load_segment(ref, pieces, rows_padded):
    parts = [ref[pl.ds(start, rows_padded), :] for start in pieces]
    return parts[0] if len(parts) == 1 else jnp.concatenate(parts, axis=0)


def load_slab(ref, pieces, rows_padded):
    return ref[pl.ds(pl.multiple_of(pieces[-1] + (rows_padded - SLAB), 16), SLAB), :]


def store_segment(ref, pieces, rows_padded, value):
    for r, start in enumerate(pieces):
        ref[pl.ds(start, rows_padded), :] = value[r * rows_padded : (r + 1) * rows_padded]


def lane_halves(shape):
    lane = lax.broadcasted_iota(jnp.int32, shape, 1)
    return lane < HEAD_DIM


def attend_kernel(mp_count, rows_padded, me_ref, q_ref, k_ref, v_ref, bias_ref, o_ref, p_ref):
    starts = segment_starts(me_ref[0], mp_count, rows_padded)
    for s in range(NSEG):
        keys = jnp.concatenate(
            [load_slab(k_ref, starts[e], rows_padded) for e in range(s)]
            + [load_segment(k_ref, starts[s], rows_padded)],
            axis=0,
        )
        values = jnp.concatenate(
            [load_slab(v_ref, starts[e], rows_padded) for e in range(s)]
            + [load_segment(v_ref, starts[s], rows_padded)],
            axis=0,
        )
        queries = load_segment(q_ref, starts[s], rows_padded)
        first_head = lane_halves(queries.shape)
        zero = jnp.zeros_like(queries)
        head_queries = (jnp.where(first_head, queries, zero), jnp.where(first_head, zero, queries))
        outs = []
        for low, high in query_blocks:
            count = SLAB * s + high
            bias = bias_ref[s, low:high, :count]
            both = []
            for h in range(2):
                scores = (
                    lax.dot_general(
                        head_queries[h][low:high],
                        keys[:count],
                        (((1,), (1,)), ((), ())),
                        preferred_element_type=f32,
                    )
                    + bias
                )
                peak = jnp.max(scores, axis=-1, keepdims=True)
                raised = jnp.exp(scores - peak)
                share = raised * (1.0 / jnp.sum(raised, axis=-1, keepdims=True))
                share = share.astype(bf16)
                p_ref[h, s * SEG_PAD + low : s * SEG_PAD + high, :count] = share
                both.append(jnp.dot(share, values[:count], preferred_element_type=f32))
            outs.append(jnp.where(first_head[low:high], both[0], both[1]))
        out = jnp.concatenate(outs, axis=0).astype(bf16)
        store_segment(o_ref, starts[s], rows_padded, out)


def attend(qkv, bias, me, mp_count, rows_padded):
    rows, width = qkv.shape
    pairs = width // 3 // 128
    return pl.pallas_call(
        functools.partial(attend_kernel, mp_count, rows_padded),
        out_shape=(
            jax.ShapeDtypeStruct((rows, width // 3), bf16),
            jax.ShapeDtypeStruct((pairs * 2, rows, KEYS), bf16),
        ),
        grid_spec=pltpu.PrefetchScalarGridSpec(
            num_scalar_prefetch=1,
            grid=(pairs,),
            in_specs=[
                pl.BlockSpec((rows, 128), lambda n, me_ref: (0, n)),
                pl.BlockSpec((rows, 128), lambda n, me_ref: (0, pairs + n)),
                pl.BlockSpec((rows, 128), lambda n, me_ref: (0, 2 * pairs + n)),
                pl.BlockSpec(bias.shape, lambda n, me_ref: (0, 0, 0)),
            ],
            out_specs=(
                pl.BlockSpec((rows, 128), lambda n, me_ref: (0, n)),
                pl.BlockSpec((2, rows, KEYS), lambda n, me_ref: (n, 0, 0)),
            ),
        ),
        compiler_params=pltpu.CompilerParams(vmem_limit_bytes=48 * 2**20),
        name="attend",
    )(me, qkv, qkv, qkv, bias)


def attend_back_kernel(
    mp_count,
    rows_padded,
    me_ref,
    q_ref,
    k_ref,
    v_ref,
    o_ref,
    g_ref,
    p_ref,
    dq_ref,
    dk_ref,
    dv_ref,
    key_sum,
    value_sum,
):
    starts = segment_starts(me_ref[0], mp_count, rows_padded)
    key_sum[...] = jnp.zeros_like(key_sum)
    value_sum[...] = jnp.zeros_like(value_sum)
    for s in range(NSEG):
        keys = jnp.concatenate(
            [load_slab(k_ref, starts[e], rows_padded) for e in range(s)]
            + [load_segment(k_ref, starts[s], rows_padded)],
            axis=0,
        )
        values = jnp.concatenate(
            [load_slab(v_ref, starts[e], rows_padded) for e in range(s)]
            + [load_segment(v_ref, starts[s], rows_padded)],
            axis=0,
        )
        queries = load_segment(q_ref, starts[s], rows_padded)
        grads = load_segment(g_ref, starts[s], rows_padded)
        outs = load_segment(o_ref, starts[s], rows_padded)
        queries_turned = queries.astype(f32).T.astype(bf16)
        grads_turned = grads.astype(f32).T.astype(bf16)
        first_head = lane_halves(queries.shape)
        zero = jnp.zeros_like(queries)
        head_grads = (jnp.where(first_head, grads, zero), jnp.where(first_head, zero, grads))
        product = grads.astype(f32) * outs.astype(f32)
        head_deltas = (
            jnp.sum(jnp.where(first_head, product, 0.0), axis=-1, keepdims=True),
            jnp.sum(jnp.where(first_head, 0.0, product), axis=-1, keepdims=True),
        )
        query_grads = []
        for low, high in query_blocks:
            count = SLAB * s + high
            both = []
            for h in range(2):
                share = p_ref[h, s * SEG_PAD + low : s * SEG_PAD + high, :count]
                share_grad = lax.dot_general(
                    head_grads[h][low:high],
                    values[:count],
                    (((1,), (1,)), ((), ())),
                    preferred_element_type=f32,
                )
                score_grad = (
                    share.astype(f32) * (share_grad - head_deltas[h][low:high])
                ).astype(bf16)
                both.append(jnp.dot(score_grad, keys[:count], preferred_element_type=f32))
                lanes = slice(h * HEAD_DIM, (h + 1) * HEAD_DIM)
                value_part = jnp.dot(
                    grads_turned[lanes, low:high], share, preferred_element_type=f32
                )
                key_part = jnp.dot(
                    queries_turned[lanes, low:high], score_grad, preferred_element_type=f32
                )
                for e in range(s):
                    place = slice((e + 1) * SEG_PAD - SLAB, (e + 1) * SEG_PAD)
                    value_sum[lanes, place] += value_part[:, e * SLAB : (e + 1) * SLAB]
                    key_sum[lanes, place] += key_part[:, e * SLAB : (e + 1) * SLAB]
                place = slice(s * SEG_PAD, s * SEG_PAD + high)
                value_sum[lanes, place] += value_part[:, s * SLAB :]
                key_sum[lanes, place] += key_part[:, s * SLAB :]
            query_grads.append(jnp.where(first_head[low:high], both[0], both[1]))
        query_grad = (jnp.concatenate(query_grads, axis=0) * score_scale).astype(bf16)
        store_segment(dq_ref, starts[s], rows_padded, query_grad)
    key_all = key_sum[...].T.astype(bf16)
    value_all = value_sum[...].T.astype(bf16)
    for s in range(NSEG):
        place = slice(s * SEG_PAD, (s + 1) * SEG_PAD)
        store_segment(dk_ref, starts[s], rows_padded, key_all[place])
        store_segment(dv_ref, starts[s], rows_padded, value_all[place])


def attend_back(qkv, out, grad, share, me, mp_count, rows_padded):
    rows, width = qkv.shape
    pairs = width // 3 // 128
    column = pl.BlockSpec((rows, 128), lambda n, me_ref: (0, n))
    piece = jax.ShapeDtypeStruct((rows, width // 3), bf16)
    return pl.pallas_call(
        functools.partial(attend_back_kernel, mp_count, rows_padded),
        out_shape=(piece, piece, piece),
        grid_spec=pltpu.PrefetchScalarGridSpec(
            num_scalar_prefetch=1,
            grid=(pairs,),
            in_specs=[
                column,
                pl.BlockSpec((rows, 128), lambda n, me_ref: (0, pairs + n)),
                pl.BlockSpec((rows, 128), lambda n, me_ref: (0, 2 * pairs + n)),
                column,
                column,
                pl.BlockSpec((2, rows, KEYS), lambda n, me_ref: (n, 0, 0)),
            ],
            out_specs=(column, column, column),
            scratch_shapes=[pltpu.VMEM((128, rows), f32), pltpu.VMEM((128, rows), f32)],
        ),
        compiler_params=pltpu.CompilerParams(vmem_limit_bytes=48 * 2**20),
        name="attend_back",
    )(me, qkv, qkv, qkv, out, grad, share)


def item_rows(present, summary, parts, rows, rows_padded):
    kept = present[:, None] * jnp.concatenate([jnp.ones((NSEG, SEG), jnp.int32), summary], axis=1)
    group = parts // NSEG
    kept = jnp.pad(kept.reshape(NSEG, group, rows), ((0, 0), (0, 0), (0, rows_padded - rows)))
    flags = np.zeros((group, rows_padded), np.int32)
    flags[:, :rows] = (np.arange(PERIOD) >= SEG).reshape(group, rows)
    return kept.reshape(NSEG, group * rows_padded), flags.reshape(group * rows_padded)


def score_bias(kept, flags):
    slab = (kept * flags[None, :])[:, SEG_PAD - SLAB :] == 1
    causal = np.tril(np.ones((SEG_PAD, SEG_PAD), bool))
    itself = np.eye(SEG_PAD, dtype=bool)
    planes = []
    for s in range(NSEG):
        own = (kept[s][None, :] == 1) & causal | itself
        pieces = [jnp.broadcast_to(slab[e][None, :], (SEG_PAD, SLAB)) for e in range(s)] + [own]
        seen = jnp.concatenate(pieces, axis=1)
        planes.append(jnp.pad(seen, ((0, 0), (0, KEYS - seen.shape[1]))))
    return jnp.where(jnp.stack(planes), 0.0, -1e30).astype(f32)


def norm_parts(value):
    center = value - jnp.mean(value, axis=-1, keepdims=True)
    spread = jnp.mean(center * center, axis=-1, keepdims=True)
    scale = lax.rsqrt(spread + norm_eps)
    return center * scale, scale


def norm_back(normed, scale, gain, grad):
    inner = grad * gain
    return scale * (
        inner
        - jnp.mean(inner, axis=-1, keepdims=True)
        - normed * jnp.mean(inner * normed, axis=-1, keepdims=True)
    )


def gelu_both(value):
    c = 0.7978845608028654
    square = value * value
    bend = jnp.tanh(c * (value + 0.044715 * value * square))
    half = 0.5 * (1.0 + bend)
    slope = half + 0.5 * value * (1.0 - bend * bend) * c * (1.0 + 3.0 * 0.044715 * square)
    return value * half, slope


def adam_step(master, grad, first, second, average, factor, rate, decay):
    clipped = grad * factor
    first_new = beta_first * first + (1.0 - beta_first) * clipped
    second_new = beta_second * second + (1.0 - beta_second) * clipped * clipped
    first_hat = first_new / (1.0 - beta_first**STEP)
    second_hat = second_new / (1.0 - beta_second**STEP)
    master_new = master - rate * (first_hat / (jnp.sqrt(second_hat) + adam_eps) + decay * master)
    average_new = average_keep * average + (1.0 - average_keep) * master_new
    return (master_new, first_new, second_new, average_new, master_new.astype(bf16))


def dot_nn(left, right):
    return jnp.dot(left, right, preferred_element_type=f32)


def dot_nt(left, right):
    return lax.dot_general(left, right, (((1,), (1,)), ((), ())), preferred_element_type=f32)


def dot_tn(left, right):
    return lax.dot_general(left, right, (((0,), (0,)), ((), ())), preferred_element_type=f32)


def per_device(
    tokens,
    cotangent,
    present,
    summary_mask,
    attention_weight,
    attention_first,
    attention_second,
    attention_average,
    hidden_weight,
    hidden_first,
    hidden_second,
    hidden_average,
    norm_params,
    norm_first,
    norm_second,
    norm_average,
    head_bias,
    head_first,
    head_second,
    head_average,
    unit_bias,
    unit_first,
    unit_second,
    unit_average,
):
    outer, inner = seq_grid()
    seqs = outer * inner
    parts = lax.axis_size("mp")
    rows = tokens.shape[0]
    rows_padded = SEG_PAD * NSEG // parts
    head_width = attention_weight.shape[2]
    depth = attention_weight.shape[1]
    me = lax.axis_index("mp")
    me_vector = me.astype(jnp.int32)[None]
    order = feature_order()
    codes = row_codes()

    inputs_own = to_blocks(tokens, order, rows_padded)
    cotangent_own = to_blocks(cotangent, order, rows_padded)
    inputs_all = gather_rows(inputs_own)
    cotangent_all = gather_rows(cotangent_own)

    attn_own = jnp.concatenate([attention_weight[n] for n in range(4)], axis=1).astype(bf16)
    attn_full = gather_weight(attn_own)
    up_full = gather_weight(hidden_weight[0].astype(bf16))
    down_full = gather_weight(hidden_weight[1].astype(bf16))
    qkv_full = attn_full[:, : 3 * head_width]
    out_full = attn_full[:, 3 * head_width :]

    packed = jnp.concatenate(
        [norm_params.reshape(-1), head_bias.reshape(-1), unit_bias]
    ).astype(bf16)
    packed = lax.all_gather(packed, "seq", axis=0, tiled=False).astype(f32)
    norm_size, head_size = norm_params.size, head_bias.size
    norm_vals = jnp.take(packed[:, :norm_size], order, axis=0).reshape(seqs, 6, depth)
    norm_vals = norm_vals.transpose(1, 0, 2).reshape(6, D)
    head_vals = packed[:, norm_size : norm_size + head_size].reshape(seqs, 2, head_width // seqs)
    head_vals = head_vals.transpose(1, 0, 2).reshape(2, head_width)
    unit_vals = packed[:, norm_size + head_size :].reshape(-1)

    kept, flags = item_rows(present[0], summary_mask[0], parts, rows, rows_padded)
    bias = score_bias(kept, flags)
    kept_parts = kept.reshape(parts, rows_padded).astype(f32)
    kept_all = jnp.take(kept_parts, jnp.stack([me ^ code for code in codes]), axis=0).reshape(-1, 1)
    kept_own = kept_all[:rows_padded]

    normed_all = norm_parts(inputs_all.astype(f32))[0]
    first_all = (normed_all * norm_vals[0] + norm_vals[1]).astype(bf16)
    qkv_bias = jnp.concatenate([head_vals[0], jnp.zeros_like(head_vals[0]), head_vals[1]])
    qkv_scale = np.concatenate(
        [np.full(head_width, score_scale, np.float32), np.ones(2 * head_width, np.float32)]
    )
    qkv = ((dot_nn(first_all, qkv_full) + qkv_bias).astype(bf16) * qkv_scale.astype(bf16))
    context, share = attend(qkv, bias, me_vector, parts, rows_padded)
    attended = scatter_rows(dot_nt(context, out_full).astype(bf16)) + norm_vals[4]
    inputs = inputs_own.astype(f32)
    middle = inputs + kept_own * attended

    normed_two, scale_two = norm_parts(middle)
    second_own = (normed_two * norm_vals[2] + norm_vals[3]).astype(bf16)
    second_all = gather_rows(second_own)
    pre_act = dot_nn(second_all, up_full) + unit_vals
    activated, slope = gelu_both(pre_act)
    activated, slope = activated.astype(bf16), slope.astype(bf16)
    feed_out = scatter_rows(dot_nt(activated, down_full).astype(bf16)) + norm_vals[5]
    block_output = from_blocks(middle + kept_own * feed_out, order, rows)

    out_grad = cotangent_own.astype(f32)
    feed_grad = (cotangent_all.astype(f32) * kept_all).astype(bf16)
    down_bias_grad = jnp.sum(kept_own * out_grad, axis=0)

    def columns(value, j, i):
        place = j * outer + i
        return value[:, place * depth : (place + 1) * depth]

    down_grad = scatter_weight(lambda j, i: dot_tn(columns(feed_grad, j, i), activated))
    pre_grad = (dot_nn(feed_grad, down_full) * slope.astype(f32)).astype(bf16)
    unit_grad = jnp.sum(pre_grad, axis=0, dtype=f32)
    second_grad = scatter_rows(dot_nt(pre_grad, up_full).astype(bf16))
    up_grad = scatter_weight(lambda j, i: dot_tn(columns(second_all, j, i), pre_grad))
    gain_two_grad = jnp.sum(second_grad * normed_two, axis=0)
    shift_two_grad = jnp.sum(second_grad, axis=0)
    middle_grad = out_grad + norm_back(normed_two, scale_two, norm_vals[2], second_grad)

    attn_grad = kept_own * middle_grad
    out_bias_grad = jnp.sum(attn_grad, axis=0)
    attn_rows = gather_rows(attn_grad.astype(bf16))
    context_grad = dot_nn(attn_rows, out_full).astype(bf16)
    out_proj_grad = scatter_weight(lambda j, i: dot_tn(columns(attn_rows, j, i), context))
    query_grad, key_grad, value_grad = attend_back(
        qkv, context, context_grad, share, me_vector, parts, rows_padded
    )
    qkv_grad = jnp.concatenate([query_grad, key_grad, value_grad], axis=1)
    head_grad = jnp.stack(
        [jnp.sum(query_grad, axis=0, dtype=f32), jnp.sum(value_grad, axis=0, dtype=f32)]
    )
    first_grad = scatter_rows(dot_nt(qkv_grad, qkv_full).astype(bf16))
    proj_grad = scatter_weight(lambda j, i: dot_tn(columns(first_all, j, i), qkv_grad))
    normed_one, scale_one = norm_parts(inputs)
    gain_one_grad = jnp.sum(first_grad * normed_one, axis=0)
    shift_one_grad = jnp.sum(first_grad, axis=0)
    input_grad = from_blocks(
        middle_grad + norm_back(normed_one, scale_one, norm_vals[0], first_grad), order, rows
    )

    vector_grad = jnp.stack(
        [
            gain_one_grad,
            shift_one_grad,
            gain_two_grad,
            shift_two_grad,
            out_bias_grad,
            down_bias_grad,
        ]
    )
    back_order = jnp.argsort(order)
    vector_grad = jnp.take(
        vector_grad.reshape(6, seqs, depth).transpose(1, 0, 2).reshape(seqs, -1), back_order, axis=0
    )
    vectors = jnp.concatenate(
        [
            vector_grad,
            head_grad.reshape(2, seqs, -1).transpose(1, 0, 2).reshape(seqs, -1),
            unit_grad.reshape(seqs, -1),
        ],
        axis=1,
    )
    vectors = lax.psum_scatter(vectors, "seq", scatter_dimension=0, tiled=False)
    norm_shard = lax.psum(vectors[:norm_size], "mp").reshape(norm_params.shape)
    head_shard = vectors[norm_size : norm_size + head_size].reshape(head_bias.shape)
    unit_shard = vectors[norm_size + head_size :]

    proj_grad = proj_grad.reshape(depth, 3, head_width).transpose(1, 0, 2)
    attn_shard = jnp.concatenate([proj_grad, out_proj_grad[None]], axis=0)
    hidden_shard = jnp.stack([up_grad, down_grad])
    leader = (me == 0).astype(f32)
    local_squares = (
        jnp.sum(attn_shard * attn_shard)
        + jnp.sum(hidden_shard * hidden_shard)
        + jnp.sum(head_shard * head_shard)
        + jnp.sum(unit_shard * unit_shard)
        + leader * jnp.sum(norm_shard * norm_shard)
    )
    grad_norm = jnp.sqrt(lax.psum(local_squares, ("seq", "mp")))
    factor = jnp.minimum(1.0, clip_limit / (grad_norm + 1e-06))
    hidden_rate = jnp.array([D ** (-0.5), FF ** (-0.5)], f32)[:, None, None]
    attention_out = adam_step(
        attention_weight,
        attn_shard,
        attention_first,
        attention_second,
        attention_average,
        factor,
        D ** (-0.5),
        weight_decay,
    )
    hidden_out = adam_step(
        hidden_weight,
        hidden_shard,
        hidden_first,
        hidden_second,
        hidden_average,
        factor,
        hidden_rate,
        weight_decay,
    )
    norm_out = adam_step(
        norm_params, norm_shard, norm_first, norm_second, norm_average, factor, vector_rate, 0.0
    )
    head_out = adam_step(
        head_bias, head_shard, head_first, head_second, head_average, factor, vector_rate, 0.0
    )
    unit_out = adam_step(
        unit_bias, unit_shard, unit_first, unit_second, unit_average, factor, vector_rate, 0.0
    )
    return (
        block_output,
        input_grad,
        grad_norm,
        *attention_out,
        *hidden_out,
        *norm_out,
        *head_out,
        *unit_out,
    )


def solution(mesh):
    token_spec = P(("seq", "mp"), None)
    weight_spec = P(None, "seq", "mp")
    norm_spec = P(None, "seq")
    head_spec = P(None, ("mp", "seq"))
    unit_spec = P(("mp", "seq"))
    return jax.shard_map(
        per_device,
        mesh=mesh,
        in_specs=(
            token_spec,
            token_spec,
            P("seq", None),
            P("seq", None, None),
            *([weight_spec] * 8),
            *([norm_spec] * 4),
            *([head_spec] * 4),
            *([unit_spec] * 4),
        ),
        out_specs=(
            token_spec,
            token_spec,
            P(),
            *([weight_spec] * 10),
            *([norm_spec] * 5),
            *([head_spec] * 5),
            *([unit_spec] * 5),
        ),
        check_vma=False,
    )
```

```python
import functools

import jax
import jax.numpy as jnp
import numpy as np
from jax import lax
from jax.experimental import pallas as pl
from jax.experimental.pallas import tpu as pltpu
from jax.sharding import PartitionSpec as P

D = 2048
HEAD_DIM = 64
FF = 8192
SUMM = 50
NSEG = 4
SEG = 256
STEP = 10
PERIOD = SEG + SUMM
SEG_PAD = 320
SLAB = 64
KEYS = SLAB * (NSEG - 1) + SEG_PAD

norm_eps = 1e-05
beta_first = 0.9
beta_second = 0.95
adam_eps = 1e-08
clip_limit = 1.0
weight_decay = 0.1
average_keep = 0.6
vector_rate = 0.4
score_scale = HEAD_DIM ** (-0.5)
query_blocks = ((0, 128), (128, 256), (256, SEG_PAD))

RATE = 0.59e9

f32 = jnp.float32
bf16 = jnp.bfloat16


def seq_grid():
    count = lax.axis_size("seq")
    inner = count // 4
    return count // inner, inner


def shift_outer(value, step):
    outer, inner = seq_grid()
    pairs = [
        (a * inner + b, ((a + step) % outer) * inner + b) for a in range(outer) for b in range(inner)
    ]
    return lax.ppermute(value, "seq", pairs)


def shift_inner(value, step):
    outer, inner = seq_grid()
    pairs = [
        (a * inner + b, a * inner + (b + step) % inner) for a in range(outer) for b in range(inner)
    ]
    return lax.ppermute(value, "seq", pairs)


def swap(value, bits):
    return lax.ppermute(value, "mp", [(m, m ^ bits) for m in range(lax.axis_size("mp"))])


def block_order():
    outer, inner = seq_grid()
    me = lax.axis_index("seq")
    mine_a, mine_b = me // inner, me % inner
    return jnp.stack(
        [
            ((mine_b - b + inner) % inner) * outer + (mine_a - a + outer) % outer
            for a in range(outer)
            for b in range(inner)
        ]
    ).astype(jnp.int32)


def feature_order():
    outer, inner = seq_grid()
    me = lax.axis_index("seq")
    mine_a, mine_b = me // inner, me % inner
    return jnp.stack(
        [
            ((mine_a - i + outer) % outer) * inner + (mine_b - j + inner) % inner
            for j in range(inner)
            for i in range(outer)
        ]
    ).astype(jnp.int32)


def after(value, *others):
    return lax.optimization_barrier((value, *others))[0]


def row_codes():
    count = lax.axis_size("mp")
    return [high * 2 + low for low in range(2) for high in range(count // 2)]


def outer_groups():
    outer, inner = seq_grid()
    return [[a * inner + b for a in range(outer)] for b in range(inner)]


def block_spots():
    outer, inner = seq_grid()
    place = lax.axis_index("seq") // inner
    return jnp.stack([(place - i + outer) % outer for i in range(outer)]).astype(jnp.int32)


def ring_line(own):
    line = [own]
    for _ in range(seq_grid()[0] - 1):
        line.append(shift_outer(line[-1], 1))
    return line


def ring_rest(part):
    rest = []
    for _ in range(seq_grid()[1] - 1):
        part = shift_inner(part, 1)
        rest.append(part)
    return rest


def ring_scatter(parts, received):
    total = None
    for i in reversed(range(len(parts))):
        part = parts[i].astype(f32) + received[i].astype(f32)
        if total is not None:
            part = part + shift_outer(total.astype(bf16), -1).astype(f32)
        total = part
    return total


def inner_sum(parts):
    inner = seq_grid()[1]
    part = shift_inner(parts[inner - 1], -1)
    for j in reversed(range(1, inner - 1)):
        part = shift_inner((parts[j].astype(f32) + part.astype(f32)).astype(bf16), -1)
    return part


def greet(peers):
    barrier = pltpu.get_barrier_semaphore()
    for peer in peers:
        pl.semaphore_signal(barrier, inc=1, device_id=peer, device_id_type=pl.DeviceIdType.MESH)
    pl.semaphore_wait(barrier, len(peers))


def others(axis, count):
    me = lax.axis_index(axis)
    return [lax.rem(me + step, count) for step in range(1, count)]


def exchange(axis, count, pieces, slots, send_sems, recv_sems):
    copies = []
    for step, peer in enumerate(others(axis, count)):
        copy = pltpu.make_async_remote_copy(
            src_ref=pieces(peer),
            dst_ref=slots.at[step],
            send_sem=send_sems.at[step],
            recv_sem=recv_sems.at[step],
            device_id={axis: peer},
            device_id_type=pl.DeviceIdType.MESH,
        )
        copy.start()
        copies.append(copy)
    return copies


def reduce_vector_kernel(
    seqs, parts, shared, in_ref, out_ref, slots, sums, send_sems, recv_sems, send_two, recv_two
):
    greet(
        [{"seq": peer} for peer in others("seq", seqs)]
        + [{"mp": peer} for peer in others("mp", parts)]
    )
    copies = exchange("seq", seqs, lambda peer: in_ref.at[peer], slots, send_sems, recv_sems)
    total = in_ref[lax.axis_index("seq")]
    for step, copy in enumerate(copies):
        copy.wait()
        total = total + slots[step]
    out_ref[...] = total
    copies = exchange(
        "mp", parts, lambda peer: out_ref.at[:shared], sums, send_two, recv_two
    )
    for copy in copies:
        copy.wait()
    head = total[:shared]
    for step in range(parts - 1):
        head = head + sums[step]
    out_ref[:shared] = head


def reduce_vector(value, shared):
    seqs, parts = lax.axis_size("seq"), lax.axis_size("mp")
    vmem = pl.BlockSpec(memory_space=pltpu.VMEM)
    block = value.shape[1:]
    return pl.pallas_call(
        functools.partial(reduce_vector_kernel, seqs, parts, shared),
        out_shape=jax.ShapeDtypeStruct(block, value.dtype),
        in_specs=[vmem],
        out_specs=vmem,
        scratch_shapes=[
            pltpu.VMEM((seqs - 1, *block), value.dtype),
            pltpu.VMEM((parts - 1, shared, *block[1:]), value.dtype),
            pltpu.SemaphoreType.DMA((seqs - 1,)),
            pltpu.SemaphoreType.DMA((seqs - 1,)),
            pltpu.SemaphoreType.DMA((parts - 1,)),
            pltpu.SemaphoreType.DMA((parts - 1,)),
        ],
        compiler_params=pltpu.CompilerParams(collective_id=1, has_side_effects=True),
        name="reduce_vector",
    )(value)


def reduce_scalar_kernel(
    seqs, parts, in_ref, out_ref, slots, sums, send_sems, recv_sems, send_two, recv_two
):
    greet(
        [{"seq": peer} for peer in others("seq", seqs)]
        + [{"mp": peer} for peer in others("mp", parts)]
    )
    copies = exchange("mp", parts, lambda peer: in_ref, sums, send_two, recv_two)
    for copy in copies:
        copy.wait()
    me = lax.axis_index("mp")
    total = jnp.zeros_like(in_ref)
    for part in range(parts):
        step = lax.rem(me + parts - part - 1 + parts, parts)
        mine = part == me
        other = sums[jnp.minimum(step, parts - 2)]
        total = total + jnp.where(mine, in_ref[...], other)
    out_ref[...] = total
    copies = exchange("seq", seqs, lambda peer: out_ref, slots, send_sems, recv_sems)
    for copy in copies:
        copy.wait()
    me = lax.axis_index("seq")
    final = jnp.zeros_like(in_ref)
    for place in range(seqs):
        step = lax.rem(me + seqs - place - 1 + seqs, seqs)
        mine = place == me
        other = slots[jnp.minimum(step, seqs - 2)]
        final = final + jnp.where(mine, total, other)
    out_ref[...] = final


def reduce_scalar(value):
    seqs, parts = lax.axis_size("seq"), lax.axis_size("mp")
    vmem = pl.BlockSpec(memory_space=pltpu.VMEM)
    return pl.pallas_call(
        functools.partial(reduce_scalar_kernel, seqs, parts),
        out_shape=jax.ShapeDtypeStruct(value.shape, value.dtype),
        in_specs=[vmem],
        out_specs=vmem,
        scratch_shapes=[
            pltpu.VMEM((seqs - 1, *value.shape), value.dtype),
            pltpu.VMEM((parts - 1, *value.shape), value.dtype),
            pltpu.SemaphoreType.DMA((seqs - 1,)),
            pltpu.SemaphoreType.DMA((seqs - 1,)),
            pltpu.SemaphoreType.DMA((parts - 1,)),
            pltpu.SemaphoreType.DMA((parts - 1,)),
        ],
        compiler_params=pltpu.CompilerParams(collective_id=0, has_side_effects=True),
        name="reduce_scalar",
    )(value)


def gather_chips(own):
    high = [own]
    for bit in range(1, lax.axis_size("mp").bit_length() - 1):
        high = high + [swap(part, 1 << bit) for part in high]
    return high


def scatter_chips(first, second):
    count = lax.axis_size("mp") // 2
    rows = 2 * first.shape[0] // count
    total = first[:rows]
    for n in range(1, count):
        at = n * rows
        if at < first.shape[0]:
            part = first[at : at + rows].astype(bf16)
        else:
            part = second[at - first.shape[0] : at - first.shape[0] + rows]
        total = total + swap(part, n * 2).astype(f32)
    return total


def other_core():
    me = lax.axis_index("mp")
    return {"mp": me + 1 - 2 * lax.rem(me, 2)}


def core_copy(src, dst, send_sem, recv_sem):
    return pltpu.make_async_remote_copy(
        src_ref=src,
        dst_ref=dst,
        send_sem=send_sem,
        recv_sem=recv_sem,
        device_id=other_core(),
        device_id_type=pl.DeviceIdType.MESH,
    )


def kernel_params(number):
    return pltpu.CompilerParams(
        vmem_limit_bytes=56 * 2**20, collective_id=number, has_side_effects=True
    )


def expected(microseconds):
    return pl.CostEstimate(
        flops=int(microseconds * RATE), bytes_accessed=0, transcendentals=0
    )


def estimate(rows, depth, columns):
    return expected(1.5 + rows * depth * columns * 2 / 7.2e8)


def resident(shape):
    return pl.BlockSpec(shape, lambda *place: (0,) * len(shape))


def arrange_kernel(lefts, blocks, grid, normed, *refs):
    pieces, rest = refs[:lefts], refs[lefts:-3]
    got, send_sem, recv_sem = refs[-3:]
    out_ref, own_ref = rest[-2:]
    step = pl.program_id(0)
    rows, width = pieces[0].shape
    wide = width // blocks
    outer, inner = grid
    me = lax.axis_index("seq")
    mine_a, mine_b = me // inner, lax.rem(me, inner)

    def copy(n):
        return core_copy(pieces[n], got.at[n], send_sem.at[n], recv_sem.at[n])

    @pl.when(step == 0)
    def _():
        greet([other_core()])
        for n in range(lefts):
            copy(n).start()

    def fill(p, load):
        if normed:
            value = load(slice(None)).astype(f32)
            mean = jnp.mean(value, axis=-1, keepdims=True)
            center = value - mean
            scale = lax.rsqrt(jnp.mean(center * center, axis=-1, keepdims=True) + norm_eps)
        for b in range(blocks):
            place = lax.rem(mine_a - b % outer + outer, outer) * inner
            place = place + lax.rem(mine_b - b // outer + inner, inner)
            here = slice(b * wide, (b + 1) * wide)
            part = load(pl.ds(pl.multiple_of(place * wide, wide), wide))
            if p == 0:
                own_ref[:, here] = part
            part = part.astype(f32)
            if normed:
                part = (part - mean) * scale * rest[0][:, here] + rest[1][:, here]
            else:
                part = part * rest[0][...]
            out_ref[:, here] = part.astype(bf16)

    for n in range(lefts):

        @pl.when(step == n)
        def _(n=n):
            fill(n, lambda columns: pieces[n][:, columns])

        @pl.when(step == lefts + n)
        def _(n=n):
            copy(n).wait()
            fill(lefts + n, lambda columns: got[n, :, columns])


def arrange(pieces, extras, extra_specs, normed, number, name):
    rows, width = pieces[0].shape
    lefts = len(pieces)
    return pl.pallas_call(
        functools.partial(arrange_kernel, lefts, lax.axis_size("seq"), seq_grid(), normed),
        out_shape=[
            jax.ShapeDtypeStruct((2 * lefts * rows, width), bf16),
            jax.ShapeDtypeStruct((rows, width), bf16),
        ],
        grid=(2 * lefts,),
        in_specs=[resident((rows, width))] * lefts + extra_specs,
        out_specs=[pl.BlockSpec((rows, width), lambda n: (n, 0)), resident((rows, width))],
        scratch_shapes=[
            pltpu.VMEM((lefts, rows, width), bf16),
            pltpu.SemaphoreType.DMA((lefts,)),
            pltpu.SemaphoreType.DMA((lefts,)),
        ],
        compiler_params=kernel_params(number),
        cost_estimate=expected(9.0),
        name=name,
    )(*pieces, *extras)


def tall_kernel(epilogue, exchanged, lefts, blocks, extras, *refs):
    weight = jnp.concatenate([ref[...] for ref in refs[lefts : lefts + blocks]], axis=0)
    rest = refs[lefts + blocks :]
    step = pl.program_id(0)
    rows = refs[0].shape[0]
    if exchanged:
        others_ref, got, send_sem, recv_sem = rest[-4:]
        rest = rest[:-4]

        def copy(n):
            return core_copy(refs[n], got.at[n], send_sem.at[n], recv_sem.at[n])

        @pl.when(step == 0)
        def _():
            greet([other_core()])
            for n in range(lefts):
                copy(n).start()

    def fill(left, at):
        result = jnp.dot(left, weight, preferred_element_type=f32)
        epilogue(result, slice(at, at + rows), rest[:extras], rest[extras:])

    for n in range(lefts):
        fill(refs[n][...], n * rows)
    if exchanged:

        @pl.when(step == 0)
        def _():
            for n in range(lefts):
                copy(n).wait()

        for n in range(lefts):
            fill(got[n], (lefts + n) * rows)

        @pl.when(step == pl.num_programs(0) - 1)
        def _():
            for n in range(lefts):
                others_ref[n * rows : (n + 1) * rows, :] = got[n]


def tall_dot(lefts, blocks, start, width, epilogue, extras, outs, name, number=None):
    rows, depth = lefts[0].shape
    exchanged = number is not None
    count = len(lefts) * (2 if exchanged else 1)
    tile = max(size for size in (128, 256, 512) if width % size == 0 and start % size == 0)
    first = start // tile
    block_depth = depth // lax.axis_size("seq")
    specs = []
    for block in blocks:
        high = block_depth if block.shape[0] // block_depth < 2 else block.shape[0]
        specs.append(pl.BlockSpec((high, tile), lambda n: (0, first + n)))
    out_shape = [jax.ShapeDtypeStruct((height, width), dtype) for height, dtype in outs]
    out_specs = [pl.BlockSpec((height, tile), lambda n: (0, n)) for height, _ in outs]
    scratch = []
    params = pltpu.CompilerParams(vmem_limit_bytes=56 * 2**20)
    if exchanged:
        out_shape.append(jax.ShapeDtypeStruct((len(lefts) * rows, depth), bf16))
        out_specs.append(resident((len(lefts) * rows, depth)))
        scratch = [
            pltpu.VMEM((len(lefts), rows, depth), bf16),
            pltpu.SemaphoreType.DMA((len(lefts),)),
            pltpu.SemaphoreType.DMA((len(lefts),)),
        ]
        params = kernel_params(number)
    return pl.pallas_call(
        functools.partial(
            tall_kernel, epilogue, exchanged, len(lefts), len(blocks), len(extras)
        ),
        out_shape=out_shape,
        grid=(width // tile,),
        in_specs=[resident(left.shape) for left in lefts]
        + specs
        + [pl.BlockSpec((extra.shape[0], tile), lambda n: (0, n)) for extra in extras],
        out_specs=out_specs,
        scratch_shapes=scratch,
        compiler_params=params,
        cost_estimate=estimate(rows * count, depth, width),
        name=name,
    )(*lefts, *blocks, *extras)


def plain_epilogue(result, here, extras, outs):
    outs[0][here, :] = result.astype(bf16)


def project_epilogue(result, here, extras, outs):
    bias, scale = extras
    outs[0][here, :] = ((result + bias[...]).astype(bf16).astype(f32) * scale[...]).astype(bf16)


def up_epilogue(result, here, extras, outs):
    value, slope = gelu_both(result + extras[0][...])
    outs[0][here, :] = value.astype(bf16)
    outs[1][here, :] = slope.astype(bf16)


def slope_epilogue(result, here, extras, outs):
    grad = (result * extras[0][here, :].astype(f32)).astype(bf16)
    outs[0][here, :] = grad
    sums = jnp.sum(grad.astype(f32), axis=0, keepdims=True)
    outs[1][...] = jnp.broadcast_to(sums, outs[1].shape)


def wide_kernel(blocks, start, left_ref, *refs):
    first_ref, second_ref, sent, got, send_sem, recv_sem = refs[blocks:]
    step = pl.program_id(0)
    columns = slice(start, start + left_ref.shape[1])

    def copy(n):
        return core_copy(sent.at[n], got.at[n], send_sem.at[n], recv_sem.at[n])

    @pl.when(step == 0)
    def _():
        greet([other_core()])

    result = lax.dot_general(
        left_ref[...],
        jnp.concatenate([ref[:, columns] for ref in refs[:blocks]], axis=0),
        (((1,), (1,)), ((), ())),
        preferred_element_type=f32,
    )
    for n in range(2):

        @pl.when(step == n)
        def _(n=n):
            sent[n] = result.astype(bf16)
            copy(n).start()

    @pl.when(step == 2)
    def _():
        copy(0).wait()
        second_ref[...] = (result + got[0].astype(f32)).astype(bf16)

    @pl.when(step == 3)
    def _():
        copy(1).wait()
        first_ref[...] = result + got[1].astype(f32)


def wide_dot(left, blocks, start, features, number, name):
    rows, width = left.shape
    tile = rows // 4
    block_depth = features // lax.axis_size("seq")
    specs = []
    for block in blocks:
        high = block_depth if block.shape[0] // block_depth < 2 else block.shape[0]
        specs.append(resident((high, block.shape[1])))
    return pl.pallas_call(
        functools.partial(wide_kernel, len(blocks), start),
        out_shape=[
            jax.ShapeDtypeStruct((tile, features), f32),
            jax.ShapeDtypeStruct((tile, features), bf16),
        ],
        grid=(4,),
        in_specs=[pl.BlockSpec((tile, width), lambda n: (3 - n, 0))] + specs,
        out_specs=[resident((tile, features)), resident((tile, features))],
        scratch_shapes=[
            pltpu.VMEM((2, tile, features), bf16),
            pltpu.VMEM((2, tile, features), bf16),
            pltpu.SemaphoreType.DMA((2,)),
            pltpu.SemaphoreType.DMA((2,)),
        ],
        compiler_params=kernel_params(number),
        cost_estimate=estimate(rows, width, features),
        name=name,
    )(left, *blocks)


def turned_kernel(shapes, split, added, spots_ref, *refs):
    refs = list(refs)
    groups = [[refs.pop(0) for _ in range(count)] for count in shapes]
    rights = [refs.pop(0) for _ in shapes]
    add_ref = refs.pop(0) if added else None

    def fill(out_ref):
        at = 0
        for lefts, right_ref in zip(groups, rights):
            width = right_ref.shape[1]
            left = jnp.concatenate([ref[...] for ref in lefts], axis=0)
            result = lax.dot_general(
                left, right_ref[...], (((0,), (0,)), ((), ())), preferred_element_type=f32
            )
            if added:
                result = result + add_ref[:, at : at + width].astype(f32)
            out_ref[:, at : at + width] = result.astype(bf16)
            at += width

    if split:
        for n, out_ref in enumerate(refs):
            pl.when(pl.program_id(0) == n)(functools.partial(fill, out_ref))
    else:
        fill(refs[0])


def turned_dot(pairs, first, spots, depth, name, split=False, add=None):
    count = spots.shape[0]
    width = sum(right.shape[1] for _, right in pairs)
    rows = pairs[0][1].shape[0]
    block = jax.ShapeDtypeStruct((depth, width), bf16)
    if split:
        out_shape, out_specs = [block] * count, [resident((depth, width))] * count
    else:
        out_shape = [jax.ShapeDtypeStruct((count * depth, width), bf16)]
        if add is None:
            out_specs = [pl.BlockSpec((depth, width), lambda n, spots_ref: (n, 0))]
        else:
            out_specs = [pl.BlockSpec((depth, width), lambda n, spots_ref: (spots_ref[n], 0))]
    adds = [] if add is None else [add]
    return pl.pallas_call(
        functools.partial(
            turned_kernel, [len(lefts) for lefts, _ in pairs], split, add is not None
        ),
        out_shape=out_shape,
        grid_spec=pltpu.PrefetchScalarGridSpec(
            num_scalar_prefetch=1,
            grid=(count,),
            in_specs=[
                pl.BlockSpec((left.shape[0], depth), lambda n, spots_ref: (0, first + n))
                for lefts, _ in pairs
                for left in lefts
            ]
            + [resident(right.shape) for _, right in pairs]
            + [pl.BlockSpec((depth, width), lambda n, spots_ref: (n, 0))] * len(adds),
            out_specs=out_specs,
        ),
        compiler_params=pltpu.CompilerParams(vmem_limit_bytes=56 * 2**20),
        cost_estimate=estimate(rows, count * depth, width),
        name=name,
    )(
        spots,
        *[left for lefts, _ in pairs for left in lefts],
        *[right for _, right in pairs],
        *adds,
    )


def far_grads(pairs, spots, depth, name, split=False):
    outer, inner = seq_grid()
    return [None] + [
        turned_dot(pairs, j * outer, spots, depth, name + "_far", split=split)
        for j in range(1, inner)
    ]


def line_scatter(pairs, received, spots, depth, name):
    near = turned_dot(pairs, 0, spots, depth, name + "_near", add=received)[0]
    return lax.psum_scatter(
        near, "seq", scatter_dimension=0, tiled=True, axis_index_groups=outer_groups()
    )


def from_blocks_kernel(blocks, order_ref, in_ref, out_ref):
    rows, width = out_ref.shape
    wide = width // blocks
    for b in range(blocks):
        there = pl.ds(pl.multiple_of(order_ref[b] * wide, wide), wide)
        out_ref[:, there] = in_ref[:rows, b * wide : (b + 1) * wide].astype(out_ref.dtype)


def from_blocks(value, order, rows):
    rows_padded, width = value.shape
    return pl.pallas_call(
        functools.partial(from_blocks_kernel, order.shape[0]),
        out_shape=jax.ShapeDtypeStruct((rows, width), bf16),
        in_specs=[
            pl.BlockSpec(memory_space=pltpu.SMEM),
            pl.BlockSpec(memory_space=pltpu.VMEM),
        ],
        out_specs=pl.BlockSpec(memory_space=pltpu.VMEM),
        compiler_params=pltpu.CompilerParams(vmem_limit_bytes=40 * 2**20),
        cost_estimate=expected(3.0),
        name="from_blocks",
    )(order, value)


def segment_starts(me, mp_count, rows_padded):
    group = mp_count // NSEG
    starts = []
    for s in range(NSEG):
        pieces = []
        for r in range(group):
            code = jnp.bitwise_xor(me, s * group + r)
            place = jnp.bitwise_and(code, 1) * (mp_count // 2) + lax.shift_right_logical(code, 1)
            pieces.append(pl.multiple_of(place * rows_padded, rows_padded))
        starts.append(pieces)
    return starts


def load_segment(ref, pieces, rows_padded):
    parts = [ref[pl.ds(start, rows_padded), :] for start in pieces]
    return parts[0] if len(parts) == 1 else jnp.concatenate(parts, axis=0)


def load_slab(ref, pieces, rows_padded):
    return ref[pl.ds(pl.multiple_of(pieces[-1] + (rows_padded - SLAB), 16), SLAB), :]


def store_segment(ref, pieces, rows_padded, value):
    for r, start in enumerate(pieces):
        ref[pl.ds(start, rows_padded), :] = value[r * rows_padded : (r + 1) * rows_padded]


def lane_halves(shape):
    lane = lax.broadcasted_iota(jnp.int32, shape, 1)
    return lane < HEAD_DIM


def attend_kernel(mp_count, rows_padded, me_ref, q_ref, k_ref, v_ref, bias_ref, o_ref, p_ref):
    starts = segment_starts(me_ref[0], mp_count, rows_padded)
    for s in range(NSEG):
        keys = jnp.concatenate(
            [load_slab(k_ref, starts[e], rows_padded) for e in range(s)]
            + [load_segment(k_ref, starts[s], rows_padded)],
            axis=0,
        )
        values = jnp.concatenate(
            [load_slab(v_ref, starts[e], rows_padded) for e in range(s)]
            + [load_segment(v_ref, starts[s], rows_padded)],
            axis=0,
        )
        queries = load_segment(q_ref, starts[s], rows_padded)
        first_head = lane_halves(queries.shape)
        zero = jnp.zeros_like(queries)
        head_queries = (jnp.where(first_head, queries, zero), jnp.where(first_head, zero, queries))
        outs = []
        for low, high in query_blocks:
            count = SLAB * s + high
            bias = bias_ref[s, low:high, :count]
            both = []
            for h in range(2):
                scores = (
                    lax.dot_general(
                        head_queries[h][low:high],
                        keys[:count],
                        (((1,), (1,)), ((), ())),
                        preferred_element_type=f32,
                    )
                    + bias
                )
                peak = jnp.max(scores, axis=-1, keepdims=True)
                raised = jnp.exp(scores - peak)
                share = raised * (1.0 / jnp.sum(raised, axis=-1, keepdims=True))
                share = share.astype(bf16)
                p_ref[h, s * SEG_PAD + low : s * SEG_PAD + high, :count] = share
                both.append(jnp.dot(share, values[:count], preferred_element_type=f32))
            outs.append(jnp.where(first_head[low:high], both[0], both[1]))
        out = jnp.concatenate(outs, axis=0).astype(bf16)
        store_segment(o_ref, starts[s], rows_padded, out)


def attend(qkv, bias, me, mp_count, rows_padded):
    rows, width = qkv.shape
    pairs = width // 3 // 128
    return pl.pallas_call(
        functools.partial(attend_kernel, mp_count, rows_padded),
        out_shape=(
            jax.ShapeDtypeStruct((rows, width // 3), bf16),
            jax.ShapeDtypeStruct((pairs * 2, rows, KEYS), bf16),
        ),
        grid_spec=pltpu.PrefetchScalarGridSpec(
            num_scalar_prefetch=1,
            grid=(pairs,),
            in_specs=[
                pl.BlockSpec((rows, 128), lambda n, me_ref: (0, n)),
                pl.BlockSpec((rows, 128), lambda n, me_ref: (0, pairs + n)),
                pl.BlockSpec((rows, 128), lambda n, me_ref: (0, 2 * pairs + n)),
                pl.BlockSpec(bias.shape, lambda n, me_ref: (0, 0, 0)),
            ],
            out_specs=(
                pl.BlockSpec((rows, 128), lambda n, me_ref: (0, n)),
                pl.BlockSpec((2, rows, KEYS), lambda n, me_ref: (n, 0, 0)),
            ),
        ),
        compiler_params=pltpu.CompilerParams(vmem_limit_bytes=48 * 2**20),
        cost_estimate=expected(36.0),
        name="attend",
    )(me, qkv, qkv, qkv, bias)


def attend_back_kernel(
    mp_count,
    rows_padded,
    me_ref,
    q_ref,
    k_ref,
    v_ref,
    o_ref,
    g_ref,
    p_ref,
    dq_ref,
    dk_ref,
    dv_ref,
    key_sum,
    value_sum,
):
    starts = segment_starts(me_ref[0], mp_count, rows_padded)
    key_sum[...] = jnp.zeros_like(key_sum)
    value_sum[...] = jnp.zeros_like(value_sum)
    for s in range(NSEG):
        keys = jnp.concatenate(
            [load_slab(k_ref, starts[e], rows_padded) for e in range(s)]
            + [load_segment(k_ref, starts[s], rows_padded)],
            axis=0,
        )
        values = jnp.concatenate(
            [load_slab(v_ref, starts[e], rows_padded) for e in range(s)]
            + [load_segment(v_ref, starts[s], rows_padded)],
            axis=0,
        )
        queries = load_segment(q_ref, starts[s], rows_padded)
        grads = load_segment(g_ref, starts[s], rows_padded)
        outs = load_segment(o_ref, starts[s], rows_padded)
        queries_turned = queries.astype(f32).T.astype(bf16)
        grads_turned = grads.astype(f32).T.astype(bf16)
        first_head = lane_halves(queries.shape)
        zero = jnp.zeros_like(queries)
        head_grads = (jnp.where(first_head, grads, zero), jnp.where(first_head, zero, grads))
        product = grads.astype(f32) * outs.astype(f32)
        head_deltas = (
            jnp.sum(jnp.where(first_head, product, 0.0), axis=-1, keepdims=True),
            jnp.sum(jnp.where(first_head, 0.0, product), axis=-1, keepdims=True),
        )
        query_grads = []
        for low, high in query_blocks:
            count = SLAB * s + high
            both = []
            for h in range(2):
                share = p_ref[h, s * SEG_PAD + low : s * SEG_PAD + high, :count]
                share_grad = lax.dot_general(
                    head_grads[h][low:high],
                    values[:count],
                    (((1,), (1,)), ((), ())),
                    preferred_element_type=f32,
                )
                score_grad = (
                    share.astype(f32) * (share_grad - head_deltas[h][low:high])
                ).astype(bf16)
                both.append(jnp.dot(score_grad, keys[:count], preferred_element_type=f32))
                lanes = slice(h * HEAD_DIM, (h + 1) * HEAD_DIM)
                value_part = jnp.dot(
                    grads_turned[lanes, low:high], share, preferred_element_type=f32
                )
                key_part = jnp.dot(
                    queries_turned[lanes, low:high], score_grad, preferred_element_type=f32
                )
                for e in range(s):
                    place = slice((e + 1) * SEG_PAD - SLAB, (e + 1) * SEG_PAD)
                    value_sum[lanes, place] += value_part[:, e * SLAB : (e + 1) * SLAB]
                    key_sum[lanes, place] += key_part[:, e * SLAB : (e + 1) * SLAB]
                place = slice(s * SEG_PAD, s * SEG_PAD + high)
                value_sum[lanes, place] += value_part[:, s * SLAB :]
                key_sum[lanes, place] += key_part[:, s * SLAB :]
            query_grads.append(jnp.where(first_head[low:high], both[0], both[1]))
        query_grad = (jnp.concatenate(query_grads, axis=0) * score_scale).astype(bf16)
        store_segment(dq_ref, starts[s], rows_padded, query_grad)
    key_all = key_sum[...].T.astype(bf16)
    value_all = value_sum[...].T.astype(bf16)
    for s in range(NSEG):
        place = slice(s * SEG_PAD, (s + 1) * SEG_PAD)
        store_segment(dk_ref, starts[s], rows_padded, key_all[place])
        store_segment(dv_ref, starts[s], rows_padded, value_all[place])


def attend_back(qkv, out, grad, share, me, mp_count, rows_padded):
    rows, width = qkv.shape
    pairs = width // 3 // 128
    column = pl.BlockSpec((rows, 128), lambda n, me_ref: (0, n))
    piece = jax.ShapeDtypeStruct((rows, width // 3), bf16)
    return pl.pallas_call(
        functools.partial(attend_back_kernel, mp_count, rows_padded),
        out_shape=(piece, piece, piece),
        grid_spec=pltpu.PrefetchScalarGridSpec(
            num_scalar_prefetch=1,
            grid=(pairs,),
            in_specs=[
                column,
                pl.BlockSpec((rows, 128), lambda n, me_ref: (0, pairs + n)),
                pl.BlockSpec((rows, 128), lambda n, me_ref: (0, 2 * pairs + n)),
                column,
                column,
                pl.BlockSpec((2, rows, KEYS), lambda n, me_ref: (n, 0, 0)),
            ],
            out_specs=(column, column, column),
            scratch_shapes=[pltpu.VMEM((128, rows), f32), pltpu.VMEM((128, rows), f32)],
        ),
        compiler_params=pltpu.CompilerParams(vmem_limit_bytes=48 * 2**20),
        cost_estimate=expected(23.0),
        name="attend_back",
    )(me, qkv, qkv, qkv, out, grad, share)


def item_rows(present, summary, parts, rows, rows_padded):
    kept = present[:, None] * jnp.concatenate([jnp.ones((NSEG, SEG), jnp.int32), summary], axis=1)
    group = parts // NSEG
    kept = jnp.pad(kept.reshape(NSEG, group, rows), ((0, 0), (0, 0), (0, rows_padded - rows)))
    flags = np.zeros((group, rows_padded), np.int32)
    flags[:, :rows] = (np.arange(PERIOD) >= SEG).reshape(group, rows)
    return kept.reshape(NSEG, group * rows_padded), flags.reshape(group * rows_padded)


def score_bias(kept, flags):
    slab = (kept * flags[None, :])[:, SEG_PAD - SLAB :] == 1
    causal = np.tril(np.ones((SEG_PAD, SEG_PAD), bool))
    itself = np.eye(SEG_PAD, dtype=bool)
    planes = []
    for s in range(NSEG):
        own = (kept[s][None, :] == 1) & causal | itself
        pieces = [jnp.broadcast_to(slab[e][None, :], (SEG_PAD, SLAB)) for e in range(s)] + [own]
        seen = jnp.concatenate(pieces, axis=1)
        planes.append(jnp.pad(seen, ((0, 0), (0, KEYS - seen.shape[1]))))
    return jnp.where(jnp.stack(planes), 0.0, -1e30).astype(f32)


def norm_parts(value):
    center = value - jnp.mean(value, axis=-1, keepdims=True)
    spread = jnp.mean(center * center, axis=-1, keepdims=True)
    scale = lax.rsqrt(spread + norm_eps)
    return center * scale, scale


def norm_back(normed, scale, gain, grad):
    inner = grad * gain
    return scale * (
        inner
        - jnp.mean(inner, axis=-1, keepdims=True)
        - normed * jnp.mean(inner * normed, axis=-1, keepdims=True)
    )


def gelu_both(value):
    c = 0.7978845608028654
    square = value * value
    bend = jnp.tanh(c * (value + 0.044715 * value * square))
    half = 0.5 * (1.0 + bend)
    slope = half + 0.5 * value * (1.0 - bend * bend) * c * (1.0 + 3.0 * 0.044715 * square)
    return value * half, slope


def adam_step(master, grad, first, second, average, factor, rate, decay):
    clipped = grad * factor
    first_new = beta_first * first + (1.0 - beta_first) * clipped
    second_new = beta_second * second + (1.0 - beta_second) * clipped * clipped
    first_hat = first_new / (1.0 - beta_first**STEP)
    second_hat = second_new / (1.0 - beta_second**STEP)
    master_new = master - rate * (first_hat / (jnp.sqrt(second_hat) + adam_eps) + decay * master)
    average_new = average_keep * average + (1.0 - average_keep) * master_new
    return (master_new, first_new, second_new, average_new, master_new.astype(bf16))


def per_device(
    tokens,
    cotangent,
    present,
    summary_mask,
    attention_weight,
    attention_first,
    attention_second,
    attention_average,
    hidden_weight,
    hidden_first,
    hidden_second,
    hidden_average,
    norm_params,
    norm_first,
    norm_second,
    norm_average,
    head_bias,
    head_first,
    head_second,
    head_average,
    unit_bias,
    unit_first,
    unit_second,
    unit_average,
):
    outer, inner = seq_grid()
    seqs = outer * inner
    parts = lax.axis_size("mp")
    rows = tokens.shape[0]
    rows_padded = SEG_PAD * NSEG // parts
    head_width = attention_weight.shape[2]
    depth = attention_weight.shape[1]
    me = lax.axis_index("mp")
    me_vector = me.astype(jnp.int32)[None]
    order = feature_order()
    back_order = block_order()
    spots = block_spots()
    codes = row_codes()
    units = hidden_weight.shape[2]
    total_rows = parts * rows_padded

    norm_size, head_size = norm_params.size, head_bias.size
    packed = jnp.concatenate([norm_params.reshape(-1), head_bias.reshape(-1), unit_bias])
    packed_size = packed.size
    packed_width = 4 * head_width
    packed = jnp.pad(packed, (0, 16 * packed_width - packed_size)).reshape(16, packed_width)
    attn_own = jnp.concatenate(
        [jnp.concatenate([attention_weight[n] for n in range(4)], axis=1), packed], axis=0
    ).astype(bf16)
    attn_line = ring_line(attn_own)
    row_pad = ((0, rows_padded - rows), (0, 0))
    tokens_all = gather_chips(jnp.pad(tokens, row_pad))
    attn_rest = [ring_rest(part) for part in attn_line]
    attn_blocks = attn_line + [rest[j] for j in range(inner - 1) for rest in attn_rest]
    cotangent_pieces = gather_chips(after(jnp.pad(cotangent, row_pad), *tokens_all))
    up_line = ring_line(after(hidden_weight[0].astype(bf16), attn_line[-1]))
    down_line = ring_line(after(hidden_weight[1].astype(bf16), up_line[-1]))
    up_first = ring_rest(after(up_line[0], attn_rest[-2][-1]))
    down_first = ring_rest(after(down_line[0], attn_rest[-1][-1]))
    up_rest = ring_rest(jnp.concatenate(after(up_line[1:], up_first[-1]), axis=0))
    down_rest = ring_rest(
        jnp.concatenate(after(down_line[1:], down_first[-1], up_rest[-1]), axis=0)
    )
    up_blocks = up_line + [part for pair in zip(up_first, up_rest) for part in pair]
    down_blocks = down_line + [part for pair in zip(down_first, down_rest) for part in pair]

    vectors = jnp.concatenate([block[depth : depth + 1] for block in attn_blocks], axis=0)
    vectors = vectors[:, :packed_size].astype(f32)
    norm_vals = vectors[:, :norm_size].reshape(seqs, 6, depth).transpose(1, 0, 2).reshape(6, D)
    vectors = jnp.take(vectors[:, norm_size:], back_order, axis=0)
    head_vals = vectors[:, :head_size].reshape(seqs, 2, head_width // seqs)
    head_vals = head_vals.transpose(1, 0, 2).reshape(2, head_width)
    unit_vals = vectors[:, head_size:].reshape(-1)

    kept, flags = item_rows(present[0], summary_mask[0], parts, rows, rows_padded)
    bias = score_bias(kept, flags)
    kept_parts = kept.reshape(parts, rows_padded).astype(f32)
    kept_all = jnp.take(kept_parts, jnp.stack([me ^ code for code in codes]), axis=0).reshape(-1, 1)
    kept_own = kept_all[:rows_padded]

    first_all, inputs_own = arrange(
        tokens_all,
        [norm_vals[0:1], norm_vals[1:2]],
        [resident((1, D))] * 2,
        True,
        2,
        "first_norm",
    )
    qkv_bias = jnp.concatenate([head_vals[0], jnp.zeros_like(head_vals[0]), head_vals[1]])
    qkv_scale = np.concatenate(
        [np.full(head_width, score_scale, np.float32), np.ones(2 * head_width, np.float32)]
    )
    qkv = tall_dot(
        [first_all],
        attn_blocks,
        0,
        3 * head_width,
        project_epilogue,
        [qkv_bias[None], qkv_scale[None]],
        [(total_rows, bf16)],
        "project",
    )[0]
    context, share = attend(qkv, bias, me_vector, parts, rows_padded)
    join_parts = wide_dot(context, attn_blocks, 3 * head_width, D, 4, "join")
    attended = scatter_chips(*join_parts) + norm_vals[4]
    feed_grad, cotangent_own = arrange(
        cotangent_pieces,
        [kept_all],
        [pl.BlockSpec((rows_padded, 1), lambda n: (n, 0))],
        False,
        3,
        "feed_grad",
    )
    inputs = inputs_own.astype(f32)
    middle = inputs + kept_own * attended

    normed_two, scale_two = norm_parts(middle)
    second_own = (normed_two * norm_vals[2] + norm_vals[3]).astype(bf16)
    second_all = gather_chips(second_own)
    activated, slope, second_others = tall_dot(
        second_all,
        up_blocks,
        0,
        units,
        up_epilogue,
        [unit_vals[None]],
        [(total_rows, bf16), (total_rows, bf16)],
        "up",
        5,
    )
    second_all = second_all + [second_others]

    out_grad = cotangent_own.astype(f32)
    down_bias_grad = jnp.sum(kept_own * out_grad, axis=0)

    down_pairs = [([feed_grad], activated)]
    down_far = far_grads(down_pairs, spots, depth, "down_grad")
    down_received = inner_sum([far and far[0] for far in down_far])
    pre_grad, unit_grad = tall_dot(
        [feed_grad],
        down_blocks,
        0,
        units,
        slope_epilogue,
        [slope],
        [(total_rows, bf16), (8, f32)],
        "down_back",
    )
    unit_grad = unit_grad[0]
    second_parts = wide_dot(pre_grad, up_blocks, 0, D, 6, "up_back")
    up_pairs = [(second_all, pre_grad)]
    up_far = far_grads(up_pairs, spots, depth, "up_grad")
    up_received = inner_sum(
        [far and after(far[0], down_received) for far in up_far]
    )
    second_grad = scatter_chips(*second_parts)
    gain_two_grad = jnp.sum(second_grad * normed_two, axis=0)
    shift_two_grad = jnp.sum(second_grad, axis=0)
    middle_grad = out_grad + norm_back(normed_two, scale_two, norm_vals[2], second_grad)

    attn_grad = kept_own * middle_grad
    out_bias_grad = jnp.sum(attn_grad, axis=0)
    attn_rows = gather_chips(attn_grad.astype(bf16))
    context_grad, attn_others = tall_dot(
        attn_rows,
        attn_blocks,
        3 * head_width,
        head_width,
        plain_epilogue,
        [],
        [(total_rows, bf16)],
        "join_back",
        7,
    )
    attn_rows = attn_rows + [attn_others]
    down_grad = line_scatter(down_pairs, down_received, spots, depth, "down_grad")
    feed_parts = wide_dot(after(activated, second_grad), down_blocks, 0, D, 8, "down")
    feed_out = scatter_chips(*after(feed_parts, *attn_rows)) + norm_vals[5]
    block_output = from_blocks(middle + kept_own * feed_out, order, rows)
    query_grad, key_grad, value_grad = attend_back(
        qkv, context, context_grad, share, me_vector, parts, rows_padded
    )
    qkv_grad = jnp.concatenate([query_grad, key_grad, value_grad], axis=1)
    head_grad = jnp.stack(
        [jnp.sum(query_grad, axis=0, dtype=f32), jnp.sum(value_grad, axis=0, dtype=f32)]
    )
    attn_pairs = [([first_all], qkv_grad), (attn_rows, context)]
    attn_far = far_grads(attn_pairs, spots, depth, "attn_grad", split=True)
    attn_received = [None] * outer
    last = up_received
    for i in reversed(range(outer)):
        last = attn_received[i] = inner_sum([far and after(far[i], last) for far in attn_far])
    up_grad = line_scatter(up_pairs, up_received, spots, depth, "up_grad")
    near = turned_dot(attn_pairs, 0, spots, depth, "attn_grad_near")[0]
    attn_shard = ring_scatter(
        [near[i * depth : (i + 1) * depth] for i in range(outer)], attn_received
    )
    first_grad = scatter_chips(*wide_dot(qkv_grad, attn_blocks, 0, D, 9, "project_back"))
    normed_one, scale_one = norm_parts(inputs)
    gain_one_grad = jnp.sum(first_grad * normed_one, axis=0)
    shift_one_grad = jnp.sum(first_grad, axis=0)
    input_grad = from_blocks(
        middle_grad + norm_back(normed_one, scale_one, norm_vals[0], first_grad), order, rows
    )

    vector_grad = jnp.stack(
        [
            gain_one_grad,
            shift_one_grad,
            gain_two_grad,
            shift_two_grad,
            out_bias_grad,
            down_bias_grad,
        ]
    )
    vector_grad = jnp.take(
        vector_grad.reshape(6, seqs, depth).transpose(1, 0, 2).reshape(seqs, -1), back_order, axis=0
    )
    norm_room = -(-norm_size // 1024) * 1024
    room = norm_room + -(-(packed_size - norm_size) // 1024) * 1024
    vectors = jnp.concatenate(
        [
            vector_grad,
            jnp.zeros((seqs, norm_room - norm_size), f32),
            head_grad.reshape(2, seqs, -1).transpose(1, 0, 2).reshape(seqs, -1),
            unit_grad.reshape(seqs, -1),
            jnp.zeros((seqs, room - norm_room - packed_size + norm_size), f32),
        ],
        axis=1,
    )
    vectors = reduce_vector(vectors.reshape(seqs, room // 128, 128), norm_room // 128)
    vectors = vectors.reshape(-1)
    norm_shard = vectors[:norm_size].reshape(norm_params.shape)
    head_shard = vectors[norm_room : norm_room + head_size].reshape(head_bias.shape)
    unit_shard = vectors[norm_room + head_size : norm_room + packed_size - norm_size]

    attn_shard = jnp.stack(
        [attn_shard[:, n * head_width : (n + 1) * head_width] for n in range(4)]
    )
    hidden_shard = jnp.stack([up_grad, down_grad]).astype(f32)
    leader = (me == 0).astype(f32)
    local_squares = (
        jnp.sum(attn_shard * attn_shard)
        + jnp.sum(hidden_shard * hidden_shard)
        + jnp.sum(head_shard * head_shard)
        + jnp.sum(unit_shard * unit_shard)
        + leader * jnp.sum(norm_shard * norm_shard)
    )
    grad_norm = jnp.sqrt(reduce_scalar(jnp.full((8, 128), local_squares))[0, 0])
    factor = jnp.minimum(1.0, clip_limit / (grad_norm + 1e-06))
    hidden_rate = jnp.array([D ** (-0.5), FF ** (-0.5)], f32)[:, None, None]
    attention_out = adam_step(
        attention_weight,
        attn_shard,
        attention_first,
        attention_second,
        attention_average,
        factor,
        D ** (-0.5),
        weight_decay,
    )
    hidden_out = adam_step(
        hidden_weight,
        hidden_shard,
        hidden_first,
        hidden_second,
        hidden_average,
        factor,
        hidden_rate,
        weight_decay,
    )
    norm_out = adam_step(
        norm_params, norm_shard, norm_first, norm_second, norm_average, factor, vector_rate, 0.0
    )
    head_out = adam_step(
        head_bias, head_shard, head_first, head_second, head_average, factor, vector_rate, 0.0
    )
    unit_out = adam_step(
        unit_bias, unit_shard, unit_first, unit_second, unit_average, factor, vector_rate, 0.0
    )
    return (
        block_output,
        input_grad,
        grad_norm,
        *attention_out,
        *hidden_out,
        *norm_out,
        *head_out,
        *unit_out,
    )


def solution(mesh):
    token_spec = P(("seq", "mp"), None)
    weight_spec = P(None, "seq", "mp")
    norm_spec = P(None, "seq")
    head_spec = P(None, ("mp", "seq"))
    unit_spec = P(("mp", "seq"))
    return jax.shard_map(
        per_device,
        mesh=mesh,
        in_specs=(
            token_spec,
            token_spec,
            P("seq", None),
            P("seq", None, None),
            *([weight_spec] * 8),
            *([norm_spec] * 4),
            *([head_spec] * 4),
            *([unit_spec] * 4),
        ),
        out_specs=(
            token_spec,
            token_spec,
            P(),
            *([weight_spec] * 10),
            *([norm_spec] * 5),
            *([head_spec] * 5),
            *([unit_spec] * 5),
        ),
        check_vma=False,
    )
```

```python
import functools

import jax
import jax.numpy as jnp
import numpy as np
from jax import lax
from jax.experimental import pallas as pl
from jax.experimental.pallas import tpu as pltpu
from jax.sharding import PartitionSpec as P

D = 2048
HEAD_DIM = 64
FF = 8192
SUMM = 50
NSEG = 4
SEG = 256
STEP = 10
PERIOD = SEG + SUMM
SEG_PAD = 320
SLAB = 64
KEYS = SLAB * (NSEG - 1) + SEG_PAD

norm_eps = 1e-05
beta_first = 0.9
beta_second = 0.95
adam_eps = 1e-08
clip_limit = 1.0
weight_decay = 0.1
average_keep = 0.6
vector_rate = 0.4
score_scale = HEAD_DIM ** (-0.5)
query_blocks = ((0, 128), (128, 256), (256, SEG_PAD))

RATE = 0.59e9

f32 = jnp.float32
bf16 = jnp.bfloat16


def seq_grid():
    count = lax.axis_size("seq")
    inner = count // 4
    return count // inner, inner


def shift_outer(value, step):
    outer, inner = seq_grid()
    pairs = [
        (a * inner + b, ((a + step) % outer) * inner + b) for a in range(outer) for b in range(inner)
    ]
    return lax.ppermute(value, "seq", pairs)


def shift_inner(value, step):
    outer, inner = seq_grid()
    pairs = [
        (a * inner + b, a * inner + (b + step) % inner) for a in range(outer) for b in range(inner)
    ]
    return lax.ppermute(value, "seq", pairs)


def swap(value, bits):
    return lax.ppermute(value, "mp", [(m, m ^ bits) for m in range(lax.axis_size("mp"))])


def block_order():
    outer, inner = seq_grid()
    me = lax.axis_index("seq")
    mine_a, mine_b = me // inner, me % inner
    return jnp.stack(
        [
            ((mine_b - b + inner) % inner) * outer + (mine_a - a + outer) % outer
            for a in range(outer)
            for b in range(inner)
        ]
    ).astype(jnp.int32)


def feature_order():
    outer, inner = seq_grid()
    me = lax.axis_index("seq")
    mine_a, mine_b = me // inner, me % inner
    return jnp.stack(
        [
            ((mine_a - i + outer) % outer) * inner + (mine_b - j + inner) % inner
            for j in range(inner)
            for i in range(outer)
        ]
    ).astype(jnp.int32)


def after(value, *others):
    return lax.optimization_barrier((value, *others))[0] if others else value


def row_codes():
    count = lax.axis_size("mp")
    return [high * 2 + low for low in range(2) for high in range(count // 2)]


def ring_rest(part):
    rest = []
    for _ in range(seq_grid()[1] - 1):
        part = shift_inner(part, 1)
        rest.append(part)
    return rest


def ring_scatter(near, received, held=(), sums=()):
    sums = list(sums)
    depth = received[0].shape[0]
    for n in range(len(sums), len(received)):
        i = len(received) - 1 - n
        total = near[i * depth : (i + 1) * depth].astype(f32) + received[i].astype(f32)
        if sums:
            last = after(sums[-1], *held[n - 1 : n])
            total = total + shift_outer(last, -1).astype(f32)
        sums.append(total.astype(bf16) if i else total)
    return sums


def greet(peers):
    barrier = pltpu.get_barrier_semaphore()
    for peer in peers:
        pl.semaphore_signal(barrier, inc=1, device_id=peer, device_id_type=pl.DeviceIdType.MESH)
    pl.semaphore_wait(barrier, len(peers))


def others(axis, count):
    me = lax.axis_index(axis)
    return [lax.rem(me + step, count) for step in range(1, count)]


def exchange(axis, count, pieces, slots, send_sems, recv_sems):
    copies = []
    for step, peer in enumerate(others(axis, count)):
        copy = pltpu.make_async_remote_copy(
            src_ref=pieces(peer),
            dst_ref=slots.at[step],
            send_sem=send_sems.at[step],
            recv_sem=recv_sems.at[step],
            device_id={axis: peer},
            device_id_type=pl.DeviceIdType.MESH,
        )
        copy.start()
        copies.append(copy)
    return copies


def in_order(axis, count, mine, slots):
    me = lax.axis_index(axis)
    total = jnp.zeros_like(mine)
    for place in range(count):
        step = lax.rem(me + 2 * count - place - 1, count)
        other = slots[jnp.minimum(step, count - 2)]
        total = total + jnp.where(place == me, mine, other)
    return total


def square_tile(value):
    return jnp.sum((value * value).reshape(-1, 8, 128), axis=0)


def reduce_kernel(seqs, parts, shared, *refs):
    vector_ref, square_ref, out_ref, total_ref = refs[:4]
    first, norms, tiles, last = refs[4:8]
    sems = refs[8:]
    greet(
        [{"seq": peer} for peer in others("seq", seqs)]
        + [{"mp": peer} for peer in others("mp", parts)]
    )
    copies = exchange("seq", seqs, lambda peer: vector_ref.at[peer], first, sems[0], sems[1])
    value = vector_ref[lax.axis_index("seq")]
    for step, copy in enumerate(copies):
        copy.wait()
        value = value + first[step]
    out_ref[...] = value
    total_ref[...] = square_ref[...] + square_tile(value[shared:])
    copies = exchange("mp", parts, lambda peer: out_ref.at[:shared], norms, sems[2], sems[3])
    copies += exchange("mp", parts, lambda peer: total_ref, tiles, sems[4], sems[5])
    for copy in copies:
        copy.wait()
    norm = in_order("mp", parts, value[:shared], norms)
    tile = in_order("mp", parts, total_ref[...], tiles) + square_tile(norm)
    out_ref[:shared] = norm
    total_ref[...] = tile
    copies = exchange("seq", seqs, lambda peer: total_ref, last, sems[6], sems[7])
    for copy in copies:
        copy.wait()
    total_ref[...] = in_order("seq", seqs, tile, last)


def reduce_all(vectors, squares, shared):
    seqs, parts = lax.axis_size("seq"), lax.axis_size("mp")
    vmem = pl.BlockSpec(memory_space=pltpu.VMEM)
    block = vectors.shape[1:]
    counts = [seqs, seqs, parts, parts, parts, parts, seqs, seqs]
    return pl.pallas_call(
        functools.partial(reduce_kernel, seqs, parts, shared),
        out_shape=[
            jax.ShapeDtypeStruct(block, f32),
            jax.ShapeDtypeStruct((8, 128), f32),
        ],
        in_specs=[vmem, vmem],
        out_specs=[vmem, vmem],
        scratch_shapes=[
            pltpu.VMEM((seqs - 1, *block), f32),
            pltpu.VMEM((parts - 1, shared, 128), f32),
            pltpu.VMEM((parts - 1, 8, 128), f32),
            pltpu.VMEM((seqs - 1, 8, 128), f32),
        ]
        + [pltpu.SemaphoreType.DMA((count - 1,)) for count in counts],
        compiler_params=pltpu.CompilerParams(
            vmem_limit_bytes=4 * 2**20, collective_id=0, has_side_effects=True
        ),
        cost_estimate=expected(12.0),
        name="reduce_all",
    )(vectors, squares)


def gather_chips(own):
    high = [own]
    for bit in range(1, lax.axis_size("mp").bit_length() - 1):
        high = high + [swap(part, 1 << bit) for part in high]
    return high


def scatter_chips(first, second):
    count = lax.axis_size("mp") // 2
    rows = 2 * first.shape[0] // count
    total = first[:rows]
    for n in range(1, count):
        at = n * rows
        if at < first.shape[0]:
            part = first[at : at + rows].astype(bf16)
        else:
            part = second[at - first.shape[0] : at - first.shape[0] + rows]
        total = total + swap(part, n * 2).astype(f32)
    return total


def other_core():
    me = lax.axis_index("mp")
    return {"mp": me + 1 - 2 * lax.rem(me, 2)}


def core_copy(src, dst, send_sem, recv_sem):
    return pltpu.make_async_remote_copy(
        src_ref=src,
        dst_ref=dst,
        send_sem=send_sem,
        recv_sem=recv_sem,
        device_id=other_core(),
        device_id_type=pl.DeviceIdType.MESH,
    )


def kernel_params(number):
    return pltpu.CompilerParams(
        vmem_limit_bytes=56 * 2**20, collective_id=number, has_side_effects=True
    )


def expected(microseconds):
    return pl.CostEstimate(
        flops=int(microseconds * RATE), bytes_accessed=0, transcendentals=0
    )


def estimate(rows, depth, columns):
    return expected(1.5 + rows * depth * columns * 2 / 7.2e8)


def resident(shape):
    return pl.BlockSpec(shape, lambda *place: (0,) * len(shape))


def arrange_kernel(lefts, blocks, grid, normed, *refs):
    pieces, rest = refs[:lefts], refs[lefts:-3]
    got, send_sem, recv_sem = refs[-3:]
    out_ref, own_ref = rest[-2:]
    step = pl.program_id(0)
    rows, width = pieces[0].shape
    wide = width // blocks
    outer, inner = grid
    me = lax.axis_index("seq")
    mine_a, mine_b = me // inner, lax.rem(me, inner)

    def copy(n):
        return core_copy(pieces[n], got.at[n], send_sem.at[n], recv_sem.at[n])

    @pl.when(step == 0)
    def _():
        greet([other_core()])
        for n in range(lefts):
            copy(n).start()

    def fill(p, load):
        if normed:
            value = load(slice(None)).astype(f32)
            mean = jnp.mean(value, axis=-1, keepdims=True)
            center = value - mean
            scale = lax.rsqrt(jnp.mean(center * center, axis=-1, keepdims=True) + norm_eps)
        for b in range(blocks):
            place = lax.rem(mine_a - b % outer + outer, outer) * inner
            place = place + lax.rem(mine_b - b // outer + inner, inner)
            here = slice(b * wide, (b + 1) * wide)
            part = load(pl.ds(pl.multiple_of(place * wide, wide), wide))
            if p == 0:
                own_ref[:, here] = part
            part = part.astype(f32)
            if normed:
                part = (part - mean) * scale * rest[0][:, here] + rest[1][:, here]
            else:
                part = part * rest[0][...]
            out_ref[:, here] = part.astype(bf16)

    for n in range(lefts):

        @pl.when(step == n)
        def _(n=n):
            fill(n, lambda columns: pieces[n][:, columns])

        @pl.when(step == lefts + n)
        def _(n=n):
            copy(n).wait()
            fill(lefts + n, lambda columns: got[n, :, columns])


def arrange(pieces, extras, extra_specs, normed, number, name):
    rows, width = pieces[0].shape
    lefts = len(pieces)
    return pl.pallas_call(
        functools.partial(arrange_kernel, lefts, lax.axis_size("seq"), seq_grid(), normed),
        out_shape=[
            jax.ShapeDtypeStruct((2 * lefts * rows, width), bf16),
            jax.ShapeDtypeStruct((rows, width), bf16),
        ],
        grid=(2 * lefts,),
        in_specs=[resident((rows, width))] * lefts + extra_specs,
        out_specs=[pl.BlockSpec((rows, width), lambda n: (n, 0)), resident((rows, width))],
        scratch_shapes=[
            pltpu.VMEM((lefts, rows, width), bf16),
            pltpu.SemaphoreType.DMA((lefts,)),
            pltpu.SemaphoreType.DMA((lefts,)),
        ],
        compiler_params=kernel_params(number),
        cost_estimate=expected(9.0),
        name=name,
    )(*pieces, *extras)


def tall_kernel(epilogue, exchanged, lefts, blocks, extras, *refs):
    weight = jnp.concatenate([ref[...] for ref in refs[lefts : lefts + blocks]], axis=0)
    rest = refs[lefts + blocks :]
    step = pl.program_id(0)
    rows = refs[0].shape[0]
    if exchanged:
        others_ref, got, send_sem, recv_sem = rest[-4:]
        rest = rest[:-4]

        def copy(n):
            return core_copy(refs[n], got.at[n], send_sem.at[n], recv_sem.at[n])

        @pl.when(step == 0)
        def _():
            greet([other_core()])
            for n in range(lefts):
                copy(n).start()

    def fill(left, at):
        result = jnp.dot(left, weight, preferred_element_type=f32)
        epilogue(result, slice(at, at + rows), rest[:extras], rest[extras:])

    for n in range(lefts):
        fill(refs[n][...], n * rows)
    if exchanged:

        @pl.when(step == 0)
        def _():
            for n in range(lefts):
                copy(n).wait()

        for n in range(lefts):
            fill(got[n], (lefts + n) * rows)

        @pl.when(step == pl.num_programs(0) - 1)
        def _():
            for n in range(lefts):
                others_ref[n * rows : (n + 1) * rows, :] = got[n]


def tall_dot(lefts, blocks, start, width, epilogue, extras, outs, name, number=None):
    rows, depth = lefts[0].shape
    exchanged = number is not None
    count = len(lefts) * (2 if exchanged else 1)
    tile = max(size for size in (128, 256, 512) if width % size == 0 and start % size == 0)
    first = start // tile
    block_depth = depth // lax.axis_size("seq")
    specs = []
    for block in blocks:
        high = block_depth if block.shape[0] // block_depth < 2 else block.shape[0]
        specs.append(pl.BlockSpec((high, tile), lambda n: (0, first + n)))
    out_shape = [jax.ShapeDtypeStruct((height, width), dtype) for height, dtype in outs]
    out_specs = [pl.BlockSpec((height, tile), lambda n: (0, n)) for height, _ in outs]
    scratch = []
    params = pltpu.CompilerParams(vmem_limit_bytes=56 * 2**20)
    if exchanged:
        out_shape.append(jax.ShapeDtypeStruct((len(lefts) * rows, depth), bf16))
        out_specs.append(resident((len(lefts) * rows, depth)))
        scratch = [
            pltpu.VMEM((len(lefts), rows, depth), bf16),
            pltpu.SemaphoreType.DMA((len(lefts),)),
            pltpu.SemaphoreType.DMA((len(lefts),)),
        ]
        params = kernel_params(number)
    return pl.pallas_call(
        functools.partial(
            tall_kernel, epilogue, exchanged, len(lefts), len(blocks), len(extras)
        ),
        out_shape=out_shape,
        grid=(width // tile,),
        in_specs=[resident(left.shape) for left in lefts]
        + specs
        + [pl.BlockSpec((extra.shape[0], tile), lambda n: (0, n)) for extra in extras],
        out_specs=out_specs,
        scratch_shapes=scratch,
        compiler_params=params,
        cost_estimate=estimate(rows * count, depth, width),
        name=name,
    )(*lefts, *blocks, *extras)


def plain_epilogue(result, here, extras, outs):
    outs[0][here, :] = result.astype(bf16)


def project_epilogue(result, here, extras, outs):
    bias, scale = extras
    outs[0][here, :] = ((result + bias[...]).astype(bf16).astype(f32) * scale[...]).astype(bf16)


def up_epilogue(result, here, extras, outs):
    value, slope = gelu_both(result + extras[0][...])
    outs[0][here, :] = value.astype(bf16)
    outs[1][here, :] = slope.astype(bf16)


def slope_epilogue(result, here, extras, outs):
    grad = (result * extras[0][here, :].astype(f32)).astype(bf16)
    outs[0][here, :] = grad
    sums = jnp.sum(grad.astype(f32), axis=0, keepdims=True)
    outs[1][...] = jnp.broadcast_to(sums, outs[1].shape)


def wide_kernel(blocks, start, left_ref, *refs):
    first_ref, second_ref, sent, got, send_sem, recv_sem = refs[blocks:]
    step = pl.program_id(0)
    columns = slice(start, start + left_ref.shape[1])

    def copy(n):
        return core_copy(sent.at[n], got.at[n], send_sem.at[n], recv_sem.at[n])

    @pl.when(step == 0)
    def _():
        greet([other_core()])

    result = lax.dot_general(
        left_ref[...],
        jnp.concatenate([ref[:, columns] for ref in refs[:blocks]], axis=0),
        (((1,), (1,)), ((), ())),
        preferred_element_type=f32,
    )
    for n in range(2):

        @pl.when(step == n)
        def _(n=n):
            sent[n] = result.astype(bf16)
            copy(n).start()

    @pl.when(step == 2)
    def _():
        copy(0).wait()
        second_ref[...] = (result + got[0].astype(f32)).astype(bf16)

    @pl.when(step == 3)
    def _():
        copy(1).wait()
        first_ref[...] = result + got[1].astype(f32)


def wide_dot(left, blocks, start, features, number, name):
    rows, width = left.shape
    tile = rows // 4
    block_depth = features // lax.axis_size("seq")
    specs = []
    for block in blocks:
        high = block_depth if block.shape[0] // block_depth < 2 else block.shape[0]
        specs.append(resident((high, block.shape[1])))
    return pl.pallas_call(
        functools.partial(wide_kernel, len(blocks), start),
        out_shape=[
            jax.ShapeDtypeStruct((tile, features), f32),
            jax.ShapeDtypeStruct((tile, features), bf16),
        ],
        grid=(4,),
        in_specs=[pl.BlockSpec((tile, width), lambda n: (3 - n, 0))] + specs,
        out_specs=[resident((tile, features)), resident((tile, features))],
        scratch_shapes=[
            pltpu.VMEM((2, tile, features), bf16),
            pltpu.VMEM((2, tile, features), bf16),
            pltpu.SemaphoreType.DMA((2,)),
            pltpu.SemaphoreType.DMA((2,)),
        ],
        compiler_params=kernel_params(number),
        cost_estimate=estimate(rows, width, features),
        name=name,
    )(left, *blocks)


def turned_kernel(shapes, sizes, *refs):
    refs = list(refs)
    groups = [[refs.pop(0) for _ in range(count)] for count in shapes]
    rights = [refs.pop(0) for _ in shapes]

    def fill(out_ref, here):
        at = 0
        for lefts, right_ref in zip(groups, rights):
            width = right_ref.shape[1]
            left = jnp.concatenate([ref[...] for ref in lefts], axis=0)
            out_ref[here, at : at + width] = lax.dot_general(
                left, right_ref[...], (((0,), (0,)), ((), ())), preferred_element_type=f32
            ).astype(bf16)
            at += width

    if sizes is None:
        fill(refs[0], slice(None))
    else:
        step = 0
        for size, out_ref in zip(sizes, refs):
            depth = out_ref.shape[0] // size
            for n in range(size):
                here = slice(n * depth, (n + 1) * depth)
                pl.when(pl.program_id(0) == step)(functools.partial(fill, out_ref, here))
                step += 1


def turned_dot(pairs, first, count, depth, name, sizes=None):
    width = sum(right.shape[1] for _, right in pairs)
    rows = pairs[0][1].shape[0]
    if sizes is None:
        out_shape = [jax.ShapeDtypeStruct((count * depth, width), bf16)]
        out_specs = [pl.BlockSpec((depth, width), lambda n: (n, 0))]
    else:
        out_shape = [jax.ShapeDtypeStruct((size * depth, width), bf16) for size in sizes]
        out_specs = [resident((size * depth, width)) for size in sizes]
    return pl.pallas_call(
        functools.partial(turned_kernel, [len(lefts) for lefts, _ in pairs], sizes),
        out_shape=out_shape,
        grid=(count,),
        in_specs=[
            pl.BlockSpec((left.shape[0], depth), lambda n: (0, first + n))
            for lefts, _ in pairs
            for left in lefts
        ]
        + [resident(right.shape) for _, right in pairs],
        out_specs=out_specs,
        compiler_params=pltpu.CompilerParams(vmem_limit_bytes=56 * 2**20),
        cost_estimate=estimate(rows, count * depth, width),
        name=name,
    )(*[left for lefts, _ in pairs for left in lefts], *[right for _, right in pairs])


def far_grads(pairs, depth, name, sizes):
    outer, inner = seq_grid()
    return [
        turned_dot(pairs, j * outer, outer, depth, name + "_far", sizes) for j in range(1, inner)
    ]


def near_grads(pairs, depth, name):
    return turned_dot(pairs, 0, seq_grid()[0], depth, name + "_near")[0]


def inner_sum(far, n, *ready):
    part = shift_inner(after(far[-1][n], *ready), -1)
    for parts in reversed(far[:-1]):
        part = shift_inner((parts[n].astype(f32) + part.astype(f32)).astype(bf16), -1)
    return part


def single_blocks(groups, depth):
    return [
        group[n * depth : (n + 1) * depth]
        for group in groups
        for n in range(group.shape[0] // depth)
    ]


def from_blocks_kernel(blocks, order_ref, in_ref, out_ref):
    rows, width = out_ref.shape
    wide = width // blocks
    for b in range(blocks):
        there = pl.ds(pl.multiple_of(order_ref[b] * wide, wide), wide)
        out_ref[:, there] = in_ref[:rows, b * wide : (b + 1) * wide].astype(out_ref.dtype)


def from_blocks(value, order, rows):
    rows_padded, width = value.shape
    return pl.pallas_call(
        functools.partial(from_blocks_kernel, order.shape[0]),
        out_shape=jax.ShapeDtypeStruct((rows, width), bf16),
        in_specs=[
            pl.BlockSpec(memory_space=pltpu.SMEM),
            pl.BlockSpec(memory_space=pltpu.VMEM),
        ],
        out_specs=pl.BlockSpec(memory_space=pltpu.VMEM),
        compiler_params=pltpu.CompilerParams(vmem_limit_bytes=12 * 2**20),
        cost_estimate=expected(3.0),
        name="from_blocks",
    )(order, value)


def segment_starts(me, mp_count, rows_padded):
    group = mp_count // NSEG
    starts = []
    for s in range(NSEG):
        pieces = []
        for r in range(group):
            code = jnp.bitwise_xor(me, s * group + r)
            place = jnp.bitwise_and(code, 1) * (mp_count // 2) + lax.shift_right_logical(code, 1)
            pieces.append(pl.multiple_of(place * rows_padded, rows_padded))
        starts.append(pieces)
    return starts


def load_segment(ref, pieces, rows_padded):
    parts = [ref[pl.ds(start, rows_padded), :] for start in pieces]
    return parts[0] if len(parts) == 1 else jnp.concatenate(parts, axis=0)


def load_slab(ref, pieces, rows_padded):
    return ref[pl.ds(pl.multiple_of(pieces[-1] + (rows_padded - SLAB), 16), SLAB), :]


def store_segment(ref, pieces, rows_padded, value):
    for r, start in enumerate(pieces):
        ref[pl.ds(start, rows_padded), :] = value[r * rows_padded : (r + 1) * rows_padded]


def lane_halves(shape):
    lane = lax.broadcasted_iota(jnp.int32, shape, 1)
    return lane < HEAD_DIM


def attend_kernel(mp_count, rows_padded, me_ref, q_ref, k_ref, v_ref, bias_ref, o_ref, p_ref):
    starts = segment_starts(me_ref[0], mp_count, rows_padded)
    for s in range(NSEG):
        keys = jnp.concatenate(
            [load_slab(k_ref, starts[e], rows_padded) for e in range(s)]
            + [load_segment(k_ref, starts[s], rows_padded)],
            axis=0,
        )
        values = jnp.concatenate(
            [load_slab(v_ref, starts[e], rows_padded) for e in range(s)]
            + [load_segment(v_ref, starts[s], rows_padded)],
            axis=0,
        )
        queries = load_segment(q_ref, starts[s], rows_padded)
        first_head = lane_halves(queries.shape)
        zero = jnp.zeros_like(queries)
        head_queries = (jnp.where(first_head, queries, zero), jnp.where(first_head, zero, queries))
        outs = []
        for low, high in query_blocks:
            count = SLAB * s + high
            bias = bias_ref[s, low:high, :count]
            both = []
            for h in range(2):
                scores = (
                    lax.dot_general(
                        head_queries[h][low:high],
                        keys[:count],
                        (((1,), (1,)), ((), ())),
                        preferred_element_type=f32,
                    )
                    + bias
                )
                peak = jnp.max(scores, axis=-1, keepdims=True)
                raised = jnp.exp(scores - peak)
                share = raised * (1.0 / jnp.sum(raised, axis=-1, keepdims=True))
                share = share.astype(bf16)
                p_ref[h, s * SEG_PAD + low : s * SEG_PAD + high, :count] = share
                both.append(jnp.dot(share, values[:count], preferred_element_type=f32))
            outs.append(jnp.where(first_head[low:high], both[0], both[1]))
        out = jnp.concatenate(outs, axis=0).astype(bf16)
        store_segment(o_ref, starts[s], rows_padded, out)


def attend(qkv, bias, me, mp_count, rows_padded):
    rows, width = qkv.shape
    pairs = width // 3 // 128
    return pl.pallas_call(
        functools.partial(attend_kernel, mp_count, rows_padded),
        out_shape=(
            jax.ShapeDtypeStruct((rows, width // 3), bf16),
            jax.ShapeDtypeStruct((pairs * 2, rows, KEYS), bf16),
        ),
        grid_spec=pltpu.PrefetchScalarGridSpec(
            num_scalar_prefetch=1,
            grid=(pairs,),
            in_specs=[
                pl.BlockSpec((rows, 128), lambda n, me_ref: (0, n)),
                pl.BlockSpec((rows, 128), lambda n, me_ref: (0, pairs + n)),
                pl.BlockSpec((rows, 128), lambda n, me_ref: (0, 2 * pairs + n)),
                pl.BlockSpec(bias.shape, lambda n, me_ref: (0, 0, 0)),
            ],
            out_specs=(
                pl.BlockSpec((rows, 128), lambda n, me_ref: (0, n)),
                pl.BlockSpec((2, rows, KEYS), lambda n, me_ref: (n, 0, 0)),
            ),
        ),
        compiler_params=pltpu.CompilerParams(vmem_limit_bytes=48 * 2**20),
        cost_estimate=expected(36.0),
        name="attend",
    )(me, qkv, qkv, qkv, bias)


def attend_back_kernel(
    mp_count,
    rows_padded,
    me_ref,
    q_ref,
    k_ref,
    v_ref,
    o_ref,
    g_ref,
    p_ref,
    dq_ref,
    dk_ref,
    dv_ref,
    key_sum,
    value_sum,
):
    starts = segment_starts(me_ref[0], mp_count, rows_padded)
    key_sum[...] = jnp.zeros_like(key_sum)
    value_sum[...] = jnp.zeros_like(value_sum)
    for s in range(NSEG):
        keys = jnp.concatenate(
            [load_slab(k_ref, starts[e], rows_padded) for e in range(s)]
            + [load_segment(k_ref, starts[s], rows_padded)],
            axis=0,
        )
        values = jnp.concatenate(
            [load_slab(v_ref, starts[e], rows_padded) for e in range(s)]
            + [load_segment(v_ref, starts[s], rows_padded)],
            axis=0,
        )
        queries = load_segment(q_ref, starts[s], rows_padded)
        grads = load_segment(g_ref, starts[s], rows_padded)
        outs = load_segment(o_ref, starts[s], rows_padded)
        queries_turned = queries.astype(f32).T.astype(bf16)
        grads_turned = grads.astype(f32).T.astype(bf16)
        first_head = lane_halves(queries.shape)
        zero = jnp.zeros_like(queries)
        head_grads = (jnp.where(first_head, grads, zero), jnp.where(first_head, zero, grads))
        product = grads.astype(f32) * outs.astype(f32)
        head_deltas = (
            jnp.sum(jnp.where(first_head, product, 0.0), axis=-1, keepdims=True),
            jnp.sum(jnp.where(first_head, 0.0, product), axis=-1, keepdims=True),
        )
        query_grads = []
        for low, high in query_blocks:
            count = SLAB * s + high
            both = []
            for h in range(2):
                share = p_ref[h, s * SEG_PAD + low : s * SEG_PAD + high, :count]
                share_grad = lax.dot_general(
                    head_grads[h][low:high],
                    values[:count],
                    (((1,), (1,)), ((), ())),
                    preferred_element_type=f32,
                )
                score_grad = (
                    share.astype(f32) * (share_grad - head_deltas[h][low:high])
                ).astype(bf16)
                both.append(jnp.dot(score_grad, keys[:count], preferred_element_type=f32))
                lanes = slice(h * HEAD_DIM, (h + 1) * HEAD_DIM)
                value_part = jnp.dot(
                    grads_turned[lanes, low:high], share, preferred_element_type=f32
                )
                key_part = jnp.dot(
                    queries_turned[lanes, low:high], score_grad, preferred_element_type=f32
                )
                for e in range(s):
                    place = slice((e + 1) * SEG_PAD - SLAB, (e + 1) * SEG_PAD)
                    value_sum[lanes, place] += value_part[:, e * SLAB : (e + 1) * SLAB]
                    key_sum[lanes, place] += key_part[:, e * SLAB : (e + 1) * SLAB]
                place = slice(s * SEG_PAD, s * SEG_PAD + high)
                value_sum[lanes, place] += value_part[:, s * SLAB :]
                key_sum[lanes, place] += key_part[:, s * SLAB :]
            query_grads.append(jnp.where(first_head[low:high], both[0], both[1]))
        query_grad = (jnp.concatenate(query_grads, axis=0) * score_scale).astype(bf16)
        store_segment(dq_ref, starts[s], rows_padded, query_grad)
    key_all = key_sum[...].T.astype(bf16)
    value_all = value_sum[...].T.astype(bf16)
    for s in range(NSEG):
        place = slice(s * SEG_PAD, (s + 1) * SEG_PAD)
        store_segment(dk_ref, starts[s], rows_padded, key_all[place])
        store_segment(dv_ref, starts[s], rows_padded, value_all[place])


def attend_back(qkv, out, grad, share, me, mp_count, rows_padded):
    rows, width = qkv.shape
    pairs = width // 3 // 128
    column = pl.BlockSpec((rows, 128), lambda n, me_ref: (0, n))
    piece = jax.ShapeDtypeStruct((rows, width // 3), bf16)
    return pl.pallas_call(
        functools.partial(attend_back_kernel, mp_count, rows_padded),
        out_shape=(piece, piece, piece),
        grid_spec=pltpu.PrefetchScalarGridSpec(
            num_scalar_prefetch=1,
            grid=(pairs,),
            in_specs=[
                column,
                pl.BlockSpec((rows, 128), lambda n, me_ref: (0, pairs + n)),
                pl.BlockSpec((rows, 128), lambda n, me_ref: (0, 2 * pairs + n)),
                column,
                column,
                pl.BlockSpec((2, rows, KEYS), lambda n, me_ref: (n, 0, 0)),
            ],
            out_specs=(column, column, column),
            scratch_shapes=[pltpu.VMEM((128, rows), f32), pltpu.VMEM((128, rows), f32)],
        ),
        compiler_params=pltpu.CompilerParams(vmem_limit_bytes=48 * 2**20),
        cost_estimate=expected(23.0),
        name="attend_back",
    )(me, qkv, qkv, qkv, out, grad, share)


def item_rows(present, summary, parts, rows, rows_padded):
    kept = present[:, None] * jnp.concatenate([jnp.ones((NSEG, SEG), jnp.int32), summary], axis=1)
    group = parts // NSEG
    kept = jnp.pad(kept.reshape(NSEG, group, rows), ((0, 0), (0, 0), (0, rows_padded - rows)))
    flags = np.zeros((group, rows_padded), np.int32)
    flags[:, :rows] = (np.arange(PERIOD) >= SEG).reshape(group, rows)
    return kept.reshape(NSEG, group * rows_padded), flags.reshape(group * rows_padded)


def score_bias(kept, flags):
    slab = (kept * flags[None, :])[:, SEG_PAD - SLAB :] == 1
    causal = np.tril(np.ones((SEG_PAD, SEG_PAD), bool))
    itself = np.eye(SEG_PAD, dtype=bool)
    planes = []
    for s in range(NSEG):
        own = (kept[s][None, :] == 1) & causal | itself
        pieces = [jnp.broadcast_to(slab[e][None, :], (SEG_PAD, SLAB)) for e in range(s)] + [own]
        seen = jnp.concatenate(pieces, axis=1)
        planes.append(jnp.pad(seen, ((0, 0), (0, KEYS - seen.shape[1]))))
    return jnp.where(jnp.stack(planes), 0.0, -1e30).astype(f32)


def norm_parts(value):
    center = value - jnp.mean(value, axis=-1, keepdims=True)
    spread = jnp.mean(center * center, axis=-1, keepdims=True)
    scale = lax.rsqrt(spread + norm_eps)
    return center * scale, scale


def norm_back(normed, scale, gain, grad):
    inner = grad * gain
    return scale * (
        inner
        - jnp.mean(inner, axis=-1, keepdims=True)
        - normed * jnp.mean(inner * normed, axis=-1, keepdims=True)
    )


def gelu_both(value):
    c = 0.7978845608028654
    square = value * value
    bend = jnp.tanh(c * (value + 0.044715 * value * square))
    half = 0.5 * (1.0 + bend)
    slope = half + 0.5 * value * (1.0 - bend * bend) * c * (1.0 + 3.0 * 0.044715 * square)
    return value * half, slope


def adam_step(master, grad, first, second, average, factor, rate, decay):
    clipped = grad * factor
    first_new = beta_first * first + (1.0 - beta_first) * clipped
    second_new = beta_second * second + (1.0 - beta_second) * clipped * clipped
    first_hat = first_new * (1.0 / (1.0 - beta_first**STEP))
    second_hat = second_new * (1.0 / (1.0 - beta_second**STEP))
    master_new = master - rate * (first_hat / (jnp.sqrt(second_hat) + adam_eps) + decay * master)
    average_new = average_keep * average + (1.0 - average_keep) * master_new
    return (master_new, first_new, second_new, average_new, master_new.astype(bf16))


def adam_kernel(square_ref, attn_ref, up_ref, down_ref, *refs):
    vector_refs, state, outs = refs[:3], refs[3:23], refs[23:]
    grad_norm = jnp.sqrt(jnp.sum(square_ref[...], keepdims=True))
    factor = jnp.minimum(1.0, clip_limit / (grad_norm + 1e-06))

    def update(part, place, grad, rate, decay):
        old = [ref[place] for ref in state[4 * part : 4 * part + 4]]
        new = adam_step(old[0], grad, *old[1:], factor, rate, decay)
        for ref, value in zip(outs[5 * part : 5 * part + 5], new):
            ref[place] = value

    width = attn_ref.shape[1] // 4
    for n in range(4):
        update(0, n, attn_ref[:, n * width : (n + 1) * width], D ** (-0.5), weight_decay)
    update(1, 0, up_ref[...], D ** (-0.5), weight_decay)
    update(1, 1, down_ref[...], FF ** (-0.5), weight_decay)

    @pl.when(pl.program_id(0) == 0)
    def _():
        for n in range(3):
            update(2 + n, slice(None), vector_refs[n][...], vector_rate, 0.0)


def adam_all(squares, shards, vectors, state):
    attn, hidden = state[0], state[4]
    depth = attn.shape[1]
    tile = 64

    def rows_of(array):
        return pl.BlockSpec((array.shape[0], tile, array.shape[2]), lambda n: (0, n, 0))

    def tall(array):
        return pl.BlockSpec((tile, array.shape[1]), lambda n: (n, 0))

    state_specs = [rows_of(array) for array in state[:8]]
    state_specs += [resident(array.shape) for array in state[8:]]
    out_shape, out_specs = [], []
    for n in range(5):
        group, specs = state[4 * n : 4 * n + 4], state_specs[4 * n : 4 * n + 4]
        out_shape += [jax.ShapeDtypeStruct(array.shape, f32) for array in group]
        out_shape.append(jax.ShapeDtypeStruct(group[0].shape, bf16))
        out_specs += specs + [specs[0]]
    return pl.pallas_call(
        adam_kernel,
        out_shape=out_shape,
        grid=(depth // tile,),
        in_specs=[resident(squares.shape)]
        + [tall(shard) for shard in shards]
        + [resident(vector.shape) for vector in vectors]
        + state_specs,
        out_specs=out_specs,
        compiler_params=pltpu.CompilerParams(vmem_limit_bytes=60 * 2**20),
        cost_estimate=expected(20.0),
        name="adam_all",
    )(squares, *shards, *vectors, *state)


def per_device(
    tokens,
    cotangent,
    present,
    summary_mask,
    attention_weight,
    attention_first,
    attention_second,
    attention_average,
    hidden_weight,
    hidden_first,
    hidden_second,
    hidden_average,
    norm_params,
    norm_first,
    norm_second,
    norm_average,
    head_bias,
    head_first,
    head_second,
    head_average,
    unit_bias,
    unit_first,
    unit_second,
    unit_average,
):
    outer, inner = seq_grid()
    seqs = outer * inner
    parts = lax.axis_size("mp")
    rows = tokens.shape[0]
    rows_padded = SEG_PAD * NSEG // parts
    head_width = attention_weight.shape[2]
    depth = attention_weight.shape[1]
    me = lax.axis_index("mp")
    me_vector = me.astype(jnp.int32)[None]
    order = feature_order()
    back_order = block_order()
    codes = row_codes()
    units = hidden_weight.shape[2]
    total_rows = parts * rows_padded

    norm_size, head_size = norm_params.size, head_bias.size
    packed = jnp.concatenate([norm_params.reshape(-1), head_bias.reshape(-1), unit_bias])
    packed_size = packed.size
    packed_width = 4 * head_width
    packed = jnp.pad(packed, (0, 16 * packed_width - packed_size)).reshape(16, packed_width)
    attn_own = jnp.concatenate(
        [jnp.concatenate([attention_weight[n] for n in range(4)], axis=1), packed], axis=0
    ).astype(bf16)
    row_pad = ((0, rows_padded - rows), (0, 0))
    tokens_all = gather_chips(jnp.pad(tokens, row_pad))
    cotangent_pieces = gather_chips(after(jnp.pad(cotangent, row_pad), *tokens_all))
    up_own, down_own = hidden_weight[0].astype(bf16), hidden_weight[1].astype(bf16)
    attn_line, attn_rest = [attn_own], [ring_rest(attn_own)]
    for i in range(1, outer):
        behind = attn_rest[i - 2] if i > 1 else []
        behind = behind + (tokens_all[1:] if i == outer - 1 else [])
        attn_line.append(shift_outer(after(attn_line[-1], *behind), 1))
        attn_rest.append(ring_rest(attn_line[-1]))
    attn_blocks = attn_line + [rest[j] for j in range(inner - 1) for rest in attn_rest]
    up_line = [up_own, shift_outer(after(up_own, attn_line[-1], *attn_rest[-2]), 1)]
    up_line.append(shift_outer(up_line[1], 1))
    up_line.append(shift_outer(up_line[2], 1))
    down_line = [down_own, shift_outer(after(down_own, up_line[2]), 1)]
    down_line.append(shift_outer(down_line[1], 1))
    down_line.append(shift_outer(down_line[2], 1))
    up_rest = [ring_rest(after(up_own, *attn_rest[-2]))]
    up_rest.append(ring_rest(after(up_line[1], *attn_rest[-1])))

    vectors = jnp.concatenate([block[depth : depth + 1] for block in attn_blocks], axis=0)
    vectors = vectors[:, :packed_size].astype(f32)
    norm_vals = vectors[:, :norm_size].reshape(seqs, 6, depth).transpose(1, 0, 2).reshape(6, D)
    vectors = jnp.take(vectors[:, norm_size:], back_order, axis=0)
    head_vals = vectors[:, :head_size].reshape(seqs, 2, head_width // seqs)
    head_vals = head_vals.transpose(1, 0, 2).reshape(2, head_width)
    unit_vals = vectors[:, head_size:].reshape(-1)

    kept, flags = item_rows(present[0], summary_mask[0], parts, rows, rows_padded)
    bias = score_bias(kept, flags)
    kept_parts = kept.reshape(parts, rows_padded).astype(f32)
    kept_all = jnp.take(kept_parts, jnp.stack([me ^ code for code in codes]), axis=0).reshape(-1, 1)
    kept_own = kept_all[:rows_padded]

    first_all, inputs_own = arrange(
        tokens_all,
        [norm_vals[0:1], norm_vals[1:2]],
        [resident((1, D))] * 2,
        True,
        2,
        "first_norm",
    )
    qkv_bias = jnp.concatenate([head_vals[0], jnp.zeros_like(head_vals[0]), head_vals[1]])
    qkv_scale = np.concatenate(
        [np.full(head_width, score_scale, np.float32), np.ones(2 * head_width, np.float32)]
    )
    qkv = tall_dot(
        [after(first_all, *cotangent_pieces)],
        attn_blocks,
        0,
        3 * head_width,
        project_epilogue,
        [qkv_bias[None], qkv_scale[None]],
        [(total_rows, bf16)],
        "project",
    )[0]
    down_rest = [ring_rest(after(down_own, qkv, *up_rest[0]))]
    qkv = after(qkv, up_line[2], *up_rest[0])
    context, share = attend(qkv, bias, me_vector, parts, rows_padded)
    up_rest.append(ring_rest(after(up_line[2], context, *up_rest[1])))
    up_rest.append(ring_rest(after(up_line[3], *up_rest[2])))
    down_rest.append(ring_rest(after(down_line[1], *up_rest[3])))
    down_rest.append(ring_rest(after(down_line[2], *up_rest[3])))
    down_rest.append(ring_rest(after(down_line[3], *down_rest[1])))
    up_blocks = up_line + [rest[j] for j in range(inner - 1) for rest in up_rest]
    down_blocks = down_line + [rest[j] for j in range(inner - 1) for rest in down_rest]
    context = after(context, *up_rest[1])
    join_parts = wide_dot(context, attn_blocks, 3 * head_width, D, 4, "join")
    join_parts = [join_parts[0], after(join_parts[1], down_line[1], *down_rest[0])]
    attended = scatter_chips(*join_parts) + norm_vals[4]
    attended = after(attended, down_line[2], *up_rest[3])
    feed_grad, cotangent_own = arrange(
        cotangent_pieces,
        [kept_all],
        [pl.BlockSpec((rows_padded, 1), lambda n: (n, 0))],
        False,
        3,
        "feed_grad",
    )
    inputs = inputs_own.astype(f32)
    middle = inputs + kept_own * attended

    normed_two, scale_two = norm_parts(middle)
    second_own = (normed_two * norm_vals[2] + norm_vals[3]).astype(bf16)
    second_all = gather_chips(second_own)
    second_all = after(second_all, down_line[3], *down_rest[1])
    activated, slope, second_others = tall_dot(
        second_all,
        up_blocks,
        0,
        units,
        up_epilogue,
        [unit_vals[None]],
        [(total_rows, bf16), (total_rows, bf16)],
        "up",
        5,
    )
    second_all = second_all + [second_others]

    out_grad = cotangent_own.astype(f32)
    down_bias_grad = jnp.sum(kept_own * out_grad, axis=0)

    activated = after(activated, *down_rest[2])
    down_pairs = [([feed_grad], activated)]
    down_far = far_grads(down_pairs, depth, "down_grad", (3, 1))
    down_last = inner_sum(down_far, 1, *down_rest[3])
    pre_grad, unit_grad = tall_dot(
        [feed_grad],
        down_blocks,
        0,
        units,
        slope_epilogue,
        [slope],
        [(total_rows, bf16), (8, f32)],
        "down_back",
    )
    unit_grad = unit_grad[0]
    down_first = inner_sum(down_far, 0, pre_grad)
    down_near = near_grads([([after(feed_grad, pre_grad)], activated)], depth, "down_grad")
    down_totals = ring_scatter(down_near, single_blocks([down_first, down_last], depth))
    pre_grad = after(pre_grad, down_last, down_near)
    second_parts = wide_dot(pre_grad, up_blocks, 0, D, 6, "up_back")
    up_pairs = [(after(second_all, *second_parts), pre_grad)]
    up_far = far_grads(up_pairs, depth, "up_grad", (1, 2, 1))
    up_near = near_grads(up_pairs, depth, "up_grad")
    second_grad = after(scatter_chips(*second_parts), up_near, *[far[2] for far in up_far])
    gain_two_grad = jnp.sum(second_grad * normed_two, axis=0)
    shift_two_grad = jnp.sum(second_grad, axis=0)
    middle_grad = out_grad + norm_back(normed_two, scale_two, norm_vals[2], second_grad)

    attn_grad = kept_own * middle_grad
    out_bias_grad = jnp.sum(attn_grad, axis=0)
    up_last = inner_sum(up_far, 2, second_grad)
    feed_parts = wide_dot(after(activated, second_grad), down_blocks, 0, D, 8, "down")
    attn_rows = after(gather_chips(attn_grad.astype(bf16)), down_first, up_last, *feed_parts)
    context_grad, attn_others = tall_dot(
        attn_rows,
        attn_blocks,
        3 * head_width,
        head_width,
        plain_epilogue,
        [],
        [(total_rows, bf16)],
        "join_back",
        7,
    )
    attn_rows = attn_rows + [attn_others]
    up_middle = inner_sum(up_far, 1, down_first)
    context_grad = after(context_grad, down_totals[2])
    feed_parts = after(feed_parts, context_grad)
    feed_out = scatter_chips(*feed_parts) + norm_vals[5]
    block_output = from_blocks(middle + kept_own * feed_out, order, rows)
    query_grad, key_grad, value_grad = attend_back(
        qkv, context, context_grad, share, me_vector, parts, rows_padded
    )
    qkv_grad = jnp.concatenate([query_grad, key_grad, value_grad], axis=1)
    head_grad = jnp.stack(
        [jnp.sum(query_grad, axis=0, dtype=f32), jnp.sum(value_grad, axis=0, dtype=f32)]
    )
    up_first = inner_sum(up_far, 0, up_last, qkv_grad)
    up_totals = ring_scatter(up_near, single_blocks([up_first, up_middle, up_last], depth))
    down_grad, up_grad = down_totals[-1], up_totals[-1]
    attn_pairs = [
        ([after(first_all, up_totals[1])], qkv_grad),
        (attn_rows, context),
    ]
    attn_far = far_grads(attn_pairs, depth, "attn_grad", (1, 1, 1, 1))
    all_far = [part for far in attn_far for part in far]
    attn_pairs = [
        ([after(first_all, down_grad, up_totals[2], *all_far)], qkv_grad),
        (attn_rows, context),
    ]
    attn_near = near_grads(attn_pairs, depth, "attn_grad")
    attn_sums = [None] * outer
    attn_sums[3] = inner_sum(attn_far, 3, up_middle)
    attn_sums[2] = inner_sum(attn_far, 2, up_first)
    attn_totals = [attn_near[3 * depth :].astype(f32) + attn_sums[3].astype(f32)]
    attn_totals[0] = attn_totals[0].astype(bf16)
    first_parts = wide_dot(
        after(qkv_grad, up_middle, attn_totals[0]), attn_blocks, 0, D, 9, "project_back"
    )
    attn_sums[1] = inner_sum(attn_far, 1, attn_sums[3], first_parts[0])
    attn_sums[0] = inner_sum(attn_far, 0, attn_sums[2])
    attn_totals = ring_scatter(attn_near, attn_sums, [up_totals[2], up_grad], attn_totals)
    first_grad = scatter_chips(*first_parts)
    normed_one, scale_one = norm_parts(inputs)
    gain_one_grad = jnp.sum(first_grad * normed_one, axis=0)
    shift_one_grad = jnp.sum(first_grad, axis=0)
    input_grad = from_blocks(
        middle_grad + norm_back(normed_one, scale_one, norm_vals[0], first_grad), order, rows
    )

    vector_grad = jnp.stack(
        [
            gain_one_grad,
            shift_one_grad,
            gain_two_grad,
            shift_two_grad,
            out_bias_grad,
            down_bias_grad,
        ]
    )
    vector_grad = jnp.take(
        vector_grad.reshape(6, seqs, depth).transpose(1, 0, 2).reshape(seqs, -1), back_order, axis=0
    )
    norm_room = -(-norm_size // 1024) * 1024
    room = norm_room + -(-(packed_size - norm_size) // 1024) * 1024
    vectors = jnp.concatenate(
        [
            vector_grad,
            jnp.zeros((seqs, norm_room - norm_size), f32),
            head_grad.reshape(2, seqs, -1).transpose(1, 0, 2).reshape(seqs, -1),
            unit_grad.reshape(seqs, -1),
            jnp.zeros((seqs, room - norm_room - packed_size + norm_size), f32),
        ],
        axis=1,
    )
    vectors = vectors.reshape(seqs, room // 128, 128)
    attn_shard = attn_totals[-1]
    squares = sum(jnp.sum(shard * shard) for shard in (attn_shard, up_grad, down_grad))
    squares = jnp.pad(squares.reshape(1, 1), ((0, 7), (0, 127)))
    vectors, squares = reduce_all(vectors, squares, norm_room // 128)
    grad_norm = jnp.sqrt(jnp.sum(squares))
    vectors = vectors.reshape(-1)
    norm_shard = vectors[:norm_size].reshape(norm_params.shape)
    head_shard = vectors[norm_room : norm_room + head_size].reshape(head_bias.shape)
    unit_shard = vectors[norm_room + head_size : norm_room + packed_size - norm_size]
    updated = adam_all(
        squares,
        [attn_shard, up_grad, down_grad],
        [norm_shard, head_shard, unit_shard[None]],
        [
            attention_weight,
            attention_first,
            attention_second,
            attention_average,
            hidden_weight,
            hidden_first,
            hidden_second,
            hidden_average,
            norm_params,
            norm_first,
            norm_second,
            norm_average,
            head_bias,
            head_first,
            head_second,
            head_average,
            unit_bias[None],
            unit_first[None],
            unit_second[None],
            unit_average[None],
        ],
    )
    return (
        block_output,
        input_grad,
        grad_norm,
        *updated[:20],
        *[value[0] for value in updated[20:]],
    )


def solution(mesh):
    token_spec = P(("seq", "mp"), None)
    weight_spec = P(None, "seq", "mp")
    norm_spec = P(None, "seq")
    head_spec = P(None, ("mp", "seq"))
    unit_spec = P(("mp", "seq"))
    return jax.shard_map(
        per_device,
        mesh=mesh,
        in_specs=(
            token_spec,
            token_spec,
            P("seq", None),
            P("seq", None, None),
            *([weight_spec] * 8),
            *([norm_spec] * 4),
            *([head_spec] * 4),
            *([unit_spec] * 4),
        ),
        out_specs=(
            token_spec,
            token_spec,
            P(),
            *([weight_spec] * 10),
            *([norm_spec] * 5),
            *([head_spec] * 5),
            *([unit_spec] * 5),
        ),
        check_vma=False,
    )
```

```python
import functools

import jax
import jax.numpy as jnp
import numpy as np
from jax import lax
from jax.experimental import pallas as pl
from jax.experimental.pallas import tpu as pltpu
from jax.sharding import PartitionSpec as P

D = 2048
HEAD_DIM = 64
FF = 8192
SUMM = 50
NSEG = 4
SEG = 256
STEP = 10
PERIOD = SEG + SUMM
SEG_PAD = 320
SLAB = 64
KEYS = SLAB * (NSEG - 1) + SEG_PAD

norm_eps = 1e-05
beta_first = 0.9
beta_second = 0.95
adam_eps = 1e-08
clip_limit = 1.0
weight_decay = 0.1
average_keep = 0.6
vector_rate = 0.4
score_scale = HEAD_DIM ** (-0.5)
query_blocks = ((0, 128), (128, SEG_PAD))

RATE = 0.59e9

f32 = jnp.float32
bf16 = jnp.bfloat16


def seq_grid():
    count = lax.axis_size("seq")
    inner = count // 4
    return count // inner, inner


def shift_outer(value, step):
    outer, inner = seq_grid()
    pairs = [
        (a * inner + b, ((a + step) % outer) * inner + b) for a in range(outer) for b in range(inner)
    ]
    return lax.ppermute(value, "seq", pairs)


def shift_inner(value, step):
    outer, inner = seq_grid()
    pairs = [
        (a * inner + b, a * inner + (b + step) % inner) for a in range(outer) for b in range(inner)
    ]
    return lax.ppermute(value, "seq", pairs)


def swap(value, bits):
    return lax.ppermute(value, "mp", [(m, m ^ bits) for m in range(lax.axis_size("mp"))])


def block_order():
    outer, inner = seq_grid()
    me = lax.axis_index("seq")
    mine_a, mine_b = me // inner, me % inner
    return jnp.stack(
        [
            ((mine_b - b + inner) % inner) * outer + (mine_a - a + outer) % outer
            for a in range(outer)
            for b in range(inner)
        ]
    ).astype(jnp.int32)


def feature_order():
    outer, inner = seq_grid()
    me = lax.axis_index("seq")
    mine_a, mine_b = me // inner, me % inner
    return jnp.stack(
        [
            ((mine_a - i + outer) % outer) * inner + (mine_b - j + inner) % inner
            for j in range(inner)
            for i in range(outer)
        ]
    ).astype(jnp.int32)


def after(value, *others):
    return lax.optimization_barrier((value, *others))[0] if others else value


def row_codes():
    count = lax.axis_size("mp")
    return [high * 2 + low for low in range(2) for high in range(count // 2)]


def ring_rest(part):
    rest = []
    for _ in range(seq_grid()[1] - 1):
        part = shift_inner(part, 1)
        rest.append(part)
    return rest


def halved():
    return seq_grid()[1] == 2


def ring_end(part, rest, ready, late=()):
    if not halved():
        return [[piece] for piece in ring_rest(after(part, *ready))]
    half = part.shape[0] // 2
    upper = shift_inner(after(part[:half], *ready), 1)
    return [[upper, shift_outer(after(rest[0][half:], *late), 1)]]


def stack_ring(line, rest, end):
    pieces = list(line)
    for j in range(seq_grid()[1] - 1):
        pieces += [blocks[j] for blocks in rest] + end[j]
    return [(piece, piece.shape[0]) for piece in pieces]


def ring_scatter(near, received, held=(), sums=()):
    sums, hop = list(sums), None
    depth = received[0].shape[0]
    for n in range(len(sums), len(received)):
        i = len(received) - 1 - n
        total = near[i * depth : (i + 1) * depth].astype(f32) + received[i].astype(f32)
        if sums:
            hop = shift_outer(after(sums[-1], *held[n - 1 : n]), -1)
            total = total + hop.astype(f32)
        sums.append(total.astype(bf16) if i else total)
    return sums, hop


def greet(peers):
    barrier = pltpu.get_barrier_semaphore()
    for peer in peers:
        pl.semaphore_signal(barrier, inc=1, device_id=peer, device_id_type=pl.DeviceIdType.MESH)
    pl.semaphore_wait(barrier, len(peers))


def others(axis, count):
    me = lax.axis_index(axis)
    return [lax.rem(me + step, count) for step in range(1, count)]


def exchange(axis, count, pieces, slots, send_sems, recv_sems):
    copies = []
    for step, peer in enumerate(others(axis, count)):
        copy = pltpu.make_async_remote_copy(
            src_ref=pieces(peer),
            dst_ref=slots.at[step],
            send_sem=send_sems.at[step],
            recv_sem=recv_sems.at[step],
            device_id={axis: peer},
            device_id_type=pl.DeviceIdType.MESH,
        )
        copy.start()
        copies.append(copy)
    return copies


def in_order(axis, count, mine, slots):
    me = lax.axis_index(axis)
    total = jnp.zeros_like(mine)
    for place in range(count):
        step = lax.rem(me + 2 * count - place - 1, count)
        other = slots[jnp.minimum(step, count - 2)]
        total = total + jnp.where(place == me, mine, other)
    return total


def square_tile(value):
    return jnp.sum((value * value).reshape(-1, 8, 128), axis=0)


def reduce_kernel(seqs, parts, shared, *refs):
    vector_ref, square_ref, out_ref, total_ref = refs[:4]
    first, norms, tiles, last = refs[4:8]
    sems = refs[8:]
    greet(
        [{"seq": peer} for peer in others("seq", seqs)]
        + [{"mp": peer} for peer in others("mp", parts)]
    )
    copies = exchange("seq", seqs, lambda peer: vector_ref.at[peer], first, sems[0], sems[1])
    value = vector_ref[lax.axis_index("seq")]
    for step, copy in enumerate(copies):
        copy.wait()
        value = value + first[step]
    out_ref[...] = value
    total_ref[...] = square_ref[...] + square_tile(value[shared:])
    copies = exchange("mp", parts, lambda peer: out_ref.at[:shared], norms, sems[2], sems[3])
    copies += exchange("mp", parts, lambda peer: total_ref, tiles, sems[4], sems[5])
    for copy in copies:
        copy.wait()
    norm = in_order("mp", parts, value[:shared], norms)
    tile = in_order("mp", parts, total_ref[...], tiles) + square_tile(norm)
    out_ref[:shared] = norm
    total_ref[...] = tile
    copies = exchange("seq", seqs, lambda peer: total_ref, last, sems[6], sems[7])
    for copy in copies:
        copy.wait()
    total_ref[...] = in_order("seq", seqs, tile, last)


def reduce_all(vectors, squares, shared):
    seqs, parts = lax.axis_size("seq"), lax.axis_size("mp")
    vmem = pl.BlockSpec(memory_space=pltpu.VMEM)
    block = vectors.shape[1:]
    counts = [seqs, seqs, parts, parts, parts, parts, seqs, seqs]
    return pl.pallas_call(
        functools.partial(reduce_kernel, seqs, parts, shared),
        out_shape=[
            jax.ShapeDtypeStruct(block, f32),
            jax.ShapeDtypeStruct((8, 128), f32),
        ],
        in_specs=[vmem, vmem],
        out_specs=[vmem, vmem],
        scratch_shapes=[
            pltpu.VMEM((seqs - 1, *block), f32),
            pltpu.VMEM((parts - 1, shared, 128), f32),
            pltpu.VMEM((parts - 1, 8, 128), f32),
            pltpu.VMEM((seqs - 1, 8, 128), f32),
        ]
        + [pltpu.SemaphoreType.DMA((count - 1,)) for count in counts],
        compiler_params=pltpu.CompilerParams(
            vmem_limit_bytes=4 * 2**20, collective_id=0, has_side_effects=True
        ),
        cost_estimate=expected(12.0),
        name="reduce_all",
    )(vectors, squares)


def gather_chips(own):
    high = [own]
    for bit in range(1, lax.axis_size("mp").bit_length() - 1):
        high = high + [swap(part, 1 << bit) for part in high]
    return high


def scatter_chips(first, second):
    count = lax.axis_size("mp") // 2
    rows = 2 * first.shape[0] // count
    total = first[:rows]
    for n in range(1, count):
        at = n * rows
        if at < first.shape[0]:
            part = first[at : at + rows].astype(bf16)
        else:
            part = second[at - first.shape[0] : at - first.shape[0] + rows]
        total = total + swap(part, n * 2).astype(f32)
    return total


def other_core():
    me = lax.axis_index("mp")
    return {"mp": me + 1 - 2 * lax.rem(me, 2)}


def core_copy(src, dst, send_sem, recv_sem):
    return pltpu.make_async_remote_copy(
        src_ref=src,
        dst_ref=dst,
        send_sem=send_sem,
        recv_sem=recv_sem,
        device_id=other_core(),
        device_id_type=pl.DeviceIdType.MESH,
    )


def kernel_params(number):
    return pltpu.CompilerParams(
        vmem_limit_bytes=56 * 2**20, collective_id=number, has_side_effects=True
    )


def expected(microseconds):
    return pl.CostEstimate(
        flops=int(microseconds * RATE), bytes_accessed=0, transcendentals=0
    )


def estimate(rows, depth, columns):
    return expected(1.5 + rows * depth * columns * 2 / 7.2e8)


def resident(shape):
    return pl.BlockSpec(shape, lambda *place: (0,) * len(shape))


def arrange_kernel(lefts, blocks, grid, normed, *refs):
    pieces, rest = refs[:lefts], refs[lefts:-3]
    got, send_sem, recv_sem = refs[-3:]
    out_ref, own_ref = rest[-2:]
    step = pl.program_id(0)
    rows, width = pieces[0].shape
    wide = width // blocks
    outer, inner = grid
    me = lax.axis_index("seq")
    mine_a, mine_b = me // inner, lax.rem(me, inner)

    def copy(n):
        return core_copy(pieces[n], got.at[n], send_sem.at[n], recv_sem.at[n])

    @pl.when(step == 0)
    def _():
        greet([other_core()])
        for n in range(lefts):
            copy(n).start()

    def fill(p, load):
        if normed:
            value = load(slice(None)).astype(f32)
            mean = jnp.mean(value, axis=-1, keepdims=True)
            center = value - mean
            scale = lax.rsqrt(jnp.mean(center * center, axis=-1, keepdims=True) + norm_eps)
        for b in range(blocks):
            place = lax.rem(mine_a - b % outer + outer, outer) * inner
            place = place + lax.rem(mine_b - b // outer + inner, inner)
            here = slice(b * wide, (b + 1) * wide)
            part = load(pl.ds(pl.multiple_of(place * wide, wide), wide))
            if p == 0:
                own_ref[:, here] = part
            part = part.astype(f32)
            if normed:
                part = (part - mean) * scale * rest[0][:, here] + rest[1][:, here]
            else:
                part = part * rest[0][...]
            out_ref[:, here] = part.astype(bf16)

    for n in range(lefts):

        @pl.when(step == n)
        def _(n=n):
            fill(n, lambda columns: pieces[n][:, columns])

        @pl.when(step == lefts + n)
        def _(n=n):
            copy(n).wait()
            fill(lefts + n, lambda columns: got[n, :, columns])


def arrange(pieces, extras, extra_specs, normed, number, name):
    rows, width = pieces[0].shape
    lefts = len(pieces)
    return pl.pallas_call(
        functools.partial(arrange_kernel, lefts, lax.axis_size("seq"), seq_grid(), normed),
        out_shape=[
            jax.ShapeDtypeStruct((2 * lefts * rows, width), bf16),
            jax.ShapeDtypeStruct((rows, width), bf16),
        ],
        grid=(2 * lefts,),
        in_specs=[resident((rows, width))] * lefts + extra_specs,
        out_specs=[pl.BlockSpec((rows, width), lambda n: (n, 0)), resident((rows, width))],
        scratch_shapes=[
            pltpu.VMEM((lefts, rows, width), bf16),
            pltpu.SemaphoreType.DMA((lefts,)),
            pltpu.SemaphoreType.DMA((lefts,)),
        ],
        compiler_params=kernel_params(number),
        cost_estimate=expected(9.0),
        name=name,
    )(*pieces, *extras)


def tall_kernel(epilogue, exchanged, lefts, blocks, extras, *refs):
    weight = jnp.concatenate([ref[...] for ref in refs[lefts : lefts + blocks]], axis=0)
    rest = refs[lefts + blocks :]
    step = pl.program_id(0)
    rows = refs[0].shape[0]
    if exchanged:
        others_ref, got, send_sem, recv_sem = rest[-4:]
        rest = rest[:-4]

        def copy(n):
            return core_copy(refs[n], got.at[n], send_sem.at[n], recv_sem.at[n])

        @pl.when(step == 0)
        def _():
            greet([other_core()])
            for n in range(lefts):
                copy(n).start()

    def fill(left, at):
        result = jnp.dot(left, weight, preferred_element_type=f32)
        epilogue(result, slice(at, at + rows), rest[:extras], rest[extras:])

    for n in range(lefts):
        fill(refs[n][...], n * rows)
    if exchanged:

        @pl.when(step == 0)
        def _():
            for n in range(lefts):
                copy(n).wait()

        for n in range(lefts):
            fill(got[n], (lefts + n) * rows)

        @pl.when(step == pl.num_programs(0) - 1)
        def _():
            for n in range(lefts):
                others_ref[n * rows : (n + 1) * rows, :] = got[n]


def tall_dot(lefts, blocks, start, width, epilogue, extras, outs, name, number=None):
    rows, depth = lefts[0].shape
    exchanged = number is not None
    count = len(lefts) * (2 if exchanged else 1)
    tile = max(size for size in (128, 256, 512) if width % size == 0 and start % size == 0)
    first = start // tile
    specs = [pl.BlockSpec((high, tile), lambda n: (0, first + n)) for _, high in blocks]
    blocks = [block for block, _ in blocks]
    out_shape = [jax.ShapeDtypeStruct((height, width), dtype) for height, dtype in outs]
    out_specs = [pl.BlockSpec((height, tile), lambda n: (0, n)) for height, _ in outs]
    scratch = []
    params = pltpu.CompilerParams(vmem_limit_bytes=56 * 2**20)
    if exchanged:
        out_shape.append(jax.ShapeDtypeStruct((len(lefts) * rows, depth), bf16))
        out_specs.append(resident((len(lefts) * rows, depth)))
        scratch = [
            pltpu.VMEM((len(lefts), rows, depth), bf16),
            pltpu.SemaphoreType.DMA((len(lefts),)),
            pltpu.SemaphoreType.DMA((len(lefts),)),
        ]
        params = kernel_params(number)
    return pl.pallas_call(
        functools.partial(
            tall_kernel, epilogue, exchanged, len(lefts), len(blocks), len(extras)
        ),
        out_shape=out_shape,
        grid=(width // tile,),
        in_specs=[resident(left.shape) for left in lefts]
        + specs
        + [pl.BlockSpec((extra.shape[0], tile), lambda n: (0, n)) for extra in extras],
        out_specs=out_specs,
        scratch_shapes=scratch,
        compiler_params=params,
        cost_estimate=estimate(rows * count, depth, width),
        name=name,
    )(*lefts, *blocks, *extras)


def plain_epilogue(result, here, extras, outs):
    outs[0][here, :] = result.astype(bf16)


def project_epilogue(result, here, extras, outs):
    bias, scale = extras
    outs[0][here, :] = ((result + bias[...]).astype(bf16).astype(f32) * scale[...]).astype(bf16)


def up_epilogue(result, here, extras, outs):
    value, slope = gelu_both(result + extras[0][...])
    outs[0][here, :] = value.astype(bf16)
    outs[1][here, :] = slope.astype(bf16)


def slope_epilogue(result, here, extras, outs):
    grad = (result * extras[0][here, :].astype(f32)).astype(bf16)
    outs[0][here, :] = grad
    sums = jnp.sum(grad.astype(f32), axis=0, keepdims=True)
    outs[1][...] = jnp.broadcast_to(sums, outs[1].shape)


def wide_kernel(blocks, start, left_ref, *refs):
    first_ref, second_ref, sent, got, send_sem, recv_sem = refs[blocks:]
    step = pl.program_id(0)
    columns = slice(start, start + left_ref.shape[1])

    def copy(n):
        return core_copy(sent.at[n], got.at[n], send_sem.at[n], recv_sem.at[n])

    @pl.when(step == 0)
    def _():
        greet([other_core()])

    result = lax.dot_general(
        left_ref[...],
        jnp.concatenate([ref[:, columns] for ref in refs[:blocks]], axis=0),
        (((1,), (1,)), ((), ())),
        preferred_element_type=f32,
    )
    for n in range(2):

        @pl.when(step == n)
        def _(n=n):
            sent[n] = result.astype(bf16)
            copy(n).start()

    @pl.when(step == 2)
    def _():
        copy(0).wait()
        second_ref[...] = (result + got[0].astype(f32)).astype(bf16)

    @pl.when(step == 3)
    def _():
        copy(1).wait()
        first_ref[...] = result + got[1].astype(f32)


def wide_dot(left, blocks, start, features, number, name, weight=1.0):
    rows, width = left.shape
    tile = rows // 4
    specs = [resident((high, block.shape[1])) for block, high in blocks]
    blocks = [block for block, _ in blocks]
    return pl.pallas_call(
        functools.partial(wide_kernel, len(blocks), start),
        out_shape=[
            jax.ShapeDtypeStruct((tile, features), f32),
            jax.ShapeDtypeStruct((tile, features), bf16),
        ],
        grid=(4,),
        in_specs=[pl.BlockSpec((tile, width), lambda n: (3 - n, 0))] + specs,
        out_specs=[resident((tile, features)), resident((tile, features))],
        scratch_shapes=[
            pltpu.VMEM((2, tile, features), bf16),
            pltpu.VMEM((2, tile, features), bf16),
            pltpu.SemaphoreType.DMA((2,)),
            pltpu.SemaphoreType.DMA((2,)),
        ],
        compiler_params=kernel_params(number),
        cost_estimate=estimate(rows, width * weight, features),
        name=name,
    )(left, *blocks)


def turned_kernel(shapes, sizes, *refs):
    refs = list(refs)
    groups = [[refs.pop(0) for _ in range(count)] for count in shapes]
    rights = [refs.pop(0) for _ in shapes]

    def fill(out_ref, here):
        at = 0
        for lefts, right_ref in zip(groups, rights):
            width = right_ref.shape[1]
            left = jnp.concatenate([ref[...] for ref in lefts], axis=0)
            out_ref[here, at : at + width] = lax.dot_general(
                left, right_ref[...], (((0,), (0,)), ((), ())), preferred_element_type=f32
            ).astype(bf16)
            at += width

    if sizes is None:
        fill(refs[0], slice(None))
    else:
        step = 0
        for size, out_ref in zip(sizes, refs):
            depth = out_ref.shape[0] // size
            for n in range(size):
                here = slice(n * depth, (n + 1) * depth)
                pl.when(pl.program_id(0) == step)(functools.partial(fill, out_ref, here))
                step += 1


def turned_dot(pairs, first, count, depth, name, sizes=None):
    width = sum(right.shape[1] for _, right in pairs)
    rows = pairs[0][1].shape[0]
    if sizes is None:
        out_shape = [jax.ShapeDtypeStruct((count * depth, width), bf16)]
        out_specs = [pl.BlockSpec((depth, width), lambda n: (n, 0))]
    else:
        out_shape = [jax.ShapeDtypeStruct((size * depth, width), bf16) for size in sizes]
        out_specs = [resident((size * depth, width)) for size in sizes]
    return pl.pallas_call(
        functools.partial(turned_kernel, [len(lefts) for lefts, _ in pairs], sizes),
        out_shape=out_shape,
        grid=(count,),
        in_specs=[
            pl.BlockSpec((left.shape[0], depth), lambda n: (0, first + n))
            for lefts, _ in pairs
            for left in lefts
        ]
        + [resident(right.shape) for _, right in pairs],
        out_specs=out_specs,
        compiler_params=pltpu.CompilerParams(vmem_limit_bytes=56 * 2**20),
        cost_estimate=estimate(rows, count * depth, width),
        name=name,
    )(*[left for lefts, _ in pairs for left in lefts], *[right for _, right in pairs])


def far_grads(pairs, depth, name, sizes):
    outer, inner = seq_grid()
    return [
        turned_dot(pairs, j * outer, outer, depth, name + "_far", sizes) for j in range(1, inner)
    ]


def near_grads(pairs, depth, name):
    return turned_dot(pairs, 0, seq_grid()[0], depth, name + "_near")[0]


def inner_sum(far, n, *ready):
    part = shift_inner(after(far[-1][n], *ready), -1)
    for parts in reversed(far[:-1]):
        part = shift_inner((parts[n].astype(f32) + part.astype(f32)).astype(bf16), -1)
    return part


def single_blocks(groups, depth):
    return [
        group[n * depth : (n + 1) * depth]
        for group in groups
        for n in range(group.shape[0] // depth)
    ]


def from_blocks_kernel(blocks, order_ref, in_ref, out_ref):
    rows, width = out_ref.shape
    wide = width // blocks
    for b in range(blocks):
        there = pl.ds(pl.multiple_of(order_ref[b] * wide, wide), wide)
        out_ref[:, there] = in_ref[:rows, b * wide : (b + 1) * wide].astype(out_ref.dtype)


def from_blocks(value, order, rows):
    rows_padded, width = value.shape
    return pl.pallas_call(
        functools.partial(from_blocks_kernel, order.shape[0]),
        out_shape=jax.ShapeDtypeStruct((rows, width), bf16),
        in_specs=[
            pl.BlockSpec(memory_space=pltpu.SMEM),
            pl.BlockSpec(memory_space=pltpu.VMEM),
        ],
        out_specs=pl.BlockSpec(memory_space=pltpu.VMEM),
        compiler_params=pltpu.CompilerParams(vmem_limit_bytes=12 * 2**20),
        cost_estimate=expected(3.0),
        name="from_blocks",
    )(order, value)


def segment_starts(me, mp_count, rows_padded):
    group = mp_count // NSEG
    starts = []
    for s in range(NSEG):
        pieces = []
        for r in range(group):
            code = jnp.bitwise_xor(me, s * group + r)
            place = jnp.bitwise_and(code, 1) * (mp_count // 2) + lax.shift_right_logical(code, 1)
            pieces.append(pl.multiple_of(place * rows_padded, rows_padded))
        starts.append(pieces)
    return starts


def load_segment(ref, pieces, rows_padded):
    parts = [ref[pl.ds(start, rows_padded), :] for start in pieces]
    return parts[0] if len(parts) == 1 else jnp.concatenate(parts, axis=0)


def load_slab(ref, pieces, rows_padded):
    return ref[pl.ds(pl.multiple_of(pieces[-1] + (rows_padded - SLAB), 16), SLAB), :]


def store_segment(ref, pieces, rows_padded, value):
    for r, start in enumerate(pieces):
        ref[pl.ds(start, rows_padded), :] = value[r * rows_padded : (r + 1) * rows_padded]


def lane_halves(shape):
    lane = lax.broadcasted_iota(jnp.int32, shape, 1)
    return lane < HEAD_DIM


def attend_kernel(mp_count, rows_padded, me_ref, q_ref, k_ref, v_ref, bias_ref, o_ref, p_ref):
    starts = segment_starts(me_ref[0], mp_count, rows_padded)
    for s in range(NSEG):
        keys = jnp.concatenate(
            [load_slab(k_ref, starts[e], rows_padded) for e in range(s)]
            + [load_segment(k_ref, starts[s], rows_padded)],
            axis=0,
        )
        values = jnp.concatenate(
            [load_slab(v_ref, starts[e], rows_padded) for e in range(s)]
            + [load_segment(v_ref, starts[s], rows_padded)],
            axis=0,
        )
        queries = load_segment(q_ref, starts[s], rows_padded)
        first_head = lane_halves(queries.shape)
        zero = jnp.zeros_like(queries)
        head_queries = (jnp.where(first_head, queries, zero), jnp.where(first_head, zero, queries))
        units = [(low, high, h) for low, high in query_blocks for h in range(2)]
        scores = [
            lax.dot_general(
                head_queries[h][low:high],
                keys[: SLAB * s + high],
                (((1,), (1,)), ((), ())),
                preferred_element_type=f32,
            )
            + bias_ref[s, low:high, : SLAB * s + high]
            for low, high, h in units
        ]
        shares = []
        for (low, high, h), score in zip(units, scores):
            raised = jnp.exp(score - jnp.max(score, axis=-1, keepdims=True))
            share = raised * (1.0 / jnp.sum(raised, axis=-1, keepdims=True))
            shares.append(share.astype(bf16))
            p_ref[h, s * SEG_PAD + low : s * SEG_PAD + high, : SLAB * s + high] = shares[-1]
        both = [
            jnp.dot(share, values[: SLAB * s + high], preferred_element_type=f32)
            for (low, high, h), share in zip(units, shares)
        ]
        outs = [
            jnp.where(first_head[low:high], both[2 * n], both[2 * n + 1])
            for n, (low, high) in enumerate(query_blocks)
        ]
        out = jnp.concatenate(outs, axis=0).astype(bf16)
        store_segment(o_ref, starts[s], rows_padded, out)


def attend(qkv, bias, me, mp_count, rows_padded):
    rows, width = qkv.shape
    pairs = width // 3 // 128
    return pl.pallas_call(
        functools.partial(attend_kernel, mp_count, rows_padded),
        out_shape=(
            jax.ShapeDtypeStruct((rows, width // 3), bf16),
            jax.ShapeDtypeStruct((pairs * 2, rows, KEYS), bf16),
        ),
        grid_spec=pltpu.PrefetchScalarGridSpec(
            num_scalar_prefetch=1,
            grid=(pairs,),
            in_specs=[
                pl.BlockSpec((rows, 128), lambda n, me_ref: (0, n)),
                pl.BlockSpec((rows, 128), lambda n, me_ref: (0, pairs + n)),
                pl.BlockSpec((rows, 128), lambda n, me_ref: (0, 2 * pairs + n)),
                pl.BlockSpec(bias.shape, lambda n, me_ref: (0, 0, 0)),
            ],
            out_specs=(
                pl.BlockSpec((rows, 128), lambda n, me_ref: (0, n)),
                pl.BlockSpec((2, rows, KEYS), lambda n, me_ref: (n, 0, 0)),
            ),
        ),
        compiler_params=pltpu.CompilerParams(vmem_limit_bytes=48 * 2**20),
        cost_estimate=expected(12.0),
        name="attend",
    )(me, qkv, qkv, qkv, bias)


def attend_back_kernel(
    mp_count,
    rows_padded,
    me_ref,
    q_ref,
    k_ref,
    v_ref,
    o_ref,
    g_ref,
    p_ref,
    dq_ref,
    dk_ref,
    dv_ref,
    key_sum,
    value_sum,
):
    starts = segment_starts(me_ref[0], mp_count, rows_padded)
    key_sum[...] = jnp.zeros_like(key_sum)
    value_sum[...] = jnp.zeros_like(value_sum)
    for s in range(NSEG):
        keys = jnp.concatenate(
            [load_slab(k_ref, starts[e], rows_padded) for e in range(s)]
            + [load_segment(k_ref, starts[s], rows_padded)],
            axis=0,
        )
        values = jnp.concatenate(
            [load_slab(v_ref, starts[e], rows_padded) for e in range(s)]
            + [load_segment(v_ref, starts[s], rows_padded)],
            axis=0,
        )
        queries = load_segment(q_ref, starts[s], rows_padded)
        grads = load_segment(g_ref, starts[s], rows_padded)
        outs = load_segment(o_ref, starts[s], rows_padded)
        queries_turned = queries.astype(f32).T.astype(bf16)
        grads_turned = grads.astype(f32).T.astype(bf16)
        first_head = lane_halves(queries.shape)
        zero = jnp.zeros_like(queries)
        head_grads = (jnp.where(first_head, grads, zero), jnp.where(first_head, zero, grads))
        product = grads.astype(f32) * outs.astype(f32)
        head_deltas = (
            jnp.sum(jnp.where(first_head, product, 0.0), axis=-1, keepdims=True),
            jnp.sum(jnp.where(first_head, 0.0, product), axis=-1, keepdims=True),
        )
        units = [(low, high, h) for low, high in query_blocks for h in range(2)]
        shares = [
            p_ref[h, s * SEG_PAD + low : s * SEG_PAD + high, : SLAB * s + high]
            for low, high, h in units
        ]
        share_grads = [
            lax.dot_general(
                head_grads[h][low:high],
                values[: SLAB * s + high],
                (((1,), (1,)), ((), ())),
                preferred_element_type=f32,
            )
            for low, high, h in units
        ]
        score_grads = [
            (share.astype(f32) * (share_grad - head_deltas[h][low:high])).astype(bf16)
            for (low, high, h), share, share_grad in zip(units, shares, share_grads)
        ]
        both = [
            jnp.dot(score_grad, keys[: SLAB * s + high], preferred_element_type=f32)
            for (low, high, h), score_grad in zip(units, score_grads)
        ]
        query_grads = [
            jnp.where(first_head[low:high], both[2 * n], both[2 * n + 1])
            for n, (low, high) in enumerate(query_blocks)
        ]
        for (low, high, h), share, score_grad in zip(units, shares, score_grads):
            lanes = slice(h * HEAD_DIM, (h + 1) * HEAD_DIM)
            value_part = jnp.dot(grads_turned[lanes, low:high], share, preferred_element_type=f32)
            key_part = jnp.dot(
                queries_turned[lanes, low:high], score_grad, preferred_element_type=f32
            )
            for e in range(s):
                place = slice((e + 1) * SEG_PAD - SLAB, (e + 1) * SEG_PAD)
                value_sum[lanes, place] += value_part[:, e * SLAB : (e + 1) * SLAB]
                key_sum[lanes, place] += key_part[:, e * SLAB : (e + 1) * SLAB]
            place = slice(s * SEG_PAD, s * SEG_PAD + high)
            value_sum[lanes, place] += value_part[:, s * SLAB :]
            key_sum[lanes, place] += key_part[:, s * SLAB :]
        query_grad = (jnp.concatenate(query_grads, axis=0) * score_scale).astype(bf16)
        store_segment(dq_ref, starts[s], rows_padded, query_grad)
    key_all = key_sum[...].T.astype(bf16)
    value_all = value_sum[...].T.astype(bf16)
    for s in range(NSEG):
        place = slice(s * SEG_PAD, (s + 1) * SEG_PAD)
        store_segment(dk_ref, starts[s], rows_padded, key_all[place])
        store_segment(dv_ref, starts[s], rows_padded, value_all[place])


def attend_back(qkv, out, grad, share, me, mp_count, rows_padded):
    rows, width = qkv.shape
    pairs = width // 3 // 128
    column = pl.BlockSpec((rows, 128), lambda n, me_ref: (0, n))
    piece = jax.ShapeDtypeStruct((rows, width // 3), bf16)
    return pl.pallas_call(
        functools.partial(attend_back_kernel, mp_count, rows_padded),
        out_shape=(piece, piece, piece),
        grid_spec=pltpu.PrefetchScalarGridSpec(
            num_scalar_prefetch=1,
            grid=(pairs,),
            in_specs=[
                column,
                pl.BlockSpec((rows, 128), lambda n, me_ref: (0, pairs + n)),
                pl.BlockSpec((rows, 128), lambda n, me_ref: (0, 2 * pairs + n)),
                column,
                column,
                pl.BlockSpec((2, rows, KEYS), lambda n, me_ref: (n, 0, 0)),
            ],
            out_specs=(column, column, column),
            scratch_shapes=[pltpu.VMEM((128, rows), f32), pltpu.VMEM((128, rows), f32)],
        ),
        compiler_params=pltpu.CompilerParams(vmem_limit_bytes=48 * 2**20),
        cost_estimate=expected(12.5),
        name="attend_back",
    )(me, qkv, qkv, qkv, out, grad, share)


def item_rows(present, summary, parts, rows, rows_padded):
    kept = present[:, None] * jnp.concatenate([jnp.ones((NSEG, SEG), jnp.int32), summary], axis=1)
    group = parts // NSEG
    kept = jnp.pad(kept.reshape(NSEG, group, rows), ((0, 0), (0, 0), (0, rows_padded - rows)))
    flags = np.zeros((group, rows_padded), np.int32)
    flags[:, :rows] = (np.arange(PERIOD) >= SEG).reshape(group, rows)
    return kept.reshape(NSEG, group * rows_padded), flags.reshape(group * rows_padded)


def score_bias(kept, flags):
    slab = (kept * flags[None, :])[:, SEG_PAD - SLAB :] == 1
    causal = np.tril(np.ones((SEG_PAD, SEG_PAD), bool))
    itself = np.eye(SEG_PAD, dtype=bool)
    planes = []
    for s in range(NSEG):
        own = (kept[s][None, :] == 1) & causal | itself
        pieces = [jnp.broadcast_to(slab[e][None, :], (SEG_PAD, SLAB)) for e in range(s)] + [own]
        seen = jnp.concatenate(pieces, axis=1)
        planes.append(jnp.pad(seen, ((0, 0), (0, KEYS - seen.shape[1]))))
    return jnp.where(jnp.stack(planes), 0.0, -1e30).astype(f32)


def norm_parts(value):
    center = value - jnp.mean(value, axis=-1, keepdims=True)
    spread = jnp.mean(center * center, axis=-1, keepdims=True)
    scale = lax.rsqrt(spread + norm_eps)
    return center * scale, scale


def norm_back(normed, scale, gain, grad):
    inner = grad * gain
    return scale * (
        inner
        - jnp.mean(inner, axis=-1, keepdims=True)
        - normed * jnp.mean(inner * normed, axis=-1, keepdims=True)
    )


def gelu_both(value):
    c = 0.7978845608028654
    square = value * value
    bend = jnp.tanh(c * (value + 0.044715 * value * square))
    half = 0.5 * (1.0 + bend)
    slope = half + 0.5 * value * (1.0 - bend * bend) * c * (1.0 + 3.0 * 0.044715 * square)
    return value * half, slope


def adam_step(master, grad, first, second, average, factor, rate, decay):
    clipped = grad * factor
    first_new = beta_first * first + (1.0 - beta_first) * clipped
    second_new = beta_second * second + (1.0 - beta_second) * clipped * clipped
    first_hat = first_new * (1.0 / (1.0 - beta_first**STEP))
    second_hat = second_new * (1.0 / (1.0 - beta_second**STEP))
    master_new = master - rate * (first_hat / (jnp.sqrt(second_hat) + adam_eps) + decay * master)
    average_new = average_keep * average + (1.0 - average_keep) * master_new
    return (master_new, first_new, second_new, average_new, master_new.astype(bf16))


def adam_kernel(square_ref, attn_ref, up_ref, down_ref, *refs):
    vector_refs, state, outs = refs[:3], refs[3:23], refs[23:]
    grad_norm = jnp.sqrt(jnp.sum(square_ref[...], keepdims=True))
    factor = jnp.minimum(1.0, clip_limit / (grad_norm + 1e-06))

    def update(part, place, grad, rate, decay):
        old = [ref[place] for ref in state[4 * part : 4 * part + 4]]
        new = adam_step(old[0], grad, *old[1:], factor, rate, decay)
        for ref, value in zip(outs[5 * part : 5 * part + 5], new):
            ref[place] = value

    width = attn_ref.shape[1] // 4
    for n in range(4):
        update(0, n, attn_ref[:, n * width : (n + 1) * width], D ** (-0.5), weight_decay)
    update(1, 0, up_ref[...], D ** (-0.5), weight_decay)
    update(1, 1, down_ref[...], FF ** (-0.5), weight_decay)

    @pl.when(pl.program_id(0) == 0)
    def _():
        for n in range(3):
            update(2 + n, slice(None), vector_refs[n][...], vector_rate, 0.0)


def adam_all(squares, shards, vectors, state):
    attn, hidden = state[0], state[4]
    depth = attn.shape[1]
    tile = 64

    def rows_of(array):
        return pl.BlockSpec((array.shape[0], tile, array.shape[2]), lambda n: (0, n, 0))

    def tall(array):
        return pl.BlockSpec((tile, array.shape[1]), lambda n: (n, 0))

    state_specs = [rows_of(array) for array in state[:8]]
    state_specs += [resident(array.shape) for array in state[8:]]
    out_shape, out_specs = [], []
    for n in range(5):
        group, specs = state[4 * n : 4 * n + 4], state_specs[4 * n : 4 * n + 4]
        out_shape += [jax.ShapeDtypeStruct(array.shape, f32) for array in group]
        out_shape.append(jax.ShapeDtypeStruct(group[0].shape, bf16))
        out_specs += specs + [specs[0]]
    return pl.pallas_call(
        adam_kernel,
        out_shape=out_shape,
        grid=(depth // tile,),
        in_specs=[resident(squares.shape)]
        + [tall(shard) for shard in shards]
        + [resident(vector.shape) for vector in vectors]
        + state_specs,
        out_specs=out_specs,
        compiler_params=pltpu.CompilerParams(vmem_limit_bytes=60 * 2**20),
        cost_estimate=expected(20.0),
        name="adam_all",
    )(squares, *shards, *vectors, *state)


def per_device(
    tokens,
    cotangent,
    present,
    summary_mask,
    attention_weight,
    attention_first,
    attention_second,
    attention_average,
    hidden_weight,
    hidden_first,
    hidden_second,
    hidden_average,
    norm_params,
    norm_first,
    norm_second,
    norm_average,
    head_bias,
    head_first,
    head_second,
    head_average,
    unit_bias,
    unit_first,
    unit_second,
    unit_average,
):
    outer, inner = seq_grid()
    seqs = outer * inner
    parts = lax.axis_size("mp")
    rows = tokens.shape[0]
    rows_padded = SEG_PAD * NSEG // parts
    head_width = attention_weight.shape[2]
    depth = attention_weight.shape[1]
    me = lax.axis_index("mp")
    me_vector = me.astype(jnp.int32)[None]
    order = feature_order()
    back_order = block_order()
    codes = row_codes()
    units = hidden_weight.shape[2]
    total_rows = parts * rows_padded

    norm_size, head_size = norm_params.size, head_bias.size
    packed = jnp.concatenate([norm_params.reshape(-1), head_bias.reshape(-1), unit_bias])
    packed_size = packed.size
    packed_width = 4 * head_width
    packed = jnp.pad(packed, (0, 16 * packed_width - packed_size)).reshape(16, packed_width)
    attn_own = jnp.concatenate(
        [jnp.concatenate([attention_weight[n] for n in range(4)], axis=1), packed], axis=0
    ).astype(bf16)
    row_pad = ((0, rows_padded - rows), (0, 0))
    tokens_all = gather_chips(jnp.pad(tokens, row_pad))
    cotangent_pieces = gather_chips(after(jnp.pad(cotangent, row_pad), *tokens_all))
    up_own, down_own = hidden_weight[0].astype(bf16), hidden_weight[1].astype(bf16)
    attn_line, attn_rest = [attn_own], [ring_rest(attn_own)]
    for i in range(1, outer):
        behind = attn_rest[i - 2] if i > 1 else []
        behind = behind + (tokens_all[1:] if i == outer - 1 else [])
        attn_line.append(shift_outer(after(attn_line[-1], *behind), 1))
        attn_rest.append(ring_rest(attn_line[-1]))
    attn_blocks = attn_line + [rest[j] for j in range(inner - 1) for rest in attn_rest]
    attn_blocks = [(block, depth) for block in attn_blocks]
    up_line = [up_own, shift_outer(after(up_own, attn_line[-1], *attn_rest[-2]), 1)]
    up_line.append(shift_outer(up_line[1], 1))
    up_line.append(shift_outer(up_line[2], 1))
    up_rest = [ring_rest(after(up_own, *attn_rest[-2]))]
    up_rest.append(ring_rest(after(up_line[1], *attn_rest[-1])))

    vectors = jnp.concatenate([block[depth : depth + 1] for block, _ in attn_blocks], axis=0)
    vectors = vectors[:, :packed_size].astype(f32)
    norm_vals = vectors[:, :norm_size].reshape(seqs, 6, depth).transpose(1, 0, 2).reshape(6, D)
    vectors = jnp.take(vectors[:, norm_size:], back_order, axis=0)
    head_vals = vectors[:, :head_size].reshape(seqs, 2, head_width // seqs)
    head_vals = head_vals.transpose(1, 0, 2).reshape(2, head_width)
    unit_vals = vectors[:, head_size:].reshape(-1)

    kept, flags = item_rows(present[0], summary_mask[0], parts, rows, rows_padded)
    bias = score_bias(kept, flags)
    kept_parts = kept.reshape(parts, rows_padded).astype(f32)
    kept_all = jnp.take(kept_parts, jnp.stack([me ^ code for code in codes]), axis=0).reshape(-1, 1)
    kept_own = kept_all[:rows_padded]

    first_all, inputs_own = arrange(
        tokens_all,
        [norm_vals[0:1], norm_vals[1:2]],
        [resident((1, D))] * 2,
        True,
        2,
        "first_norm",
    )
    qkv_bias = jnp.concatenate([head_vals[0], jnp.zeros_like(head_vals[0]), head_vals[1]])
    qkv_scale = np.concatenate(
        [np.full(head_width, score_scale, np.float32), np.ones(2 * head_width, np.float32)]
    )
    qkv = tall_dot(
        [after(first_all, *cotangent_pieces)],
        attn_blocks,
        0,
        3 * head_width,
        project_epilogue,
        [qkv_bias[None], qkv_scale[None]],
        [(total_rows, bf16)],
        "project",
    )[0]
    down_rest = [ring_rest(after(down_own, qkv, *up_rest[0]))]
    qkv = after(qkv, up_line[2], *up_rest[0])
    context, share = attend(qkv, bias, me_vector, parts, rows_padded)
    down_line = [down_own, shift_outer(after(down_own, context), 1)]
    up_rest.append(ring_rest(after(up_line[2], context, *up_rest[1])))
    up_end = ring_end(up_line[3], up_rest[2], up_rest[2])
    up_ends = [part for parts in up_end for part in parts]
    down_line.append(shift_outer(after(down_line[1], up_ends[-1]), 1))
    down_line.append(shift_outer(down_line[2], 1))
    down_rest.append(ring_rest(after(down_line[1], up_ends[0])))
    up_blocks = stack_ring(up_line, up_rest, up_end)
    context = after(context, *up_rest[1])
    join_parts = wide_dot(context, attn_blocks, 3 * head_width, D, 4, "join")
    join_parts = [join_parts[0], after(join_parts[1], up_line[3], *down_rest[0])]
    attended = scatter_chips(*join_parts) + norm_vals[4]
    attended = after(attended, down_line[1], *up_rest[2])
    feed_grad, cotangent_own = arrange(
        cotangent_pieces,
        [kept_all],
        [pl.BlockSpec((rows_padded, 1), lambda n: (n, 0))],
        False,
        3,
        "feed_grad",
    )
    inputs = inputs_own.astype(f32)
    middle = inputs + kept_own * attended

    normed_two, scale_two = norm_parts(middle)
    second_own = (normed_two * norm_vals[2] + norm_vals[3]).astype(bf16)
    second_all = gather_chips(second_own)
    down_rest.append(ring_rest(after(down_line[2], second_all[1])))
    second_all = after(second_all, feed_grad, down_line[2], *down_rest[1])
    activated, slope, second_others = tall_dot(
        second_all,
        up_blocks,
        0,
        units,
        up_epilogue,
        [unit_vals[None]],
        [(total_rows, bf16), (total_rows, bf16)],
        "up",
        5,
    )
    second_all = second_all + [second_others]

    out_grad = cotangent_own.astype(f32)
    down_bias_grad = jnp.sum(kept_own * out_grad, axis=0)

    down_end = ring_end(down_line[3], down_rest[2], [activated, *down_rest[1]], [activated])
    down_ends = [part for parts in down_end for part in parts]
    down_blocks = stack_ring(down_line, down_rest, down_end)
    activated = after(activated, down_line[3], *down_rest[2])
    down_pairs = [([feed_grad], activated)]
    down_far = far_grads(down_pairs, depth, "down_grad", (3, 1))
    down_last = inner_sum(down_far, 1, *down_ends)
    pre_grad, unit_grad = tall_dot(
        [feed_grad],
        down_blocks,
        0,
        units,
        slope_epilogue,
        [slope],
        [(total_rows, bf16), (8, f32)],
        "down_back",
    )
    unit_grad = unit_grad[0]
    down_first = inner_sum(down_far, 0, pre_grad)
    down_near = near_grads([([after(feed_grad, pre_grad)], activated)], depth, "down_grad")
    down_totals, _ = ring_scatter(down_near, single_blocks([down_first, down_last], depth))
    pre_grad = after(pre_grad, down_last, down_near)
    second_parts = wide_dot(pre_grad, up_blocks, 0, D, 6, "up_back")
    up_pairs = [(after(second_all, *second_parts), pre_grad)]
    up_far = far_grads(up_pairs, depth, "up_grad", (2, 1, 1))
    up_near = near_grads(up_pairs, depth, "up_grad")
    second_grad = after(scatter_chips(*second_parts), up_near, *[far[2] for far in up_far])
    gain_two_grad = jnp.sum(second_grad * normed_two, axis=0)
    shift_two_grad = jnp.sum(second_grad, axis=0)
    middle_grad = out_grad + norm_back(normed_two, scale_two, norm_vals[2], second_grad)

    attn_grad = kept_own * middle_grad
    out_bias_grad = jnp.sum(attn_grad, axis=0)
    up_last = inner_sum(up_far, 2, second_grad)
    feed_parts = wide_dot(after(activated, second_grad), down_blocks, 0, D, 8, "down")
    attn_rows = after(gather_chips(attn_grad.astype(bf16)), down_first, up_last, *feed_parts)
    context_grad, attn_others = tall_dot(
        attn_rows,
        attn_blocks,
        3 * head_width,
        head_width,
        plain_epilogue,
        [],
        [(total_rows, bf16)],
        "join_back",
        7,
    )
    attn_rows = attn_rows + [attn_others]
    up_middle = inner_sum(up_far, 1, down_first)
    up_first = inner_sum(up_far, 0, up_last, context_grad)
    context_grad = after(context_grad, down_totals[2])
    feed_parts = after(feed_parts, context_grad)
    feed_out = scatter_chips(*feed_parts) + norm_vals[5]
    block_output = from_blocks(middle + kept_own * feed_out, order, rows)
    query_grad, key_grad, value_grad = attend_back(
        qkv, context, context_grad, share, me_vector, parts, rows_padded
    )
    qkv_grad = jnp.concatenate([query_grad, key_grad, value_grad], axis=1)
    head_grad = jnp.stack(
        [jnp.sum(query_grad, axis=0, dtype=f32), jnp.sum(value_grad, axis=0, dtype=f32)]
    )
    up_totals, up_hop = ring_scatter(up_near, single_blocks([up_first, up_middle, up_last], depth))
    down_grad, up_grad = down_totals[-1], up_totals[-1]
    attn_pairs = [
        ([after(first_all, up_totals[1])], qkv_grad),
        (attn_rows, context),
    ]
    attn_far = far_grads(attn_pairs, depth, "attn_grad", (1, 1, 1, 1))
    all_far = [part for far in attn_far for part in far]
    first_parts = wide_dot(after(qkv_grad, *all_far), attn_blocks, 0, D, 9, "project_back")
    attn_pairs = [
        ([after(first_all, down_grad, up_totals[2], *first_parts)], qkv_grad),
        (attn_rows, context),
    ]
    attn_near = near_grads(attn_pairs, depth, "attn_grad")
    attn_sums = [None] * outer
    attn_sums[3] = inner_sum(attn_far, 3, up_middle)
    attn_sums[2] = inner_sum(attn_far, 2, up_first)
    attn_total = attn_near[3 * depth :].astype(f32) + attn_sums[3].astype(f32)
    attn_total = attn_total.astype(bf16)
    attn_sums[1] = inner_sum(attn_far, 1, attn_total, up_hop)
    attn_sums[0] = inner_sum(attn_far, 0, attn_sums[2])
    attn_totals, _ = ring_scatter(attn_near, attn_sums, [up_hop], [attn_total])
    first_grad = scatter_chips(*first_parts)
    normed_one, scale_one = norm_parts(inputs)
    gain_one_grad = jnp.sum(first_grad * normed_one, axis=0)
    shift_one_grad = jnp.sum(first_grad, axis=0)
    input_grad = from_blocks(
        middle_grad + norm_back(normed_one, scale_one, norm_vals[0], first_grad), order, rows
    )

    vector_grad = jnp.stack(
        [
            gain_one_grad,
            shift_one_grad,
            gain_two_grad,
            shift_two_grad,
            out_bias_grad,
            down_bias_grad,
        ]
    )
    vector_grad = jnp.take(
        vector_grad.reshape(6, seqs, depth).transpose(1, 0, 2).reshape(seqs, -1), back_order, axis=0
    )
    norm_room = -(-norm_size // 1024) * 1024
    room = norm_room + -(-(packed_size - norm_size) // 1024) * 1024
    vectors = jnp.concatenate(
        [
            vector_grad,
            jnp.zeros((seqs, norm_room - norm_size), f32),
            head_grad.reshape(2, seqs, -1).transpose(1, 0, 2).reshape(seqs, -1),
            unit_grad.reshape(seqs, -1),
            jnp.zeros((seqs, room - norm_room - packed_size + norm_size), f32),
        ],
        axis=1,
    )
    vectors = vectors.reshape(seqs, room // 128, 128)
    attn_shard = attn_totals[-1]
    squares = sum(jnp.sum(shard * shard) for shard in (attn_shard, up_grad, down_grad))
    squares = jnp.pad(squares.reshape(1, 1), ((0, 7), (0, 127)))
    vectors, squares = reduce_all(vectors, squares, norm_room // 128)
    grad_norm = jnp.sqrt(jnp.sum(squares))
    vectors = vectors.reshape(-1)
    norm_shard = vectors[:norm_size].reshape(norm_params.shape)
    head_shard = vectors[norm_room : norm_room + head_size].reshape(head_bias.shape)
    unit_shard = vectors[norm_room + head_size : norm_room + packed_size - norm_size]
    updated = adam_all(
        squares,
        [attn_shard, up_grad, down_grad],
        [norm_shard, head_shard, unit_shard[None]],
        [
            attention_weight,
            attention_first,
            attention_second,
            attention_average,
            hidden_weight,
            hidden_first,
            hidden_second,
            hidden_average,
            norm_params,
            norm_first,
            norm_second,
            norm_average,
            head_bias,
            head_first,
            head_second,
            head_average,
            unit_bias[None],
            unit_first[None],
            unit_second[None],
            unit_average[None],
        ],
    )
    return (
        block_output,
        input_grad,
        grad_norm,
        *updated[:20],
        *[value[0] for value in updated[20:]],
    )


def solution(mesh):
    token_spec = P(("seq", "mp"), None)
    weight_spec = P(None, "seq", "mp")
    norm_spec = P(None, "seq")
    head_spec = P(None, ("mp", "seq"))
    unit_spec = P(("mp", "seq"))
    return jax.shard_map(
        per_device,
        mesh=mesh,
        in_specs=(
            token_spec,
            token_spec,
            P("seq", None),
            P("seq", None, None),
            *([weight_spec] * 8),
            *([norm_spec] * 4),
            *([head_spec] * 4),
            *([unit_spec] * 4),
        ),
        out_specs=(
            token_spec,
            token_spec,
            P(),
            *([weight_spec] * 10),
            *([norm_spec] * 5),
            *([head_spec] * 5),
            *([unit_spec] * 5),
        ),
        check_vma=False,
    )
```

```python
import functools

import jax
import jax.numpy as jnp
import numpy as np
from jax import lax
from jax.experimental import pallas as pl
from jax.experimental.pallas import tpu as pltpu
from jax.sharding import PartitionSpec as P

D = 2048
HEAD_DIM = 64
FF = 8192
SUMM = 50
NSEG = 4
SEG = 256
STEP = 10
PERIOD = SEG + SUMM
SEG_PAD = 320
SLAB = 64
KEYS = SLAB * (NSEG - 1) + SEG_PAD

norm_eps = 1e-05
beta_first = 0.9
beta_second = 0.95
adam_eps = 1e-08
clip_limit = 1.0
weight_decay = 0.1
average_keep = 0.6
vector_rate = 0.4
score_scale = HEAD_DIM ** (-0.5)
query_blocks = ((0, 128), (128, SEG_PAD))

RATE = 0.59e9

f32 = jnp.float32
bf16 = jnp.bfloat16


def seq_grid():
    count = lax.axis_size("seq")
    inner = count // 4
    return count // inner, inner


def shift_outer(value, step):
    outer, inner = seq_grid()
    pairs = [
        (a * inner + b, ((a + step) % outer) * inner + b) for a in range(outer) for b in range(inner)
    ]
    return lax.ppermute(value, "seq", pairs)


def shift_inner(value, step):
    outer, inner = seq_grid()
    pairs = [
        (a * inner + b, a * inner + (b + step) % inner) for a in range(outer) for b in range(inner)
    ]
    return lax.ppermute(value, "seq", pairs)


def swap(value, bits):
    return lax.ppermute(value, "mp", [(m, m ^ bits) for m in range(lax.axis_size("mp"))])


def block_order():
    outer, inner = seq_grid()
    me = lax.axis_index("seq")
    mine_a, mine_b = me // inner, me % inner
    return jnp.stack(
        [
            ((mine_b - b + inner) % inner) * outer + (mine_a - a + outer) % outer
            for a in range(outer)
            for b in range(inner)
        ]
    ).astype(jnp.int32)


def feature_order():
    outer, inner = seq_grid()
    me = lax.axis_index("seq")
    mine_a, mine_b = me // inner, me % inner
    return jnp.stack(
        [
            ((mine_a - i + outer) % outer) * inner + (mine_b - j + inner) % inner
            for j in range(inner)
            for i in range(outer)
        ]
    ).astype(jnp.int32)


def after(value, *others):
    return lax.optimization_barrier((value, *others))[0] if others else value


def row_codes():
    count = lax.axis_size("mp")
    return [high * 2 + low for low in range(2) for high in range(count // 2)]


def ring_rest(part):
    rest = []
    for _ in range(seq_grid()[1] - 1):
        part = shift_inner(part, 1)
        rest.append(part)
    return rest


def halved():
    return seq_grid()[1] == 2


def ring_end(part, rest, ready, late=()):
    if not halved():
        return [[piece] for piece in ring_rest(after(part, *ready))]
    half = (part.shape[0] + 31) // 32 * 16
    upper = shift_inner(after(part[:half], *ready), 1)
    return [[upper, shift_outer(after(rest[0][half:], *late), 1)]]


def stack_ring(line, rest, end):
    pieces = list(line)
    for j in range(seq_grid()[1] - 1):
        pieces += [blocks[j] for blocks in rest] + end[j]
    return [(piece, piece.shape[0]) for piece in pieces]


def ring_scatter(near, received, held=(), sums=(), late=()):
    sums, hop = list(sums), None
    depth = received[0].shape[0]
    for n in range(len(sums), len(received)):
        i = len(received) - 1 - n
        part = received[i] if i else after(received[i], *late)
        total = near[i * depth : (i + 1) * depth].astype(f32) + part.astype(f32)
        if sums:
            hop = shift_outer(after(sums[-1], *held[n - 1 : n]), -1)
            total = total + hop.astype(f32)
        sums.append(total.astype(bf16) if i else total)
    return sums, hop


def greet(peers):
    barrier = pltpu.get_barrier_semaphore()
    for peer in peers:
        pl.semaphore_signal(barrier, inc=1, device_id=peer, device_id_type=pl.DeviceIdType.MESH)
    pl.semaphore_wait(barrier, len(peers))


def others(axis, count):
    me = lax.axis_index(axis)
    return [lax.rem(me + step, count) for step in range(1, count)]


def exchange(axis, count, pieces, slots, send_sems, recv_sems):
    copies = []
    for step, peer in enumerate(others(axis, count)):
        copy = pltpu.make_async_remote_copy(
            src_ref=pieces(peer),
            dst_ref=slots.at[step],
            send_sem=send_sems.at[step],
            recv_sem=recv_sems.at[step],
            device_id={axis: peer},
            device_id_type=pl.DeviceIdType.MESH,
        )
        copy.start()
        copies.append(copy)
    return copies


def in_order(axis, count, mine, slots):
    me = lax.axis_index(axis)
    total = jnp.zeros_like(mine)
    for place in range(count):
        step = lax.rem(me + 2 * count - place - 1, count)
        other = slots[jnp.minimum(step, count - 2)]
        total = total + jnp.where(place == me, mine, other)
    return total


def square_tile(value):
    return jnp.sum((value * value).reshape(-1, 8, 128), axis=0)


def reduce_kernel(seqs, parts, shared, *refs):
    vector_ref, square_ref, out_ref, total_ref = refs[:4]
    first, norms, tiles, last = refs[4:8]
    sems = refs[8:]
    greet(
        [{"seq": peer} for peer in others("seq", seqs)]
        + [{"mp": peer} for peer in others("mp", parts)]
    )
    copies = exchange("seq", seqs, lambda peer: vector_ref.at[peer], first, sems[0], sems[1])
    value = vector_ref[lax.axis_index("seq")]
    for step, copy in enumerate(copies):
        copy.wait()
        value = value + first[step]
    out_ref[...] = value
    total_ref[...] = square_ref[...] + square_tile(value[shared:])
    copies = exchange("mp", parts, lambda peer: out_ref.at[:shared], norms, sems[2], sems[3])
    copies += exchange("mp", parts, lambda peer: total_ref, tiles, sems[4], sems[5])
    for copy in copies:
        copy.wait()
    norm = in_order("mp", parts, value[:shared], norms)
    tile = in_order("mp", parts, total_ref[...], tiles) + square_tile(norm)
    out_ref[:shared] = norm
    total_ref[...] = tile
    copies = exchange("seq", seqs, lambda peer: total_ref, last, sems[6], sems[7])
    for copy in copies:
        copy.wait()
    total_ref[...] = in_order("seq", seqs, tile, last)


def reduce_all(vectors, squares, shared):
    seqs, parts = lax.axis_size("seq"), lax.axis_size("mp")
    vmem = pl.BlockSpec(memory_space=pltpu.VMEM)
    block = vectors.shape[1:]
    counts = [seqs, seqs, parts, parts, parts, parts, seqs, seqs]
    return pl.pallas_call(
        functools.partial(reduce_kernel, seqs, parts, shared),
        out_shape=[
            jax.ShapeDtypeStruct(block, f32),
            jax.ShapeDtypeStruct((8, 128), f32),
        ],
        in_specs=[vmem, vmem],
        out_specs=[vmem, vmem],
        scratch_shapes=[
            pltpu.VMEM((seqs - 1, *block), f32),
            pltpu.VMEM((parts - 1, shared, 128), f32),
            pltpu.VMEM((parts - 1, 8, 128), f32),
            pltpu.VMEM((seqs - 1, 8, 128), f32),
        ]
        + [pltpu.SemaphoreType.DMA((count - 1,)) for count in counts],
        compiler_params=pltpu.CompilerParams(
            vmem_limit_bytes=4 * 2**20, collective_id=0, has_side_effects=True
        ),
        cost_estimate=expected(12.0),
        name="reduce_all",
    )(vectors, squares)


def gather_chips(own):
    high = [own]
    for bit in range(1, lax.axis_size("mp").bit_length() - 1):
        high = high + [swap(part, 1 << bit) for part in high]
    return high


def scatter_chips(first, second):
    count = lax.axis_size("mp") // 2
    rows = 2 * first.shape[0] // count
    total = first[:rows]
    for n in range(1, count):
        at = n * rows
        if at < first.shape[0]:
            part = first[at : at + rows].astype(bf16)
        else:
            part = second[at - first.shape[0] : at - first.shape[0] + rows]
        total = total + swap(part, n * 2).astype(f32)
    return total


def other_core():
    me = lax.axis_index("mp")
    return {"mp": me + 1 - 2 * lax.rem(me, 2)}


def core_copy(src, dst, send_sem, recv_sem):
    return pltpu.make_async_remote_copy(
        src_ref=src,
        dst_ref=dst,
        send_sem=send_sem,
        recv_sem=recv_sem,
        device_id=other_core(),
        device_id_type=pl.DeviceIdType.MESH,
    )


def kernel_params(number):
    return pltpu.CompilerParams(
        vmem_limit_bytes=56 * 2**20, collective_id=number, has_side_effects=True
    )


def expected(microseconds):
    return pl.CostEstimate(
        flops=int(microseconds * RATE), bytes_accessed=0, transcendentals=0
    )


def estimate(rows, depth, columns):
    return expected(1.5 + rows * depth * columns * 2 / 7.2e8)


def resident(shape):
    return pl.BlockSpec(shape, lambda *place: (0,) * len(shape))


def arrange_kernel(lefts, blocks, grid, normed, *refs):
    pieces, rest = refs[:lefts], refs[lefts:-3]
    got, send_sem, recv_sem = refs[-3:]
    out_ref, own_ref = rest[-2:]
    step = pl.program_id(0)
    rows, width = pieces[0].shape
    wide = width // blocks
    outer, inner = grid
    me = lax.axis_index("seq")
    mine_a, mine_b = me // inner, lax.rem(me, inner)

    def copy(n):
        return core_copy(pieces[n], got.at[n], send_sem.at[n], recv_sem.at[n])

    @pl.when(step == 0)
    def _():
        greet([other_core()])
        for n in range(lefts):
            copy(n).start()

    def fill(p, load):
        if normed:
            value = load(slice(None)).astype(f32)
            mean = jnp.mean(value, axis=-1, keepdims=True)
            center = value - mean
            scale = lax.rsqrt(jnp.mean(center * center, axis=-1, keepdims=True) + norm_eps)
        for b in range(blocks):
            place = lax.rem(mine_a - b % outer + outer, outer) * inner
            place = place + lax.rem(mine_b - b // outer + inner, inner)
            here = slice(b * wide, (b + 1) * wide)
            part = load(pl.ds(pl.multiple_of(place * wide, wide), wide))
            if p == 0:
                own_ref[:, here] = part
            part = part.astype(f32)
            if normed:
                part = (part - mean) * scale * rest[0][:, here] + rest[1][:, here]
            else:
                part = part * rest[0][...]
            out_ref[:, here] = part.astype(bf16)

    for n in range(lefts):

        @pl.when(step == n)
        def _(n=n):
            fill(n, lambda columns: pieces[n][:, columns])

        @pl.when(step == lefts + n)
        def _(n=n):
            copy(n).wait()
            fill(lefts + n, lambda columns: got[n, :, columns])


def arrange(pieces, extras, extra_specs, normed, number, name):
    rows, width = pieces[0].shape
    lefts = len(pieces)
    return pl.pallas_call(
        functools.partial(arrange_kernel, lefts, lax.axis_size("seq"), seq_grid(), normed),
        out_shape=[
            jax.ShapeDtypeStruct((2 * lefts * rows, width), bf16),
            jax.ShapeDtypeStruct((rows, width), bf16),
        ],
        grid=(2 * lefts,),
        in_specs=[resident((rows, width))] * lefts + extra_specs,
        out_specs=[pl.BlockSpec((rows, width), lambda n: (n, 0)), resident((rows, width))],
        scratch_shapes=[
            pltpu.VMEM((lefts, rows, width), bf16),
            pltpu.SemaphoreType.DMA((lefts,)),
            pltpu.SemaphoreType.DMA((lefts,)),
        ],
        compiler_params=kernel_params(number),
        cost_estimate=expected(9.0),
        name=name,
    )(*pieces, *extras)


def tall_kernel(epilogue, exchanged, lefts, blocks, extras, *refs):
    weight = jnp.concatenate([ref[...] for ref in refs[lefts : lefts + blocks]], axis=0)
    rest = refs[lefts + blocks :]
    step = pl.program_id(0)
    rows = refs[0].shape[0]
    if exchanged:
        others_ref, got, send_sem, recv_sem = rest[-4:]
        rest = rest[:-4]

        def copy(n):
            return core_copy(refs[n], got.at[n], send_sem.at[n], recv_sem.at[n])

        @pl.when(step == 0)
        def _():
            greet([other_core()])
            for n in range(lefts):
                copy(n).start()

    def fill(left, at):
        result = jnp.dot(left, weight, preferred_element_type=f32)
        epilogue(result, slice(at, at + rows), rest[:extras], rest[extras:])

    for n in range(lefts):
        fill(refs[n][...], n * rows)
    if exchanged:

        @pl.when(step == 0)
        def _():
            for n in range(lefts):
                copy(n).wait()

        for n in range(lefts):
            fill(got[n], (lefts + n) * rows)

        @pl.when(step == pl.num_programs(0) - 1)
        def _():
            for n in range(lefts):
                others_ref[n * rows : (n + 1) * rows, :] = got[n]


def tall_dot(lefts, blocks, start, width, epilogue, extras, outs, name, number=None):
    rows, depth = lefts[0].shape
    exchanged = number is not None
    count = len(lefts) * (2 if exchanged else 1)
    tile = max(size for size in (128, 256, 512) if width % size == 0 and start % size == 0)
    first = start // tile
    specs = [pl.BlockSpec((high, tile), lambda n: (0, first + n)) for _, high in blocks]
    blocks = [block for block, _ in blocks]
    out_shape = [jax.ShapeDtypeStruct((height, width), dtype) for height, dtype in outs]
    out_specs = [pl.BlockSpec((height, tile), lambda n: (0, n)) for height, _ in outs]
    scratch = []
    params = pltpu.CompilerParams(vmem_limit_bytes=56 * 2**20)
    if exchanged:
        out_shape.append(jax.ShapeDtypeStruct((len(lefts) * rows, depth), bf16))
        out_specs.append(resident((len(lefts) * rows, depth)))
        scratch = [
            pltpu.VMEM((len(lefts), rows, depth), bf16),
            pltpu.SemaphoreType.DMA((len(lefts),)),
            pltpu.SemaphoreType.DMA((len(lefts),)),
        ]
        params = kernel_params(number)
    return pl.pallas_call(
        functools.partial(
            tall_kernel, epilogue, exchanged, len(lefts), len(blocks), len(extras)
        ),
        out_shape=out_shape,
        grid=(width // tile,),
        in_specs=[resident(left.shape) for left in lefts]
        + specs
        + [pl.BlockSpec((extra.shape[0], tile), lambda n: (0, n)) for extra in extras],
        out_specs=out_specs,
        scratch_shapes=scratch,
        compiler_params=params,
        cost_estimate=estimate(rows * count, depth, width),
        name=name,
    )(*lefts, *blocks, *extras)


def plain_epilogue(result, here, extras, outs):
    outs[0][here, :] = result.astype(bf16)


def project_epilogue(result, here, extras, outs):
    bias, scale = extras
    outs[0][here, :] = ((result + bias[...]).astype(bf16).astype(f32) * scale[...]).astype(bf16)


def up_epilogue(result, here, extras, outs):
    value, slope = gelu_both(result + extras[0][...])
    outs[0][here, :] = value.astype(bf16)
    outs[1][here, :] = slope.astype(bf16)


def slope_epilogue(result, here, extras, outs):
    grad = (result * extras[0][here, :].astype(f32)).astype(bf16)
    outs[0][here, :] = grad
    sums = jnp.sum(grad.astype(f32), axis=0, keepdims=True)
    outs[1][...] = jnp.broadcast_to(sums, outs[1].shape)


def wide_kernel(blocks, start, left_ref, *refs):
    first_ref, second_ref, sent, got, send_sem, recv_sem = refs[blocks:]
    step = pl.program_id(0)
    columns = slice(start, start + left_ref.shape[1])

    def copy(n):
        return core_copy(sent.at[n], got.at[n], send_sem.at[n], recv_sem.at[n])

    @pl.when(step == 0)
    def _():
        greet([other_core()])

    result = lax.dot_general(
        left_ref[...],
        jnp.concatenate([ref[:, columns] for ref in refs[:blocks]], axis=0),
        (((1,), (1,)), ((), ())),
        preferred_element_type=f32,
    )
    for n in range(2):

        @pl.when(step == n)
        def _(n=n):
            sent[n] = result.astype(bf16)
            copy(n).start()

    @pl.when(step == 2)
    def _():
        copy(0).wait()
        second_ref[...] = (result + got[0].astype(f32)).astype(bf16)

    @pl.when(step == 3)
    def _():
        copy(1).wait()
        first_ref[...] = result + got[1].astype(f32)


def wide_dot(left, blocks, start, features, number, name, weight=1.0):
    rows, width = left.shape
    tile = rows // 4
    specs = [resident((high, block.shape[1])) for block, high in blocks]
    blocks = [block for block, _ in blocks]
    return pl.pallas_call(
        functools.partial(wide_kernel, len(blocks), start),
        out_shape=[
            jax.ShapeDtypeStruct((tile, features), f32),
            jax.ShapeDtypeStruct((tile, features), bf16),
        ],
        grid=(4,),
        in_specs=[pl.BlockSpec((tile, width), lambda n: (3 - n, 0))] + specs,
        out_specs=[resident((tile, features)), resident((tile, features))],
        scratch_shapes=[
            pltpu.VMEM((2, tile, features), bf16),
            pltpu.VMEM((2, tile, features), bf16),
            pltpu.SemaphoreType.DMA((2,)),
            pltpu.SemaphoreType.DMA((2,)),
        ],
        compiler_params=kernel_params(number),
        cost_estimate=estimate(rows, width * weight, features),
        name=name,
    )(left, *blocks)


def turned_kernel(shapes, sizes, *refs):
    refs = list(refs)
    groups = [[refs.pop(0) for _ in range(count)] for count in shapes]
    rights = [refs.pop(0) for _ in shapes]

    def fill(out_ref, here):
        at = 0
        for lefts, right_ref in zip(groups, rights):
            width = right_ref.shape[1]
            left = jnp.concatenate([ref[...] for ref in lefts], axis=0)
            out_ref[here, at : at + width] = lax.dot_general(
                left, right_ref[...], (((0,), (0,)), ((), ())), preferred_element_type=f32
            ).astype(bf16)
            at += width

    if sizes is None:
        fill(refs[0], slice(None))
    else:
        step = 0
        for size, out_ref in zip(sizes, refs):
            depth = out_ref.shape[0] // size
            for n in range(size):
                here = slice(n * depth, (n + 1) * depth)
                pl.when(pl.program_id(0) == step)(functools.partial(fill, out_ref, here))
                step += 1


def turned_dot(pairs, first, count, depth, name, sizes=None):
    width = sum(right.shape[1] for _, right in pairs)
    rows = pairs[0][1].shape[0]
    if sizes is None:
        out_shape = [jax.ShapeDtypeStruct((count * depth, width), bf16)]
        out_specs = [pl.BlockSpec((depth, width), lambda n: (n, 0))]
    else:
        out_shape = [jax.ShapeDtypeStruct((size * depth, width), bf16) for size in sizes]
        out_specs = [resident((size * depth, width)) for size in sizes]
    return pl.pallas_call(
        functools.partial(turned_kernel, [len(lefts) for lefts, _ in pairs], sizes),
        out_shape=out_shape,
        grid=(count,),
        in_specs=[
            pl.BlockSpec((left.shape[0], depth), lambda n: (0, first + n))
            for lefts, _ in pairs
            for left in lefts
        ]
        + [resident(right.shape) for _, right in pairs],
        out_specs=out_specs,
        compiler_params=pltpu.CompilerParams(vmem_limit_bytes=56 * 2**20),
        cost_estimate=estimate(rows, count * depth, width),
        name=name,
    )(*[left for lefts, _ in pairs for left in lefts], *[right for _, right in pairs])


def far_grads(pairs, depth, name, sizes):
    outer, inner = seq_grid()
    return [
        turned_dot(pairs, j * outer, outer, depth, name + "_far", sizes) for j in range(1, inner)
    ]


def near_grads(pairs, depth, name):
    return turned_dot(pairs, 0, seq_grid()[0], depth, name + "_near")[0]


def inner_sum(far, n, *ready):
    part = shift_inner(after(far[-1][n], *ready), -1)
    for parts in reversed(far[:-1]):
        part = shift_inner((parts[n].astype(f32) + part.astype(f32)).astype(bf16), -1)
    return part


def single_blocks(groups, depth):
    return [
        group[n * depth : (n + 1) * depth]
        for group in groups
        for n in range(group.shape[0] // depth)
    ]


def from_blocks_kernel(blocks, order_ref, in_ref, out_ref):
    rows, width = out_ref.shape
    wide = width // blocks
    for b in range(blocks):
        there = pl.ds(pl.multiple_of(order_ref[b] * wide, wide), wide)
        out_ref[:, there] = in_ref[:rows, b * wide : (b + 1) * wide].astype(out_ref.dtype)


def from_blocks(value, order, rows):
    rows_padded, width = value.shape
    return pl.pallas_call(
        functools.partial(from_blocks_kernel, order.shape[0]),
        out_shape=jax.ShapeDtypeStruct((rows, width), bf16),
        in_specs=[
            pl.BlockSpec(memory_space=pltpu.SMEM),
            pl.BlockSpec(memory_space=pltpu.VMEM),
        ],
        out_specs=pl.BlockSpec(memory_space=pltpu.VMEM),
        compiler_params=pltpu.CompilerParams(vmem_limit_bytes=12 * 2**20),
        cost_estimate=expected(3.0),
        name="from_blocks",
    )(order, value)


def segment_starts(me, mp_count, rows_padded):
    group = mp_count // NSEG
    starts = []
    for s in range(NSEG):
        pieces = []
        for r in range(group):
            code = jnp.bitwise_xor(me, s * group + r)
            place = jnp.bitwise_and(code, 1) * (mp_count // 2) + lax.shift_right_logical(code, 1)
            pieces.append(pl.multiple_of(place * rows_padded, rows_padded))
        starts.append(pieces)
    return starts


def load_segment(ref, pieces, rows_padded):
    parts = [ref[pl.ds(start, rows_padded), :] for start in pieces]
    return parts[0] if len(parts) == 1 else jnp.concatenate(parts, axis=0)


def load_slab(ref, pieces, rows_padded):
    return ref[pl.ds(pl.multiple_of(pieces[-1] + (rows_padded - SLAB), 16), SLAB), :]


def store_segment(ref, pieces, rows_padded, value):
    for r, start in enumerate(pieces):
        ref[pl.ds(start, rows_padded), :] = value[r * rows_padded : (r + 1) * rows_padded]


def lane_halves(shape):
    lane = lax.broadcasted_iota(jnp.int32, shape, 1)
    return lane < HEAD_DIM


def attend_kernel(mp_count, rows_padded, me_ref, q_ref, k_ref, v_ref, bias_ref, o_ref, p_ref):
    starts = segment_starts(me_ref[0], mp_count, rows_padded)
    for s in range(NSEG):
        keys = jnp.concatenate(
            [load_slab(k_ref, starts[e], rows_padded) for e in range(s)]
            + [load_segment(k_ref, starts[s], rows_padded)],
            axis=0,
        )
        values = jnp.concatenate(
            [load_slab(v_ref, starts[e], rows_padded) for e in range(s)]
            + [load_segment(v_ref, starts[s], rows_padded)],
            axis=0,
        )
        queries = load_segment(q_ref, starts[s], rows_padded)
        first_head = lane_halves(queries.shape)
        zero = jnp.zeros_like(queries)
        head_queries = (jnp.where(first_head, queries, zero), jnp.where(first_head, zero, queries))
        units = [(low, high, h) for low, high in query_blocks for h in range(2)]
        scores = [
            lax.dot_general(
                head_queries[h][low:high],
                keys[: SLAB * s + high],
                (((1,), (1,)), ((), ())),
                preferred_element_type=f32,
            )
            + bias_ref[s, low:high, : SLAB * s + high]
            for low, high, h in units
        ]
        shares = []
        for (low, high, h), score in zip(units, scores):
            raised = jnp.exp(score - jnp.max(score, axis=-1, keepdims=True))
            share = raised * (1.0 / jnp.sum(raised, axis=-1, keepdims=True))
            shares.append(share.astype(bf16))
            p_ref[h, s * SEG_PAD + low : s * SEG_PAD + high, : SLAB * s + high] = shares[-1]
        both = [
            jnp.dot(share, values[: SLAB * s + high], preferred_element_type=f32)
            for (low, high, h), share in zip(units, shares)
        ]
        outs = [
            jnp.where(first_head[low:high], both[2 * n], both[2 * n + 1])
            for n, (low, high) in enumerate(query_blocks)
        ]
        out = jnp.concatenate(outs, axis=0).astype(bf16)
        store_segment(o_ref, starts[s], rows_padded, out)


def attend(qkv, bias, me, mp_count, rows_padded):
    rows, width = qkv.shape
    pairs = width // 3 // 128
    return pl.pallas_call(
        functools.partial(attend_kernel, mp_count, rows_padded),
        out_shape=(
            jax.ShapeDtypeStruct((rows, width // 3), bf16),
            jax.ShapeDtypeStruct((pairs * 2, rows, KEYS), bf16),
        ),
        grid_spec=pltpu.PrefetchScalarGridSpec(
            num_scalar_prefetch=1,
            grid=(pairs,),
            in_specs=[
                pl.BlockSpec((rows, 128), lambda n, me_ref: (0, n)),
                pl.BlockSpec((rows, 128), lambda n, me_ref: (0, pairs + n)),
                pl.BlockSpec((rows, 128), lambda n, me_ref: (0, 2 * pairs + n)),
                pl.BlockSpec(bias.shape, lambda n, me_ref: (0, 0, 0)),
            ],
            out_specs=(
                pl.BlockSpec((rows, 128), lambda n, me_ref: (0, n)),
                pl.BlockSpec((2, rows, KEYS), lambda n, me_ref: (n, 0, 0)),
            ),
        ),
        compiler_params=pltpu.CompilerParams(vmem_limit_bytes=48 * 2**20),
        cost_estimate=expected(12.0),
        name="attend",
    )(me, qkv, qkv, qkv, bias)


def attend_back_kernel(
    mp_count,
    rows_padded,
    me_ref,
    q_ref,
    k_ref,
    v_ref,
    o_ref,
    g_ref,
    p_ref,
    dq_ref,
    dk_ref,
    dv_ref,
    key_sum,
    value_sum,
):
    starts = segment_starts(me_ref[0], mp_count, rows_padded)
    key_sum[...] = jnp.zeros_like(key_sum)
    value_sum[...] = jnp.zeros_like(value_sum)
    for s in range(NSEG):
        keys = jnp.concatenate(
            [load_slab(k_ref, starts[e], rows_padded) for e in range(s)]
            + [load_segment(k_ref, starts[s], rows_padded)],
            axis=0,
        )
        values = jnp.concatenate(
            [load_slab(v_ref, starts[e], rows_padded) for e in range(s)]
            + [load_segment(v_ref, starts[s], rows_padded)],
            axis=0,
        )
        queries = load_segment(q_ref, starts[s], rows_padded)
        grads = load_segment(g_ref, starts[s], rows_padded)
        outs = load_segment(o_ref, starts[s], rows_padded)
        queries_turned = queries.astype(f32).T.astype(bf16)
        grads_turned = grads.astype(f32).T.astype(bf16)
        first_head = lane_halves(queries.shape)
        zero = jnp.zeros_like(queries)
        head_grads = (jnp.where(first_head, grads, zero), jnp.where(first_head, zero, grads))
        product = grads.astype(f32) * outs.astype(f32)
        head_deltas = (
            jnp.sum(jnp.where(first_head, product, 0.0), axis=-1, keepdims=True),
            jnp.sum(jnp.where(first_head, 0.0, product), axis=-1, keepdims=True),
        )
        units = [(low, high, h) for low, high in query_blocks for h in range(2)]
        shares = [
            p_ref[h, s * SEG_PAD + low : s * SEG_PAD + high, : SLAB * s + high]
            for low, high, h in units
        ]
        share_grads = [
            lax.dot_general(
                head_grads[h][low:high],
                values[: SLAB * s + high],
                (((1,), (1,)), ((), ())),
                preferred_element_type=f32,
            )
            for low, high, h in units
        ]
        score_grads = [
            (share.astype(f32) * (share_grad - head_deltas[h][low:high])).astype(bf16)
            for (low, high, h), share, share_grad in zip(units, shares, share_grads)
        ]
        both = [
            jnp.dot(score_grad, keys[: SLAB * s + high], preferred_element_type=f32)
            for (low, high, h), score_grad in zip(units, score_grads)
        ]
        query_grads = [
            jnp.where(first_head[low:high], both[2 * n], both[2 * n + 1])
            for n, (low, high) in enumerate(query_blocks)
        ]
        for (low, high, h), share, score_grad in zip(units, shares, score_grads):
            lanes = slice(h * HEAD_DIM, (h + 1) * HEAD_DIM)
            value_part = jnp.dot(grads_turned[lanes, low:high], share, preferred_element_type=f32)
            key_part = jnp.dot(
                queries_turned[lanes, low:high], score_grad, preferred_element_type=f32
            )
            for e in range(s):
                place = slice((e + 1) * SEG_PAD - SLAB, (e + 1) * SEG_PAD)
                value_sum[lanes, place] += value_part[:, e * SLAB : (e + 1) * SLAB]
                key_sum[lanes, place] += key_part[:, e * SLAB : (e + 1) * SLAB]
            place = slice(s * SEG_PAD, s * SEG_PAD + high)
            value_sum[lanes, place] += value_part[:, s * SLAB :]
            key_sum[lanes, place] += key_part[:, s * SLAB :]
        query_grad = (jnp.concatenate(query_grads, axis=0) * score_scale).astype(bf16)
        store_segment(dq_ref, starts[s], rows_padded, query_grad)
    key_all = key_sum[...].T.astype(bf16)
    value_all = value_sum[...].T.astype(bf16)
    for s in range(NSEG):
        place = slice(s * SEG_PAD, (s + 1) * SEG_PAD)
        store_segment(dk_ref, starts[s], rows_padded, key_all[place])
        store_segment(dv_ref, starts[s], rows_padded, value_all[place])


def attend_back(qkv, out, grad, share, me, mp_count, rows_padded):
    rows, width = qkv.shape
    pairs = width // 3 // 128
    column = pl.BlockSpec((rows, 128), lambda n, me_ref: (0, n))
    piece = jax.ShapeDtypeStruct((rows, width // 3), bf16)
    return pl.pallas_call(
        functools.partial(attend_back_kernel, mp_count, rows_padded),
        out_shape=(piece, piece, piece),
        grid_spec=pltpu.PrefetchScalarGridSpec(
            num_scalar_prefetch=1,
            grid=(pairs,),
            in_specs=[
                column,
                pl.BlockSpec((rows, 128), lambda n, me_ref: (0, pairs + n)),
                pl.BlockSpec((rows, 128), lambda n, me_ref: (0, 2 * pairs + n)),
                column,
                column,
                pl.BlockSpec((2, rows, KEYS), lambda n, me_ref: (n, 0, 0)),
            ],
            out_specs=(column, column, column),
            scratch_shapes=[pltpu.VMEM((128, rows), f32), pltpu.VMEM((128, rows), f32)],
        ),
        compiler_params=pltpu.CompilerParams(vmem_limit_bytes=48 * 2**20),
        cost_estimate=expected(12.5),
        name="attend_back",
    )(me, qkv, qkv, qkv, out, grad, share)


def item_rows(present, summary, parts, rows, rows_padded):
    kept = present[:, None] * jnp.concatenate([jnp.ones((NSEG, SEG), jnp.int32), summary], axis=1)
    group = parts // NSEG
    kept = jnp.pad(kept.reshape(NSEG, group, rows), ((0, 0), (0, 0), (0, rows_padded - rows)))
    flags = np.zeros((group, rows_padded), np.int32)
    flags[:, :rows] = (np.arange(PERIOD) >= SEG).reshape(group, rows)
    return kept.reshape(NSEG, group * rows_padded), flags.reshape(group * rows_padded)


def score_bias(kept, flags):
    slab = (kept * flags[None, :])[:, SEG_PAD - SLAB :] == 1
    causal = np.tril(np.ones((SEG_PAD, SEG_PAD), bool))
    itself = np.eye(SEG_PAD, dtype=bool)
    planes = []
    for s in range(NSEG):
        own = (kept[s][None, :] == 1) & causal | itself
        pieces = [jnp.broadcast_to(slab[e][None, :], (SEG_PAD, SLAB)) for e in range(s)] + [own]
        seen = jnp.concatenate(pieces, axis=1)
        planes.append(jnp.pad(seen, ((0, 0), (0, KEYS - seen.shape[1]))))
    return jnp.where(jnp.stack(planes), 0.0, -1e30).astype(f32)


def norm_parts(value):
    center = value - jnp.mean(value, axis=-1, keepdims=True)
    spread = jnp.mean(center * center, axis=-1, keepdims=True)
    scale = lax.rsqrt(spread + norm_eps)
    return center * scale, scale


def norm_back(normed, scale, gain, grad):
    inner = grad * gain
    return scale * (
        inner
        - jnp.mean(inner, axis=-1, keepdims=True)
        - normed * jnp.mean(inner * normed, axis=-1, keepdims=True)
    )


def gelu_both(value):
    c = 0.7978845608028654
    square = value * value
    bend = jnp.tanh(c * (value + 0.044715 * value * square))
    half = 0.5 * (1.0 + bend)
    slope = half + 0.5 * value * (1.0 - bend * bend) * c * (1.0 + 3.0 * 0.044715 * square)
    return value * half, slope


def adam_step(master, grad, first, second, average, factor, rate, decay):
    clipped = grad * factor
    first_new = beta_first * first + (1.0 - beta_first) * clipped
    second_new = beta_second * second + (1.0 - beta_second) * clipped * clipped
    first_hat = first_new * (1.0 / (1.0 - beta_first**STEP))
    second_hat = second_new * (1.0 / (1.0 - beta_second**STEP))
    master_new = master - rate * (first_hat / (jnp.sqrt(second_hat) + adam_eps) + decay * master)
    average_new = average_keep * average + (1.0 - average_keep) * master_new
    return (master_new, first_new, second_new, average_new, master_new.astype(bf16))


def vector_kernel(square_ref, *refs):
    vector_refs, state, outs = refs[:3], refs[3:15], refs[15:]
    grad_norm = jnp.sqrt(jnp.sum(square_ref[...], keepdims=True))
    factor = jnp.minimum(1.0, clip_limit / (grad_norm + 1e-06))
    for n in range(3):
        old = [ref[...] for ref in state[4 * n : 4 * n + 4]]
        new = adam_step(old[0], vector_refs[n][...], *old[1:], factor, vector_rate, 0.0)
        for ref, value in zip(outs[5 * n : 5 * n + 5], new):
            ref[...] = value


def adam_vectors(squares, vectors, state):
    vmem = pl.BlockSpec(memory_space=pltpu.VMEM)
    out_shape = []
    for n in range(3):
        group = state[4 * n : 4 * n + 4]
        out_shape += [jax.ShapeDtypeStruct(array.shape, f32) for array in group]
        out_shape.append(jax.ShapeDtypeStruct(group[0].shape, bf16))
    return pl.pallas_call(
        vector_kernel,
        out_shape=out_shape,
        in_specs=[vmem] * (1 + len(vectors) + len(state)),
        out_specs=[vmem] * len(out_shape),
        compiler_params=pltpu.CompilerParams(vmem_limit_bytes=4 * 2**20),
        cost_estimate=expected(3.0),
        name="adam_vectors",
    )(squares, *vectors, *state)


def per_device(
    tokens,
    cotangent,
    present,
    summary_mask,
    attention_weight,
    attention_first,
    attention_second,
    attention_average,
    hidden_weight,
    hidden_first,
    hidden_second,
    hidden_average,
    norm_params,
    norm_first,
    norm_second,
    norm_average,
    head_bias,
    head_first,
    head_second,
    head_average,
    unit_bias,
    unit_first,
    unit_second,
    unit_average,
):
    outer, inner = seq_grid()
    seqs = outer * inner
    parts = lax.axis_size("mp")
    rows = tokens.shape[0]
    rows_padded = SEG_PAD * NSEG // parts
    head_width = attention_weight.shape[2]
    depth = attention_weight.shape[1]
    me = lax.axis_index("mp")
    me_vector = me.astype(jnp.int32)[None]
    order = feature_order()
    back_order = block_order()
    codes = row_codes()
    units = hidden_weight.shape[2]
    total_rows = parts * rows_padded

    norm_size, head_size = norm_params.size, head_bias.size
    packed = jnp.concatenate([norm_params.reshape(-1), head_bias.reshape(-1), unit_bias])
    packed_size = packed.size
    packed_width = 4 * head_width
    packed = jnp.pad(packed, (0, 16 * packed_width - packed_size)).reshape(16, packed_width)
    attn_own = jnp.concatenate(
        [jnp.concatenate([attention_weight[n] for n in range(4)], axis=1), packed], axis=0
    ).astype(bf16)
    row_pad = ((0, rows_padded - rows), (0, 0))
    tokens_all = gather_chips(jnp.pad(tokens, row_pad))
    cotangent_pieces = gather_chips(after(jnp.pad(cotangent, row_pad), *tokens_all))
    up_own, down_own = hidden_weight[0].astype(bf16), hidden_weight[1].astype(bf16)
    attn_line, attn_rest = [attn_own], [ring_rest(attn_own)]
    for i in range(1, outer):
        behind = attn_rest[i - 2] if i > 1 else []
        behind = behind + (tokens_all[1:] if i == outer - 1 else [])
        attn_line.append(shift_outer(after(attn_line[-1], *behind), 1))
        if i < outer - 1:
            attn_rest.append(ring_rest(attn_line[-1]))
    attn_end = ring_end(attn_line[3], attn_rest[2], [])
    attn_ends = [part for parts in attn_end for part in parts]
    attn_blocks, vectors, at = [], [], 0
    for piece, high in stack_ring(attn_line, attn_rest, attn_end):
        used = min(high, depth - at % depth)
        if high > used:
            vectors.append(piece[used : used + 1, :packed_size])
        attn_blocks.append((piece, used))
        at += used
    up_line = [up_own, shift_outer(after(up_own, attn_ends[-1]), 1)]
    up_line.append(shift_outer(up_line[1], 1))
    up_line.append(shift_outer(up_line[2], 1))
    up_rest = [ring_rest(after(up_own, attn_ends[0]))]
    up_rest.append(ring_rest(after(up_line[1], *up_rest[0])))

    vectors = jnp.concatenate(vectors, axis=0).astype(f32)
    norm_vals = vectors[:, :norm_size].reshape(seqs, 6, depth).transpose(1, 0, 2).reshape(6, D)
    vectors = jnp.take(vectors[:, norm_size:], back_order, axis=0)
    head_vals = vectors[:, :head_size].reshape(seqs, 2, head_width // seqs)
    head_vals = head_vals.transpose(1, 0, 2).reshape(2, head_width)
    unit_vals = vectors[:, head_size:].reshape(-1)

    kept, flags = item_rows(present[0], summary_mask[0], parts, rows, rows_padded)
    bias = score_bias(kept, flags)
    kept_parts = kept.reshape(parts, rows_padded).astype(f32)
    kept_all = jnp.take(kept_parts, jnp.stack([me ^ code for code in codes]), axis=0).reshape(-1, 1)
    kept_own = kept_all[:rows_padded]

    first_all, inputs_own = arrange(
        tokens_all,
        [norm_vals[0:1], norm_vals[1:2]],
        [resident((1, D))] * 2,
        True,
        2,
        "first_norm",
    )
    qkv_bias = jnp.concatenate([head_vals[0], jnp.zeros_like(head_vals[0]), head_vals[1]])
    qkv_scale = np.concatenate(
        [np.full(head_width, score_scale, np.float32), np.ones(2 * head_width, np.float32)]
    )
    qkv = tall_dot(
        [after(first_all, *cotangent_pieces)],
        attn_blocks,
        0,
        3 * head_width,
        project_epilogue,
        [qkv_bias[None], qkv_scale[None]],
        [(total_rows, bf16)],
        "project",
    )[0]
    down_rest = []
    down_line = [down_own, shift_outer(after(down_own, qkv), 1)]
    qkv = after(qkv, up_line[1])
    context, share = attend(qkv, bias, me_vector, parts, rows_padded)
    up_rest.append(ring_rest(after(up_line[2], context, *up_rest[1])))
    up_end = ring_end(up_line[3], up_rest[2], up_rest[2])
    up_ends = [part for parts in up_end for part in parts]
    down_line.append(shift_outer(after(down_line[1], up_ends[-1]), 1))
    down_line.append(shift_outer(down_line[2], 1))
    up_blocks = stack_ring(up_line, up_rest, up_end)
    context = after(context, up_line[2], *up_rest[0])
    join_parts = wide_dot(context, attn_blocks, 3 * head_width, D, 4, "join")
    down_rest.append(ring_rest(after(down_own, *up_rest[2])))
    down_rest.append(ring_rest(after(down_line[1], up_ends[0])))
    join_parts = [join_parts[0], after(join_parts[1], down_line[1], *up_rest[1])]
    attended = scatter_chips(*join_parts) + norm_vals[4]
    attended = after(attended, up_line[3], *down_rest[0])
    feed_grad, cotangent_own = arrange(
        cotangent_pieces,
        [kept_all],
        [pl.BlockSpec((rows_padded, 1), lambda n: (n, 0))],
        False,
        3,
        "feed_grad",
    )
    inputs = inputs_own.astype(f32)
    middle = inputs + kept_own * attended

    normed_two, scale_two = norm_parts(middle)
    second_own = (normed_two * norm_vals[2] + norm_vals[3]).astype(bf16)
    second_all = gather_chips(second_own)
    down_rest.append(ring_rest(after(down_line[2], second_all[1])))
    second_all = after(second_all, feed_grad, down_line[2], *down_rest[1])
    activated, slope, second_others = tall_dot(
        second_all,
        up_blocks,
        0,
        units,
        up_epilogue,
        [unit_vals[None]],
        [(total_rows, bf16), (total_rows, bf16)],
        "up",
        5,
    )
    second_all = second_all + [second_others]

    out_grad = cotangent_own.astype(f32)
    down_bias_grad = jnp.sum(kept_own * out_grad, axis=0)

    down_end = ring_end(down_line[3], down_rest[2], [activated, *down_rest[1]], [activated])
    down_ends = [part for parts in down_end for part in parts]
    down_blocks = stack_ring(down_line, down_rest, down_end)
    activated = after(activated, down_line[3], *down_rest[2])
    down_pairs = [([feed_grad], activated)]
    down_far = far_grads(down_pairs, depth, "down_grad", (3, 1))
    down_last = inner_sum(down_far, 1, *down_ends)
    pre_grad, unit_grad = tall_dot(
        [feed_grad],
        down_blocks,
        0,
        units,
        slope_epilogue,
        [slope],
        [(total_rows, bf16), (8, f32)],
        "down_back",
    )
    unit_grad = unit_grad[0]
    down_first = inner_sum(down_far, 0, pre_grad)
    down_near = near_grads([([after(feed_grad, pre_grad)], activated)], depth, "down_grad")
    down_blocks_in = single_blocks([down_first, down_last], depth)
    down_totals = ring_scatter(down_near, down_blocks_in)[0][:-1]
    pre_grad = after(pre_grad, down_last, down_near)
    second_parts = wide_dot(pre_grad, up_blocks, 0, D, 6, "up_back")
    up_pairs = [(after(second_all, *second_parts), pre_grad)]
    up_far = far_grads(up_pairs, depth, "up_grad", (2, 1, 1))
    up_near = near_grads(up_pairs, depth, "up_grad")
    second_grad = after(scatter_chips(*second_parts), up_near, *[far[2] for far in up_far])
    gain_two_grad = jnp.sum(second_grad * normed_two, axis=0)
    shift_two_grad = jnp.sum(second_grad, axis=0)
    middle_grad = out_grad + norm_back(normed_two, scale_two, norm_vals[2], second_grad)

    attn_grad = kept_own * middle_grad
    out_bias_grad = jnp.sum(attn_grad, axis=0)
    up_last = inner_sum(up_far, 2, second_grad)
    feed_parts = wide_dot(after(activated, second_grad), down_blocks, 0, D, 8, "down")
    attn_rows = after(gather_chips(attn_grad.astype(bf16)), down_first, up_last, *feed_parts)
    context_grad, attn_others = tall_dot(
        attn_rows,
        attn_blocks,
        3 * head_width,
        head_width,
        plain_epilogue,
        [],
        [(total_rows, bf16)],
        "join_back",
        7,
    )
    attn_rows = attn_rows + [attn_others]
    up_middle = inner_sum(up_far, 1, down_first)
    up_first = inner_sum(up_far, 0, up_last, context_grad)
    context_grad = after(context_grad, down_totals[2])
    query_grad, key_grad, value_grad = attend_back(
        qkv, context, context_grad, share, me_vector, parts, rows_padded
    )
    qkv_grad = jnp.concatenate([query_grad, key_grad, value_grad], axis=1)
    head_grad = jnp.stack(
        [jnp.sum(query_grad, axis=0, dtype=f32), jnp.sum(value_grad, axis=0, dtype=f32)]
    )
    up_totals, up_hop = ring_scatter(up_near, single_blocks([up_first, up_middle, up_last], depth))
    up_grad = up_totals[-1]
    attn_pairs = [
        ([after(first_all, up_totals[1])], qkv_grad),
        (attn_rows, context),
    ]
    attn_far = far_grads(attn_pairs, depth, "attn_grad", (1, 1, 1, 1))
    all_far = [part for far in attn_far for part in far]
    first_parts = wide_dot(after(qkv_grad, *all_far), attn_blocks, 0, D, 9, "project_back")
    attn_pairs = [
        ([after(first_all, up_totals[2], *first_parts)], qkv_grad),
        (attn_rows, context),
    ]
    attn_near = near_grads(attn_pairs, depth, "attn_grad")
    attn_sums = [None] * outer
    attn_sums[3] = inner_sum(attn_far, 3, up_middle)
    attn_sums[2] = inner_sum(attn_far, 2, up_first)
    attn_total = attn_near[3 * depth :].astype(f32) + attn_sums[3].astype(f32)
    attn_total = attn_total.astype(bf16)
    attn_sums[1] = inner_sum(attn_far, 1, attn_total, up_hop)
    attn_sums[0] = inner_sum(attn_far, 0, attn_sums[2])
    attn_totals, _ = ring_scatter(attn_near, attn_sums, [up_hop], [attn_total])
    down_grad = ring_scatter(down_near, down_blocks_in, (), down_totals, [attn_total])[0][-1]
    feed_out = scatter_chips(*after(feed_parts, attn_total)) + norm_vals[5]
    block_output = from_blocks(middle + kept_own * feed_out, order, rows)
    first_grad = scatter_chips(*first_parts)
    normed_one, scale_one = norm_parts(inputs)
    gain_one_grad = jnp.sum(first_grad * normed_one, axis=0)
    shift_one_grad = jnp.sum(first_grad, axis=0)
    input_grad = from_blocks(
        middle_grad + norm_back(normed_one, scale_one, norm_vals[0], first_grad), order, rows
    )

    vector_grad = jnp.stack(
        [
            gain_one_grad,
            shift_one_grad,
            gain_two_grad,
            shift_two_grad,
            out_bias_grad,
            down_bias_grad,
        ]
    )
    vector_grad = jnp.take(
        vector_grad.reshape(6, seqs, depth).transpose(1, 0, 2).reshape(seqs, -1), back_order, axis=0
    )
    norm_room = -(-norm_size // 1024) * 1024
    room = norm_room + -(-(packed_size - norm_size) // 1024) * 1024
    vectors = jnp.concatenate(
        [
            vector_grad,
            jnp.zeros((seqs, norm_room - norm_size), f32),
            head_grad.reshape(2, seqs, -1).transpose(1, 0, 2).reshape(seqs, -1),
            unit_grad.reshape(seqs, -1),
            jnp.zeros((seqs, room - norm_room - packed_size + norm_size), f32),
        ],
        axis=1,
    )
    vectors = vectors.reshape(seqs, room // 128, 128)
    attn_shard = attn_totals[-1]
    squares = sum(jnp.sum(shard * shard) for shard in (attn_shard, up_grad, down_grad))
    squares = jnp.pad(squares.reshape(1, 1), ((0, 7), (0, 127)))
    vectors, squares = reduce_all(vectors, squares, norm_room // 128)
    grad_norm = jnp.sqrt(jnp.sum(squares))
    vectors = vectors.reshape(-1)
    norm_shard = vectors[:norm_size].reshape(norm_params.shape)
    head_shard = vectors[norm_room : norm_room + head_size].reshape(head_bias.shape)
    unit_shard = vectors[norm_room + head_size : norm_room + packed_size - norm_size]
    factor = jnp.minimum(1.0, clip_limit / (grad_norm + 1e-06))
    hidden_rate = jnp.array([D ** (-0.5), FF ** (-0.5)], f32)[:, None, None]
    attn_shard = jnp.stack(
        [attn_shard[:, n * head_width : (n + 1) * head_width] for n in range(4)]
    )
    hidden_out = adam_step(
        hidden_weight,
        jnp.stack([up_grad, down_grad]),
        hidden_first,
        hidden_second,
        hidden_average,
        factor,
        hidden_rate,
        weight_decay,
    )
    attention_out = adam_step(
        attention_weight,
        attn_shard,
        attention_first,
        attention_second,
        attention_average,
        factor,
        D ** (-0.5),
        weight_decay,
    )
    updated = adam_vectors(
        squares,
        [norm_shard, head_shard, unit_shard[None]],
        [
            norm_params,
            norm_first,
            norm_second,
            norm_average,
            head_bias,
            head_first,
            head_second,
            head_average,
            unit_bias[None],
            unit_first[None],
            unit_second[None],
            unit_average[None],
        ],
    )
    return (
        block_output,
        input_grad,
        grad_norm,
        *attention_out,
        *hidden_out,
        *updated[:10],
        *[value[0] for value in updated[10:]],
    )


def solution(mesh):
    token_spec = P(("seq", "mp"), None)
    weight_spec = P(None, "seq", "mp")
    norm_spec = P(None, "seq")
    head_spec = P(None, ("mp", "seq"))
    unit_spec = P(("mp", "seq"))
    return jax.shard_map(
        per_device,
        mesh=mesh,
        in_specs=(
            token_spec,
            token_spec,
            P("seq", None),
            P("seq", None, None),
            *([weight_spec] * 8),
            *([norm_spec] * 4),
            *([head_spec] * 4),
            *([unit_spec] * 4),
        ),
        out_specs=(
            token_spec,
            token_spec,
            P(),
            *([weight_spec] * 10),
            *([norm_spec] * 5),
            *([head_spec] * 5),
            *([unit_spec] * 5),
        ),
        check_vma=False,
    )
```

```python
import functools

import jax
import jax.numpy as jnp
import numpy as np
from jax import lax
from jax.experimental import pallas as pl
from jax.experimental.pallas import tpu as pltpu
from jax.sharding import PartitionSpec as P

D = 2048
HEAD_DIM = 64
FF = 8192
SUMM = 50
NSEG = 4
SEG = 256
STEP = 10
PERIOD = SEG + SUMM
SEG_PAD = 320
SLAB = 64
KEYS = SLAB * (NSEG - 1) + SEG_PAD

norm_eps = 1e-05
beta_first = 0.9
beta_second = 0.95
adam_eps = 1e-08
clip_limit = 1.0
weight_decay = 0.1
average_keep = 0.6
vector_rate = 0.4
score_scale = HEAD_DIM ** (-0.5)
query_blocks = ((0, 128), (128, SEG_PAD))

RATE = 0.66e9

f32 = jnp.float32
bf16 = jnp.bfloat16


def seq_grid():
    count = lax.axis_size("seq")
    inner = count // 4
    return count // inner, inner


def shift_outer(value, step):
    outer, inner = seq_grid()
    pairs = [
        (a * inner + b, ((a + step) % outer) * inner + b) for a in range(outer) for b in range(inner)
    ]
    return lax.ppermute(value, "seq", pairs)


def shift_inner(value, step):
    outer, inner = seq_grid()
    pairs = [
        (a * inner + b, a * inner + (b + step) % inner) for a in range(outer) for b in range(inner)
    ]
    return lax.ppermute(value, "seq", pairs)


def swap(value, bits):
    return lax.ppermute(value, "mp", [(m, m ^ bits) for m in range(lax.axis_size("mp"))])


def block_order():
    outer, inner = seq_grid()
    me = lax.axis_index("seq")
    mine_a, mine_b = me // inner, me % inner
    return jnp.stack(
        [
            ((mine_b - b + inner) % inner) * outer + (mine_a - a + outer) % outer
            for a in range(outer)
            for b in range(inner)
        ]
    ).astype(jnp.int32)


def feature_order():
    outer, inner = seq_grid()
    me = lax.axis_index("seq")
    mine_a, mine_b = me // inner, me % inner
    return jnp.stack(
        [
            ((mine_a - i + outer) % outer) * inner + (mine_b - j + inner) % inner
            for j in range(inner)
            for i in range(outer)
        ]
    ).astype(jnp.int32)


def after(value, *others):
    return lax.optimization_barrier((value, *others))[0] if others else value


def row_codes():
    count = lax.axis_size("mp")
    return [high * 2 + low for low in range(2) for high in range(count // 2)]


def ring_rest(part):
    rest = []
    for _ in range(seq_grid()[1] - 1):
        part = shift_inner(part, 1)
        rest.append(part)
    return rest


def halved():
    return seq_grid()[1] == 2


def ring_end(part, rest, ready, late=()):
    if not halved():
        return [[piece] for piece in ring_rest(after(part, *ready))]
    half = (part.shape[0] + 31) // 32 * 16
    upper = shift_inner(after(part[:half], *ready), 1)
    return [[upper, shift_outer(after(rest[0][half:], *late), 1)]]


def stack_ring(line, rest, end):
    pieces = list(line)
    for j in range(seq_grid()[1] - 1):
        pieces += [blocks[j] for blocks in rest] + end[j]
    return [(piece, piece.shape[0]) for piece in pieces]


def ring_scatter(near, received, held=(), sums=(), late=()):
    sums, hop = list(sums), None
    depth = received[0].shape[0]
    for n in range(len(sums), len(received)):
        i = len(received) - 1 - n
        part = received[i] if i else after(received[i], *late)
        total = near[i * depth : (i + 1) * depth].astype(f32) + part.astype(f32)
        if sums:
            hop = shift_outer(after(sums[-1], *held[n - 1 : n]), -1)
            total = total + hop.astype(f32)
        sums.append(total.astype(bf16) if i else total)
    return sums, hop


def greet(peers):
    barrier = pltpu.get_barrier_semaphore()
    for peer in peers:
        pl.semaphore_signal(barrier, inc=1, device_id=peer, device_id_type=pl.DeviceIdType.MESH)
    pl.semaphore_wait(barrier, len(peers))


def others(axis, count):
    me = lax.axis_index(axis)
    return [lax.rem(me + step, count) for step in range(1, count)]


def exchange(axis, count, pieces, slots, send_sems, recv_sems):
    copies = []
    for step, peer in enumerate(others(axis, count)):
        copy = pltpu.make_async_remote_copy(
            src_ref=pieces(peer),
            dst_ref=slots.at[step],
            send_sem=send_sems.at[step],
            recv_sem=recv_sems.at[step],
            device_id={axis: peer},
            device_id_type=pl.DeviceIdType.MESH,
        )
        copy.start()
        copies.append(copy)
    return copies


def in_order(axis, count, mine, slots):
    me = lax.axis_index(axis)
    total = jnp.zeros_like(mine)
    for place in range(count):
        step = lax.rem(me + 2 * count - place - 1, count)
        other = slots[jnp.minimum(step, count - 2)]
        total = total + jnp.where(place == me, mine, other)
    return total


def square_tile(value):
    return jnp.sum((value * value).reshape(-1, 8, 128), axis=0)


def reduce_kernel(seqs, parts, shared, *refs):
    vector_ref, square_ref, out_ref, total_ref = refs[:4]
    first, norms, tiles, last = refs[4:8]
    sems = refs[8:]
    greet(
        [{"seq": peer} for peer in others("seq", seqs)]
        + [{"mp": peer} for peer in others("mp", parts)]
    )
    copies = exchange("seq", seqs, lambda peer: vector_ref.at[peer], first, sems[0], sems[1])
    value = vector_ref[lax.axis_index("seq")]
    for step, copy in enumerate(copies):
        copy.wait()
        value = value + first[step]
    out_ref[...] = value
    total_ref[...] = square_ref[...] + square_tile(value[shared:])
    copies = exchange("mp", parts, lambda peer: out_ref.at[:shared], norms, sems[2], sems[3])
    copies += exchange("mp", parts, lambda peer: total_ref, tiles, sems[4], sems[5])
    for copy in copies:
        copy.wait()
    norm = in_order("mp", parts, value[:shared], norms)
    tile = in_order("mp", parts, total_ref[...], tiles) + square_tile(norm)
    out_ref[:shared] = norm
    total_ref[...] = tile
    copies = exchange("seq", seqs, lambda peer: total_ref, last, sems[6], sems[7])
    for copy in copies:
        copy.wait()
    total_ref[...] = in_order("seq", seqs, tile, last)


def reduce_all(vectors, squares, shared):
    seqs, parts = lax.axis_size("seq"), lax.axis_size("mp")
    vmem = pl.BlockSpec(memory_space=pltpu.VMEM)
    block = vectors.shape[1:]
    counts = [seqs, seqs, parts, parts, parts, parts, seqs, seqs]
    return pl.pallas_call(
        functools.partial(reduce_kernel, seqs, parts, shared),
        out_shape=[
            jax.ShapeDtypeStruct(block, f32),
            jax.ShapeDtypeStruct((8, 128), f32),
        ],
        in_specs=[vmem, vmem],
        out_specs=[vmem, vmem],
        scratch_shapes=[
            pltpu.VMEM((seqs - 1, *block), f32),
            pltpu.VMEM((parts - 1, shared, 128), f32),
            pltpu.VMEM((parts - 1, 8, 128), f32),
            pltpu.VMEM((seqs - 1, 8, 128), f32),
        ]
        + [pltpu.SemaphoreType.DMA((count - 1,)) for count in counts],
        compiler_params=pltpu.CompilerParams(
            vmem_limit_bytes=4 * 2**20, collective_id=0, has_side_effects=True
        ),
        cost_estimate=expected(12.0),
        name="reduce_all",
    )(vectors, squares)


def gather_chips(own):
    high = [own]
    for bit in range(1, lax.axis_size("mp").bit_length() - 1):
        high = high + [swap(part, 1 << bit) for part in high]
    return high


def scatter_chips(first, second):
    count = lax.axis_size("mp") // 2
    rows = 2 * first.shape[0] // count
    total = first[:rows]
    for n in range(1, count):
        at = n * rows
        if at < first.shape[0]:
            part = first[at : at + rows].astype(bf16)
        else:
            part = second[at - first.shape[0] : at - first.shape[0] + rows]
        total = total + swap(part, n * 2).astype(f32)
    return total


def other_core():
    me = lax.axis_index("mp")
    return {"mp": me + 1 - 2 * lax.rem(me, 2)}


def core_copy(src, dst, send_sem, recv_sem):
    return pltpu.make_async_remote_copy(
        src_ref=src,
        dst_ref=dst,
        send_sem=send_sem,
        recv_sem=recv_sem,
        device_id=other_core(),
        device_id_type=pl.DeviceIdType.MESH,
    )


def kernel_params(number):
    return pltpu.CompilerParams(
        vmem_limit_bytes=56 * 2**20, collective_id=number, has_side_effects=True
    )


def expected(microseconds):
    return pl.CostEstimate(
        flops=int(microseconds * RATE), bytes_accessed=0, transcendentals=0
    )


def estimate(rows, depth, columns):
    return expected(1.5 + rows * depth * columns * 2 / 7.2e8)


def resident(shape):
    return pl.BlockSpec(shape, lambda *place: (0,) * len(shape))


def arrange_kernel(lefts, blocks, grid, normed, *refs):
    pieces, rest = refs[:lefts], refs[lefts:-3]
    got, send_sem, recv_sem = refs[-3:]
    out_ref, own_ref = rest[-2:]
    step = pl.program_id(0)
    rows, width = pieces[0].shape
    wide = width // blocks
    outer, inner = grid
    me = lax.axis_index("seq")
    mine_a, mine_b = me // inner, lax.rem(me, inner)

    def copy(n):
        return core_copy(pieces[n], got.at[n], send_sem.at[n], recv_sem.at[n])

    @pl.when(step == 0)
    def _():
        greet([other_core()])
        for n in range(lefts):
            copy(n).start()

    def fill(p, load):
        if normed:
            value = load(slice(None)).astype(f32)
            mean = jnp.mean(value, axis=-1, keepdims=True)
            center = value - mean
            scale = lax.rsqrt(jnp.mean(center * center, axis=-1, keepdims=True) + norm_eps)
        for b in range(blocks):
            place = lax.rem(mine_a - b % outer + outer, outer) * inner
            place = place + lax.rem(mine_b - b // outer + inner, inner)
            here = slice(b * wide, (b + 1) * wide)
            part = load(pl.ds(pl.multiple_of(place * wide, wide), wide))
            if p == 0:
                own_ref[:, here] = part
            part = part.astype(f32)
            if normed:
                part = (part - mean) * scale * rest[0][:, here] + rest[1][:, here]
            else:
                part = part * rest[0][...]
            out_ref[:, here] = part.astype(bf16)

    for n in range(lefts):

        @pl.when(step == n)
        def _(n=n):
            fill(n, lambda columns: pieces[n][:, columns])

        @pl.when(step == lefts + n)
        def _(n=n):
            copy(n).wait()
            fill(lefts + n, lambda columns: got[n, :, columns])


def arrange(pieces, extras, extra_specs, normed, number, name):
    rows, width = pieces[0].shape
    lefts = len(pieces)
    return pl.pallas_call(
        functools.partial(arrange_kernel, lefts, lax.axis_size("seq"), seq_grid(), normed),
        out_shape=[
            jax.ShapeDtypeStruct((2 * lefts * rows, width), bf16),
            jax.ShapeDtypeStruct((rows, width), bf16),
        ],
        grid=(2 * lefts,),
        in_specs=[resident((rows, width))] * lefts + extra_specs,
        out_specs=[pl.BlockSpec((rows, width), lambda n: (n, 0)), resident((rows, width))],
        scratch_shapes=[
            pltpu.VMEM((lefts, rows, width), bf16),
            pltpu.SemaphoreType.DMA((lefts,)),
            pltpu.SemaphoreType.DMA((lefts,)),
        ],
        compiler_params=kernel_params(number),
        cost_estimate=expected(9.0),
        name=name,
    )(*pieces, *extras)


def tall_kernel(epilogue, exchanged, lefts, blocks, extras, *refs):
    weight = jnp.concatenate([ref[...] for ref in refs[lefts : lefts + blocks]], axis=0)
    rest = refs[lefts + blocks :]
    step = pl.program_id(0)
    rows = refs[0].shape[0]
    if exchanged:
        others_ref, got, send_sem, recv_sem = rest[-4:]
        rest = rest[:-4]

        def copy(n):
            return core_copy(refs[n], got.at[n], send_sem.at[n], recv_sem.at[n])

        @pl.when(step == 0)
        def _():
            greet([other_core()])
            for n in range(lefts):
                copy(n).start()

    def fill(left, at):
        result = jnp.dot(left, weight, preferred_element_type=f32)
        epilogue(result, slice(at, at + rows), rest[:extras], rest[extras:])

    for n in range(lefts):
        fill(refs[n][...], n * rows)
    if exchanged:

        @pl.when(step == 0)
        def _():
            for n in range(lefts):
                copy(n).wait()

        for n in range(lefts):
            fill(got[n], (lefts + n) * rows)

        @pl.when(step == pl.num_programs(0) - 1)
        def _():
            for n in range(lefts):
                others_ref[n * rows : (n + 1) * rows, :] = got[n]


def tall_dot(lefts, blocks, start, width, epilogue, extras, outs, name, number=None):
    rows, depth = lefts[0].shape
    exchanged = number is not None
    count = len(lefts) * (2 if exchanged else 1)
    tile = max(size for size in (128, 256, 512) if width % size == 0 and start % size == 0)
    first = start // tile
    specs = [pl.BlockSpec((high, tile), lambda n: (0, first + n)) for _, high in blocks]
    blocks = [block for block, _ in blocks]
    out_shape = [jax.ShapeDtypeStruct((height, width), dtype) for height, dtype in outs]
    out_specs = [pl.BlockSpec((height, tile), lambda n: (0, n)) for height, _ in outs]
    scratch = []
    params = pltpu.CompilerParams(vmem_limit_bytes=56 * 2**20)
    if exchanged:
        out_shape.append(jax.ShapeDtypeStruct((len(lefts) * rows, depth), bf16))
        out_specs.append(resident((len(lefts) * rows, depth)))
        scratch = [
            pltpu.VMEM((len(lefts), rows, depth), bf16),
            pltpu.SemaphoreType.DMA((len(lefts),)),
            pltpu.SemaphoreType.DMA((len(lefts),)),
        ]
        params = kernel_params(number)
    return pl.pallas_call(
        functools.partial(
            tall_kernel, epilogue, exchanged, len(lefts), len(blocks), len(extras)
        ),
        out_shape=out_shape,
        grid=(width // tile,),
        in_specs=[resident(left.shape) for left in lefts]
        + specs
        + [pl.BlockSpec((extra.shape[0], tile), lambda n: (0, n)) for extra in extras],
        out_specs=out_specs,
        scratch_shapes=scratch,
        compiler_params=params,
        cost_estimate=estimate(rows * count, depth, width),
        name=name,
    )(*lefts, *blocks, *extras)


def plain_epilogue(result, here, extras, outs):
    outs[0][here, :] = result.astype(bf16)


def project_epilogue(result, here, extras, outs):
    bias, scale = extras
    outs[0][here, :] = ((result + bias[...]).astype(bf16).astype(f32) * scale[...]).astype(bf16)


def up_epilogue(result, here, extras, outs):
    value, slope = gelu_both(result + extras[0][...])
    outs[0][here, :] = value.astype(bf16)
    outs[1][here, :] = slope.astype(bf16)


def slope_epilogue(result, here, extras, outs):
    grad = (result * extras[0][here, :].astype(f32)).astype(bf16)
    outs[0][here, :] = grad
    sums = jnp.sum(grad.astype(f32), axis=0, keepdims=True)
    outs[1][...] = jnp.broadcast_to(sums, outs[1].shape)


def wide_kernel(blocks, start, left_ref, *refs):
    first_ref, second_ref, sent, got, send_sem, recv_sem = refs[blocks:]
    step = pl.program_id(0)
    columns = slice(start, start + left_ref.shape[1])

    def copy(n):
        return core_copy(sent.at[n], got.at[n], send_sem.at[n], recv_sem.at[n])

    @pl.when(step == 0)
    def _():
        greet([other_core()])

    result = lax.dot_general(
        left_ref[...],
        jnp.concatenate([ref[:, columns] for ref in refs[:blocks]], axis=0),
        (((1,), (1,)), ((), ())),
        preferred_element_type=f32,
    )
    for n in range(2):

        @pl.when(step == n)
        def _(n=n):
            sent[n] = result.astype(bf16)
            copy(n).start()

    @pl.when(step == 2)
    def _():
        copy(0).wait()
        second_ref[...] = (result + got[0].astype(f32)).astype(bf16)

    @pl.when(step == 3)
    def _():
        copy(1).wait()
        first_ref[...] = result + got[1].astype(f32)


def wide_dot(left, blocks, start, features, number, name, weight=1.0):
    rows, width = left.shape
    tile = rows // 4
    specs = [resident((high, block.shape[1])) for block, high in blocks]
    blocks = [block for block, _ in blocks]
    return pl.pallas_call(
        functools.partial(wide_kernel, len(blocks), start),
        out_shape=[
            jax.ShapeDtypeStruct((tile, features), f32),
            jax.ShapeDtypeStruct((tile, features), bf16),
        ],
        grid=(4,),
        in_specs=[pl.BlockSpec((tile, width), lambda n: (3 - n, 0))] + specs,
        out_specs=[resident((tile, features)), resident((tile, features))],
        scratch_shapes=[
            pltpu.VMEM((2, tile, features), bf16),
            pltpu.VMEM((2, tile, features), bf16),
            pltpu.SemaphoreType.DMA((2,)),
            pltpu.SemaphoreType.DMA((2,)),
        ],
        compiler_params=kernel_params(number),
        cost_estimate=estimate(rows, width * weight, features),
        name=name,
    )(left, *blocks)


def turned_kernel(shapes, sizes, *refs):
    refs = list(refs)
    groups = [[refs.pop(0) for _ in range(count)] for count in shapes]
    rights = [refs.pop(0) for _ in shapes]

    def fill(out_ref, here):
        at = 0
        for lefts, right_ref in zip(groups, rights):
            width = right_ref.shape[1]
            left = jnp.concatenate([ref[...] for ref in lefts], axis=0)
            out_ref[here, at : at + width] = lax.dot_general(
                left, right_ref[...], (((0,), (0,)), ((), ())), preferred_element_type=f32
            ).astype(bf16)
            at += width

    if sizes is None:
        fill(refs[0], slice(None))
    else:
        step = 0
        for size, out_ref in zip(sizes, refs):
            depth = out_ref.shape[0] // size
            for n in range(size):
                here = slice(n * depth, (n + 1) * depth)
                pl.when(pl.program_id(0) == step)(functools.partial(fill, out_ref, here))
                step += 1


def turned_dot(pairs, first, count, depth, name, sizes=None):
    width = sum(right.shape[1] for _, right in pairs)
    rows = pairs[0][1].shape[0]
    if sizes is None:
        out_shape = [jax.ShapeDtypeStruct((count * depth, width), bf16)]
        out_specs = [pl.BlockSpec((depth, width), lambda n: (n, 0))]
    else:
        out_shape = [jax.ShapeDtypeStruct((size * depth, width), bf16) for size in sizes]
        out_specs = [resident((size * depth, width)) for size in sizes]
    return pl.pallas_call(
        functools.partial(turned_kernel, [len(lefts) for lefts, _ in pairs], sizes),
        out_shape=out_shape,
        grid=(count,),
        in_specs=[
            pl.BlockSpec((left.shape[0], depth), lambda n: (0, first + n))
            for lefts, _ in pairs
            for left in lefts
        ]
        + [resident(right.shape) for _, right in pairs],
        out_specs=out_specs,
        compiler_params=pltpu.CompilerParams(vmem_limit_bytes=56 * 2**20),
        cost_estimate=estimate(rows, count * depth, width),
        name=name,
    )(*[left for lefts, _ in pairs for left in lefts], *[right for _, right in pairs])


def far_grads(pairs, depth, name, sizes):
    outer, inner = seq_grid()
    return [
        turned_dot(pairs, j * outer, outer, depth, name + "_far", sizes) for j in range(1, inner)
    ]


def near_grads(pairs, depth, name):
    return turned_dot(pairs, 0, seq_grid()[0], depth, name + "_near")[0]


def inner_sum(far, n, *ready):
    part = shift_inner(after(far[-1][n], *ready), -1)
    for parts in reversed(far[:-1]):
        part = shift_inner((parts[n].astype(f32) + part.astype(f32)).astype(bf16), -1)
    return part


def single_blocks(groups, depth):
    return [
        group[n * depth : (n + 1) * depth]
        for group in groups
        for n in range(group.shape[0] // depth)
    ]


def from_blocks_kernel(blocks, order_ref, in_ref, out_ref):
    rows, width = out_ref.shape
    wide = width // blocks
    for b in range(blocks):
        there = pl.ds(pl.multiple_of(order_ref[b] * wide, wide), wide)
        out_ref[:, there] = in_ref[:rows, b * wide : (b + 1) * wide].astype(out_ref.dtype)


def from_blocks(value, order, rows):
    rows_padded, width = value.shape
    return pl.pallas_call(
        functools.partial(from_blocks_kernel, order.shape[0]),
        out_shape=jax.ShapeDtypeStruct((rows, width), bf16),
        in_specs=[
            pl.BlockSpec(memory_space=pltpu.SMEM),
            pl.BlockSpec(memory_space=pltpu.VMEM),
        ],
        out_specs=pl.BlockSpec(memory_space=pltpu.VMEM),
        compiler_params=pltpu.CompilerParams(vmem_limit_bytes=12 * 2**20),
        cost_estimate=expected(3.0),
        name="from_blocks",
    )(order, value)


def segment_starts(me, mp_count, rows_padded):
    group = mp_count // NSEG
    starts = []
    for s in range(NSEG):
        pieces = []
        for r in range(group):
            code = jnp.bitwise_xor(me, s * group + r)
            place = jnp.bitwise_and(code, 1) * (mp_count // 2) + lax.shift_right_logical(code, 1)
            pieces.append(pl.multiple_of(place * rows_padded, rows_padded))
        starts.append(pieces)
    return starts


def load_segment(ref, pieces, rows_padded):
    parts = [ref[pl.ds(start, rows_padded), :] for start in pieces]
    return parts[0] if len(parts) == 1 else jnp.concatenate(parts, axis=0)


def load_slab(ref, pieces, rows_padded):
    return ref[pl.ds(pl.multiple_of(pieces[-1] + (rows_padded - SLAB), 16), SLAB), :]


def store_segment(ref, pieces, rows_padded, value):
    for r, start in enumerate(pieces):
        ref[pl.ds(start, rows_padded), :] = value[r * rows_padded : (r + 1) * rows_padded]


def lane_halves(shape):
    lane = lax.broadcasted_iota(jnp.int32, shape, 1)
    return lane < HEAD_DIM


def attend_kernel(mp_count, rows_padded, me_ref, q_ref, k_ref, v_ref, bias_ref, o_ref, p_ref):
    starts = segment_starts(me_ref[0], mp_count, rows_padded)
    for s in range(NSEG):
        keys = jnp.concatenate(
            [load_slab(k_ref, starts[e], rows_padded) for e in range(s)]
            + [load_segment(k_ref, starts[s], rows_padded)],
            axis=0,
        )
        values = jnp.concatenate(
            [load_slab(v_ref, starts[e], rows_padded) for e in range(s)]
            + [load_segment(v_ref, starts[s], rows_padded)],
            axis=0,
        )
        queries = load_segment(q_ref, starts[s], rows_padded)
        first_head = lane_halves(queries.shape)
        zero = jnp.zeros_like(queries)
        head_queries = (jnp.where(first_head, queries, zero), jnp.where(first_head, zero, queries))
        units = [(low, high, h) for low, high in query_blocks for h in range(2)]
        scores = [
            lax.dot_general(
                head_queries[h][low:high],
                keys[: SLAB * s + high],
                (((1,), (1,)), ((), ())),
                preferred_element_type=f32,
            )
            + bias_ref[s, low:high, : SLAB * s + high]
            for low, high, h in units
        ]
        shares = []
        for (low, high, h), score in zip(units, scores):
            raised = jnp.exp(score - jnp.max(score, axis=-1, keepdims=True))
            share = raised * (1.0 / jnp.sum(raised, axis=-1, keepdims=True))
            shares.append(share.astype(bf16))
            p_ref[h, s * SEG_PAD + low : s * SEG_PAD + high, : SLAB * s + high] = shares[-1]
        both = [
            jnp.dot(share, values[: SLAB * s + high], preferred_element_type=f32)
            for (low, high, h), share in zip(units, shares)
        ]
        outs = [
            jnp.where(first_head[low:high], both[2 * n], both[2 * n + 1])
            for n, (low, high) in enumerate(query_blocks)
        ]
        out = jnp.concatenate(outs, axis=0).astype(bf16)
        store_segment(o_ref, starts[s], rows_padded, out)


def attend(qkv, bias, me, mp_count, rows_padded):
    rows, width = qkv.shape
    pairs = width // 3 // 128
    return pl.pallas_call(
        functools.partial(attend_kernel, mp_count, rows_padded),
        out_shape=(
            jax.ShapeDtypeStruct((rows, width // 3), bf16),
            jax.ShapeDtypeStruct((pairs * 2, rows, KEYS), bf16),
        ),
        grid_spec=pltpu.PrefetchScalarGridSpec(
            num_scalar_prefetch=1,
            grid=(pairs,),
            in_specs=[
                pl.BlockSpec((rows, 128), lambda n, me_ref: (0, n)),
                pl.BlockSpec((rows, 128), lambda n, me_ref: (0, pairs + n)),
                pl.BlockSpec((rows, 128), lambda n, me_ref: (0, 2 * pairs + n)),
                pl.BlockSpec(bias.shape, lambda n, me_ref: (0, 0, 0)),
            ],
            out_specs=(
                pl.BlockSpec((rows, 128), lambda n, me_ref: (0, n)),
                pl.BlockSpec((2, rows, KEYS), lambda n, me_ref: (n, 0, 0)),
            ),
        ),
        compiler_params=pltpu.CompilerParams(vmem_limit_bytes=48 * 2**20),
        cost_estimate=expected(12.0),
        name="attend",
    )(me, qkv, qkv, qkv, bias)


def attend_back_kernel(
    mp_count,
    rows_padded,
    me_ref,
    q_ref,
    k_ref,
    v_ref,
    o_ref,
    g_ref,
    p_ref,
    dq_ref,
    dk_ref,
    dv_ref,
    key_sum,
    value_sum,
):
    starts = segment_starts(me_ref[0], mp_count, rows_padded)
    key_sum[...] = jnp.zeros_like(key_sum)
    value_sum[...] = jnp.zeros_like(value_sum)
    for s in range(NSEG):
        keys = jnp.concatenate(
            [load_slab(k_ref, starts[e], rows_padded) for e in range(s)]
            + [load_segment(k_ref, starts[s], rows_padded)],
            axis=0,
        )
        values = jnp.concatenate(
            [load_slab(v_ref, starts[e], rows_padded) for e in range(s)]
            + [load_segment(v_ref, starts[s], rows_padded)],
            axis=0,
        )
        queries = load_segment(q_ref, starts[s], rows_padded)
        grads = load_segment(g_ref, starts[s], rows_padded)
        outs = load_segment(o_ref, starts[s], rows_padded)
        queries_turned = queries.astype(f32).T.astype(bf16)
        grads_turned = grads.astype(f32).T.astype(bf16)
        first_head = lane_halves(queries.shape)
        zero = jnp.zeros_like(queries)
        head_grads = (jnp.where(first_head, grads, zero), jnp.where(first_head, zero, grads))
        product = grads.astype(f32) * outs.astype(f32)
        head_deltas = (
            jnp.sum(jnp.where(first_head, product, 0.0), axis=-1, keepdims=True),
            jnp.sum(jnp.where(first_head, 0.0, product), axis=-1, keepdims=True),
        )
        units = [(low, high, h) for low, high in query_blocks for h in range(2)]
        shares = [
            p_ref[h, s * SEG_PAD + low : s * SEG_PAD + high, : SLAB * s + high]
            for low, high, h in units
        ]
        share_grads = [
            lax.dot_general(
                head_grads[h][low:high],
                values[: SLAB * s + high],
                (((1,), (1,)), ((), ())),
                preferred_element_type=f32,
            )
            for low, high, h in units
        ]
        score_grads = [
            (share.astype(f32) * (share_grad - head_deltas[h][low:high])).astype(bf16)
            for (low, high, h), share, share_grad in zip(units, shares, share_grads)
        ]
        both = [
            jnp.dot(score_grad, keys[: SLAB * s + high], preferred_element_type=f32)
            for (low, high, h), score_grad in zip(units, score_grads)
        ]
        query_grads = [
            jnp.where(first_head[low:high], both[2 * n], both[2 * n + 1])
            for n, (low, high) in enumerate(query_blocks)
        ]
        for (low, high, h), share, score_grad in zip(units, shares, score_grads):
            lanes = slice(h * HEAD_DIM, (h + 1) * HEAD_DIM)
            value_part = jnp.dot(grads_turned[lanes, low:high], share, preferred_element_type=f32)
            key_part = jnp.dot(
                queries_turned[lanes, low:high], score_grad, preferred_element_type=f32
            )
            for e in range(s):
                place = slice((e + 1) * SEG_PAD - SLAB, (e + 1) * SEG_PAD)
                value_sum[lanes, place] += value_part[:, e * SLAB : (e + 1) * SLAB]
                key_sum[lanes, place] += key_part[:, e * SLAB : (e + 1) * SLAB]
            place = slice(s * SEG_PAD, s * SEG_PAD + high)
            value_sum[lanes, place] += value_part[:, s * SLAB :]
            key_sum[lanes, place] += key_part[:, s * SLAB :]
        query_grad = (jnp.concatenate(query_grads, axis=0) * score_scale).astype(bf16)
        store_segment(dq_ref, starts[s], rows_padded, query_grad)
    key_all = key_sum[...].T.astype(bf16)
    value_all = value_sum[...].T.astype(bf16)
    for s in range(NSEG):
        place = slice(s * SEG_PAD, (s + 1) * SEG_PAD)
        store_segment(dk_ref, starts[s], rows_padded, key_all[place])
        store_segment(dv_ref, starts[s], rows_padded, value_all[place])


def attend_back(qkv, out, grad, share, me, mp_count, rows_padded):
    rows, width = qkv.shape
    pairs = width // 3 // 128
    column = pl.BlockSpec((rows, 128), lambda n, me_ref: (0, n))
    piece = jax.ShapeDtypeStruct((rows, width // 3), bf16)
    return pl.pallas_call(
        functools.partial(attend_back_kernel, mp_count, rows_padded),
        out_shape=(piece, piece, piece),
        grid_spec=pltpu.PrefetchScalarGridSpec(
            num_scalar_prefetch=1,
            grid=(pairs,),
            in_specs=[
                column,
                pl.BlockSpec((rows, 128), lambda n, me_ref: (0, pairs + n)),
                pl.BlockSpec((rows, 128), lambda n, me_ref: (0, 2 * pairs + n)),
                column,
                column,
                pl.BlockSpec((2, rows, KEYS), lambda n, me_ref: (n, 0, 0)),
            ],
            out_specs=(column, column, column),
            scratch_shapes=[pltpu.VMEM((128, rows), f32), pltpu.VMEM((128, rows), f32)],
        ),
        compiler_params=pltpu.CompilerParams(vmem_limit_bytes=48 * 2**20),
        cost_estimate=expected(12.5),
        name="attend_back",
    )(me, qkv, qkv, qkv, out, grad, share)


def item_rows(present, summary, parts, rows, rows_padded):
    kept = present[:, None] * jnp.concatenate([jnp.ones((NSEG, SEG), jnp.int32), summary], axis=1)
    group = parts // NSEG
    kept = jnp.pad(kept.reshape(NSEG, group, rows), ((0, 0), (0, 0), (0, rows_padded - rows)))
    flags = np.zeros((group, rows_padded), np.int32)
    flags[:, :rows] = (np.arange(PERIOD) >= SEG).reshape(group, rows)
    return kept.reshape(NSEG, group * rows_padded), flags.reshape(group * rows_padded)


def score_bias(kept, flags):
    slab = (kept * flags[None, :])[:, SEG_PAD - SLAB :] == 1
    causal = np.tril(np.ones((SEG_PAD, SEG_PAD), bool))
    itself = np.eye(SEG_PAD, dtype=bool)
    planes = []
    for s in range(NSEG):
        own = (kept[s][None, :] == 1) & causal | itself
        pieces = [jnp.broadcast_to(slab[e][None, :], (SEG_PAD, SLAB)) for e in range(s)] + [own]
        seen = jnp.concatenate(pieces, axis=1)
        planes.append(jnp.pad(seen, ((0, 0), (0, KEYS - seen.shape[1]))))
    return jnp.where(jnp.stack(planes), 0.0, -1e30).astype(f32)


def norm_parts(value):
    center = value - jnp.mean(value, axis=-1, keepdims=True)
    spread = jnp.mean(center * center, axis=-1, keepdims=True)
    scale = lax.rsqrt(spread + norm_eps)
    return center * scale, scale


def norm_back(normed, scale, gain, grad):
    inner = grad * gain
    return scale * (
        inner
        - jnp.mean(inner, axis=-1, keepdims=True)
        - normed * jnp.mean(inner * normed, axis=-1, keepdims=True)
    )


def gelu_both(value):
    c = 0.7978845608028654
    square = value * value
    bend = jnp.tanh(c * (value + 0.044715 * value * square))
    half = 0.5 * (1.0 + bend)
    slope = half + 0.5 * value * (1.0 - bend * bend) * c * (1.0 + 3.0 * 0.044715 * square)
    return value * half, slope


def adam_step(master, grad, first, second, average, factor, rate, decay):
    clipped = grad * factor
    first_new = beta_first * first + (1.0 - beta_first) * clipped
    second_new = beta_second * second + (1.0 - beta_second) * clipped * clipped
    first_hat = first_new * (1.0 / (1.0 - beta_first**STEP))
    second_hat = second_new * (1.0 / (1.0 - beta_second**STEP))
    master_new = master - rate * (first_hat / (jnp.sqrt(second_hat) + adam_eps) + decay * master)
    average_new = average_keep * average + (1.0 - average_keep) * master_new
    return (master_new, first_new, second_new, average_new, master_new.astype(bf16))


def vector_kernel(square_ref, *refs):
    vector_refs, state, outs = refs[:3], refs[3:15], refs[15:]
    grad_norm = jnp.sqrt(jnp.sum(square_ref[...], keepdims=True))
    factor = jnp.minimum(1.0, clip_limit / (grad_norm + 1e-06))
    for n in range(3):
        old = [ref[...] for ref in state[4 * n : 4 * n + 4]]
        new = adam_step(old[0], vector_refs[n][...], *old[1:], factor, vector_rate, 0.0)
        for ref, value in zip(outs[5 * n : 5 * n + 5], new):
            ref[...] = value


def adam_vectors(squares, vectors, state):
    vmem = pl.BlockSpec(memory_space=pltpu.VMEM)
    out_shape = []
    for n in range(3):
        group = state[4 * n : 4 * n + 4]
        out_shape += [jax.ShapeDtypeStruct(array.shape, f32) for array in group]
        out_shape.append(jax.ShapeDtypeStruct(group[0].shape, bf16))
    return pl.pallas_call(
        vector_kernel,
        out_shape=out_shape,
        in_specs=[vmem] * (1 + len(vectors) + len(state)),
        out_specs=[vmem] * len(out_shape),
        compiler_params=pltpu.CompilerParams(vmem_limit_bytes=4 * 2**20),
        cost_estimate=expected(3.0),
        name="adam_vectors",
    )(squares, *vectors, *state)


def per_device(
    tokens,
    cotangent,
    present,
    summary_mask,
    attention_weight,
    attention_first,
    attention_second,
    attention_average,
    hidden_weight,
    hidden_first,
    hidden_second,
    hidden_average,
    norm_params,
    norm_first,
    norm_second,
    norm_average,
    head_bias,
    head_first,
    head_second,
    head_average,
    unit_bias,
    unit_first,
    unit_second,
    unit_average,
):
    outer, inner = seq_grid()
    seqs = outer * inner
    parts = lax.axis_size("mp")
    rows = tokens.shape[0]
    rows_padded = SEG_PAD * NSEG // parts
    head_width = attention_weight.shape[2]
    depth = attention_weight.shape[1]
    me = lax.axis_index("mp")
    me_vector = me.astype(jnp.int32)[None]
    order = feature_order()
    back_order = block_order()
    codes = row_codes()
    units = hidden_weight.shape[2]
    total_rows = parts * rows_padded

    norm_size, head_size = norm_params.size, head_bias.size
    packed = jnp.concatenate([norm_params.reshape(-1), head_bias.reshape(-1), unit_bias])
    packed_size = packed.size
    packed_width = 4 * head_width
    packed = jnp.pad(packed, (0, 16 * packed_width - packed_size)).reshape(16, packed_width)
    attn_own = jnp.concatenate(
        [jnp.concatenate([attention_weight[n] for n in range(4)], axis=1), packed], axis=0
    ).astype(bf16)
    row_pad = ((0, rows_padded - rows), (0, 0))
    tokens_all = gather_chips(jnp.pad(tokens, row_pad))
    cotangent_pieces = gather_chips(after(jnp.pad(cotangent, row_pad), *tokens_all))
    up_own, down_own = hidden_weight[0].astype(bf16), hidden_weight[1].astype(bf16)
    attn_line, attn_rest = [attn_own], [ring_rest(attn_own)]
    for i in range(1, outer):
        behind = attn_rest[i - 2] if i > 1 else []
        behind = behind + (tokens_all[1:] if i == outer - 1 else [])
        attn_line.append(shift_outer(after(attn_line[-1], *behind), 1))
        if i < outer - 1:
            attn_rest.append(ring_rest(attn_line[-1]))
    attn_end = ring_end(attn_line[3], attn_rest[2], [])
    attn_ends = [part for parts in attn_end for part in parts]
    attn_blocks, vectors, at = [], [], 0
    for piece, high in stack_ring(attn_line, attn_rest, attn_end):
        used = min(high, depth - at % depth)
        if high > used:
            vectors.append(piece[used : used + 1, :packed_size])
        attn_blocks.append((piece, used))
        at += used
    up_line = [up_own, shift_outer(after(up_own, attn_ends[-1]), 1)]
    up_line.append(shift_outer(up_line[1], 1))
    up_line.append(shift_outer(up_line[2], 1))
    up_rest = [ring_rest(after(up_own, attn_ends[0]))]
    up_rest.append(ring_rest(after(up_line[1], *up_rest[0])))

    vectors = jnp.concatenate(vectors, axis=0).astype(f32)
    norm_vals = vectors[:, :norm_size].reshape(seqs, 6, depth).transpose(1, 0, 2).reshape(6, D)
    vectors = jnp.take(vectors[:, norm_size:], back_order, axis=0)
    head_vals = vectors[:, :head_size].reshape(seqs, 2, head_width // seqs)
    head_vals = head_vals.transpose(1, 0, 2).reshape(2, head_width)
    unit_vals = vectors[:, head_size:].reshape(-1)

    kept, flags = item_rows(present[0], summary_mask[0], parts, rows, rows_padded)
    bias = score_bias(kept, flags)
    kept_parts = kept.reshape(parts, rows_padded).astype(f32)
    kept_all = jnp.take(kept_parts, jnp.stack([me ^ code for code in codes]), axis=0).reshape(-1, 1)
    kept_own = kept_all[:rows_padded]

    first_all, inputs_own = arrange(
        tokens_all,
        [norm_vals[0:1], norm_vals[1:2]],
        [resident((1, D))] * 2,
        True,
        2,
        "first_norm",
    )
    qkv_bias = jnp.concatenate([head_vals[0], jnp.zeros_like(head_vals[0]), head_vals[1]])
    qkv_scale = np.concatenate(
        [np.full(head_width, score_scale, np.float32), np.ones(2 * head_width, np.float32)]
    )
    qkv = tall_dot(
        [after(first_all, *cotangent_pieces)],
        attn_blocks,
        0,
        3 * head_width,
        project_epilogue,
        [qkv_bias[None], qkv_scale[None]],
        [(total_rows, bf16)],
        "project",
    )[0]
    down_rest = []
    down_line = [down_own, shift_outer(after(down_own, qkv), 1)]
    qkv = after(qkv, up_line[1])
    context, share = attend(qkv, bias, me_vector, parts, rows_padded)
    up_rest.append(ring_rest(after(up_line[2], context, *up_rest[1])))
    up_end = ring_end(up_line[3], up_rest[2], up_rest[2])
    up_ends = [part for parts in up_end for part in parts]
    down_line.append(shift_outer(after(down_line[1], up_ends[-1]), 1))
    down_line.append(shift_outer(down_line[2], 1))
    up_blocks = stack_ring(up_line, up_rest, up_end)
    context = after(context, up_line[2], *up_rest[0])
    join_parts = wide_dot(context, attn_blocks, 3 * head_width, D, 4, "join")
    down_rest.append(ring_rest(after(down_own, *up_rest[2])))
    down_rest.append(ring_rest(after(down_line[1], up_ends[0])))
    join_parts = [join_parts[0], after(join_parts[1], down_line[1], *up_rest[1])]
    attended = scatter_chips(*join_parts) + norm_vals[4]
    attended = after(attended, up_line[3], *down_rest[0])
    feed_grad, cotangent_own = arrange(
        cotangent_pieces,
        [kept_all],
        [pl.BlockSpec((rows_padded, 1), lambda n: (n, 0))],
        False,
        3,
        "feed_grad",
    )
    inputs = inputs_own.astype(f32)
    middle = inputs + kept_own * attended

    normed_two, scale_two = norm_parts(middle)
    second_own = (normed_two * norm_vals[2] + norm_vals[3]).astype(bf16)
    second_all = gather_chips(second_own)
    down_rest.append(ring_rest(after(down_line[2], second_all[1])))
    second_all = after(second_all, feed_grad, down_line[2], *down_rest[1])
    activated, slope, second_others = tall_dot(
        second_all,
        up_blocks,
        0,
        units,
        up_epilogue,
        [unit_vals[None]],
        [(total_rows, bf16), (total_rows, bf16)],
        "up",
        5,
    )
    second_all = second_all + [second_others]

    out_grad = cotangent_own.astype(f32)
    down_bias_grad = jnp.sum(kept_own * out_grad, axis=0)

    down_end = ring_end(down_line[3], down_rest[2], [activated, *down_rest[1]], [activated])
    down_ends = [part for parts in down_end for part in parts]
    down_blocks = stack_ring(down_line, down_rest, down_end)
    activated = after(activated, down_line[3], *down_rest[2])
    down_pairs = [([feed_grad], activated)]
    down_far = far_grads(down_pairs, depth, "down_grad", (3, 1))
    down_last = inner_sum(down_far, 1, *down_ends)
    pre_grad, unit_grad = tall_dot(
        [feed_grad],
        down_blocks,
        0,
        units,
        slope_epilogue,
        [slope],
        [(total_rows, bf16), (8, f32)],
        "down_back",
    )
    unit_grad = unit_grad[0]
    down_first = inner_sum(down_far, 0, pre_grad)
    down_near = near_grads([([after(feed_grad, pre_grad)], activated)], depth, "down_grad")
    down_blocks_in = single_blocks([down_first, down_last], depth)
    down_totals = ring_scatter(down_near, down_blocks_in)[0][:-1]
    pre_grad = after(pre_grad, down_last, down_near)
    second_parts = wide_dot(pre_grad, up_blocks, 0, D, 6, "up_back")
    up_pairs = [(after(second_all, *second_parts), pre_grad)]
    up_far = far_grads(up_pairs, depth, "up_grad", (2, 1, 1))
    up_near = near_grads(up_pairs, depth, "up_grad")
    second_grad = after(scatter_chips(*second_parts), up_near, *[far[2] for far in up_far])
    gain_two_grad = jnp.sum(second_grad * normed_two, axis=0)
    shift_two_grad = jnp.sum(second_grad, axis=0)
    middle_grad = out_grad + norm_back(normed_two, scale_two, norm_vals[2], second_grad)

    attn_grad = kept_own * middle_grad
    out_bias_grad = jnp.sum(attn_grad, axis=0)
    up_last = inner_sum(up_far, 2, second_grad)
    feed_parts = wide_dot(after(activated, second_grad), down_blocks, 0, D, 8, "down")
    attn_rows = after(gather_chips(attn_grad.astype(bf16)), down_first, up_last, *feed_parts)
    context_grad, attn_others = tall_dot(
        attn_rows,
        attn_blocks,
        3 * head_width,
        head_width,
        plain_epilogue,
        [],
        [(total_rows, bf16)],
        "join_back",
        7,
    )
    attn_rows = attn_rows + [attn_others]
    up_middle = inner_sum(up_far, 1, down_first)
    up_first = inner_sum(up_far, 0, up_last, context_grad)
    context_grad = after(context_grad, down_totals[2])
    query_grad, key_grad, value_grad = attend_back(
        qkv, context, context_grad, share, me_vector, parts, rows_padded
    )
    qkv_grad = jnp.concatenate([query_grad, key_grad, value_grad], axis=1)
    head_grad = jnp.stack(
        [jnp.sum(query_grad, axis=0, dtype=f32), jnp.sum(value_grad, axis=0, dtype=f32)]
    )
    up_totals, up_hop = ring_scatter(up_near, single_blocks([up_first, up_middle, up_last], depth))
    up_grad = up_totals[-1]
    attn_pairs = [
        ([after(first_all, up_totals[1])], qkv_grad),
        (attn_rows, context),
    ]
    attn_far = far_grads(attn_pairs, depth, "attn_grad", (1, 1, 1, 1))
    all_far = [part for far in attn_far for part in far]
    first_parts = wide_dot(after(qkv_grad, *all_far), attn_blocks, 0, D, 9, "project_back")
    attn_pairs = [
        ([after(first_all, up_totals[2], *first_parts)], qkv_grad),
        (attn_rows, context),
    ]
    attn_near = near_grads(attn_pairs, depth, "attn_grad")
    attn_sums = [None] * outer
    attn_sums[3] = inner_sum(attn_far, 3, up_middle)
    attn_sums[2] = inner_sum(attn_far, 2, up_first)
    attn_total = attn_near[3 * depth :].astype(f32) + attn_sums[3].astype(f32)
    attn_total = attn_total.astype(bf16)
    attn_sums[1] = inner_sum(attn_far, 1, attn_total, up_hop)
    attn_sums[0] = inner_sum(attn_far, 0, attn_sums[2])
    attn_totals, _ = ring_scatter(attn_near, attn_sums, [up_hop], [attn_total])
    down_grad = ring_scatter(down_near, down_blocks_in, (), down_totals, [attn_total])[0][-1]
    feed_out = scatter_chips(*after(feed_parts, attn_total)) + norm_vals[5]
    block_output = from_blocks(middle + kept_own * feed_out, order, rows)
    first_grad = scatter_chips(*first_parts)
    normed_one, scale_one = norm_parts(inputs)
    gain_one_grad = jnp.sum(first_grad * normed_one, axis=0)
    shift_one_grad = jnp.sum(first_grad, axis=0)
    input_grad = from_blocks(
        middle_grad + norm_back(normed_one, scale_one, norm_vals[0], first_grad), order, rows
    )

    vector_grad = jnp.stack(
        [
            gain_one_grad,
            shift_one_grad,
            gain_two_grad,
            shift_two_grad,
            out_bias_grad,
            down_bias_grad,
        ]
    )
    vector_grad = jnp.take(
        vector_grad.reshape(6, seqs, depth).transpose(1, 0, 2).reshape(seqs, -1), back_order, axis=0
    )
    norm_room = -(-norm_size // 1024) * 1024
    room = norm_room + -(-(packed_size - norm_size) // 1024) * 1024
    vectors = jnp.concatenate(
        [
            vector_grad,
            jnp.zeros((seqs, norm_room - norm_size), f32),
            head_grad.reshape(2, seqs, -1).transpose(1, 0, 2).reshape(seqs, -1),
            unit_grad.reshape(seqs, -1),
            jnp.zeros((seqs, room - norm_room - packed_size + norm_size), f32),
        ],
        axis=1,
    )
    vectors = vectors.reshape(seqs, room // 128, 128)
    attn_shard = attn_totals[-1]
    squares = sum(jnp.sum(shard * shard) for shard in (attn_shard, up_grad, down_grad))
    squares = jnp.pad(squares.reshape(1, 1), ((0, 7), (0, 127)))
    vectors, squares = reduce_all(vectors, squares, norm_room // 128)
    grad_norm = jnp.sqrt(jnp.sum(squares))
    vectors = vectors.reshape(-1)
    norm_shard = vectors[:norm_size].reshape(norm_params.shape)
    head_shard = vectors[norm_room : norm_room + head_size].reshape(head_bias.shape)
    unit_shard = vectors[norm_room + head_size : norm_room + packed_size - norm_size]
    factor = jnp.minimum(1.0, clip_limit / (grad_norm + 1e-06))
    hidden_rate = jnp.array([D ** (-0.5), FF ** (-0.5)], f32)[:, None, None]
    attn_shard = jnp.stack(
        [attn_shard[:, n * head_width : (n + 1) * head_width] for n in range(4)]
    )
    hidden_out = adam_step(
        hidden_weight,
        jnp.stack([up_grad, down_grad]),
        hidden_first,
        hidden_second,
        hidden_average,
        factor,
        hidden_rate,
        weight_decay,
    )
    attention_out = adam_step(
        attention_weight,
        attn_shard,
        attention_first,
        attention_second,
        attention_average,
        factor,
        D ** (-0.5),
        weight_decay,
    )
    updated = adam_vectors(
        squares,
        [norm_shard, head_shard, unit_shard[None]],
        [
            norm_params,
            norm_first,
            norm_second,
            norm_average,
            head_bias,
            head_first,
            head_second,
            head_average,
            unit_bias[None],
            unit_first[None],
            unit_second[None],
            unit_average[None],
        ],
    )
    return (
        block_output,
        input_grad,
        grad_norm,
        *attention_out,
        *hidden_out,
        *updated[:10],
        *[value[0] for value in updated[10:]],
    )


def solution(mesh):
    token_spec = P(("seq", "mp"), None)
    weight_spec = P(None, "seq", "mp")
    norm_spec = P(None, "seq")
    head_spec = P(None, ("mp", "seq"))
    unit_spec = P(("mp", "seq"))
    return jax.shard_map(
        per_device,
        mesh=mesh,
        in_specs=(
            token_spec,
            token_spec,
            P("seq", None),
            P("seq", None, None),
            *([weight_spec] * 8),
            *([norm_spec] * 4),
            *([head_spec] * 4),
            *([unit_spec] * 4),
        ),
        out_specs=(
            token_spec,
            token_spec,
            P(),
            *([weight_spec] * 10),
            *([norm_spec] * 5),
            *([head_spec] * 5),
            *([unit_spec] * 5),
        ),
        check_vma=False,
    )
```
